128 devices in a mesh: section: 2 (over x_lo), dp: 2 (over x_hi), seq: 32 (over y, z, core).
Axes of the slice: x: 4 (x_hi: 2, x_lo: 2; x = x_hi * 2 + x_lo), y: 4, z: 4, core: 2. Of those that a mesh axis runs over, the one named last changes fastest.
Arguments:
- inputs: bfloat16 [4, 2048, 1536], P('dp', 'seq'), may hold values from -6 to 6
- prefix: int32 [4], P('dp'), may hold values from 204 to 1024
- cotangent: bfloat16 [4, 2048, 1536], P('dp', 'seq'), may hold values from -6 to 6
- attn_gain: bfloat16 [2, 1536], P('section', ('dp', 'seq')), may hold values from 0.5 to 1.5
- w_query: bfloat16 [2, 1536, 1536], P('section', ('dp', 'seq')), may hold values from -0.15625 to 0.15625
- w_key: bfloat16 [2, 1536, 768], P('section', ('dp', 'seq')), may hold values from -0.15625 to 0.15625
- w_value: bfloat16 [2, 1536, 768], P('section', ('dp', 'seq')), may hold values from -0.15625 to 0.15625
- w_out: bfloat16 [2, 1536, 1536], P('section', ('dp', 'seq')), may hold values from -1.75 to 1.75
- mlp_gain: bfloat16 [2, 1536], P('section', ('dp', 'seq')), may hold values from 0.5 to 1.5
- w_gate: bfloat16 [2, 1536, 4096], P('section', ('dp', 'seq')), may hold values from -0.15625 to 0.15625
- w_up: bfloat16 [2, 1536, 4096], P('section', ('dp', 'seq')), may hold values from -0.15625 to 0.15625
- w_down: bfloat16 [2, 4096, 1536], P('section', ('dp', 'seq')), may hold values from -0.09375 to 0.09375
Outputs:
- layer_outs: bfloat16 [2, 4, 2048, 1536], P('section', 'dp', 'seq')
- layer_grads: bfloat16 [2, 4, 2048, 1536], P('section', 'dp', 'seq')
- grad_attn_gain: float32 [2, 1536], P('section', ('dp', 'seq'))
- grad_w_query: float32 [2, 1536, 1536], P('section', ('dp', 'seq'))
- grad_w_key: float32 [2, 1536, 768], P('section', ('dp', 'seq'))
- grad_w_value: float32 [2, 1536, 768], P('section', ('dp', 'seq'))
- grad_w_out: float32 [2, 1536, 1536], P('section', ('dp', 'seq'))
- grad_mlp_gain: float32 [2, 1536], P('section', ('dp', 'seq'))
- grad_w_gate: float32 [2, 1536, 4096], P('section', ('dp', 'seq'))
- grad_w_up: float32 [2, 1536, 4096], P('section', ('dp', 'seq'))
- grad_w_down: float32 [2, 4096, 1536], P('section', ('dp', 'seq'))
The draws below stay inside these ranges and needn't reach their ends.
All inputs are finite; a program needn't handle non-finite values.
Results may differ from the reference program's by a relative error of at most 0.039.
Values may be sent and summed in bfloat16 or wider, within the bound.
A program may use at most 320 MiB of HBM per device.

```python
import math
import jax
import jax.numpy as jnp
from jax import lax

D = 1536
HEADS = 16
KV_HEADS = 8
HEAD = 96
FF = 4096
LEN = 2048
SEQS = 4
LAYERS = 2
QW = 1536
KW = 768
N_SECTION = 2


def with_ends(drawn, own_key, low, high):
    spot = [jax.random.randint(jax.random.fold_in(own_key, axis), (), 0, length) for axis, length in enumerate(drawn.shape)]
    longest = drawn.shape.index(max(drawn.shape))
    next_to = spot[:longest] + [(spot[longest] + 1) % drawn.shape[longest]] + spot[longest + 1:]
    return drawn.at[tuple(spot)].set(low).at[tuple(next_to)].set(high)


def shard_levels(own_key, dims, cuts, smallest, top_value):
    def one(axis_at, parts):
        heights = jax.random.uniform(jax.random.fold_in(jax.random.fold_in(own_key, 6), axis_at), (parts,), jnp.float32, smallest / len(cuts), top_value / len(cuts))
        return jnp.repeat(jnp.exp(heights), dims[axis_at] // parts).reshape((-1,) + (1,) * (len(dims) - axis_at - 1))

    level = one(*cuts[0])
    for cut in cuts[1:]:
        level = level * one(*cut)
    return level


def gaussian(key, dims, spread, limit, cuts=(), kind=jnp.bfloat16):
    values = spread * jax.random.normal(key, dims, jnp.float32)
    if cuts:
        values = values * shard_levels(key, dims, cuts, -0.22, 0.18)
    return jnp.clip(values, -limit, limit).astype(kind)


def setup_inputs(seed: int = 0) -> dict:
    key_of = jax.random.split(jax.random.key(seed), 13)
    inputs = gaussian(key_of[0], (SEQS, LEN, D), 1.0, 6.0, ((0, 2), (1, 32)))
    prefix = with_ends(jax.random.randint(key_of[1], (SEQS,), LEN // 10, LEN // 2 + 1), jax.random.fold_in(key_of[1], 1), LEN // 10, (LEN // 2 + 1) - 1).astype(jnp.int32)
    cotangent = gaussian(key_of[2], (SEQS, LEN, D), 1.0, 6.0, ((0, 2), (1, 32)))
    attn_gain = jnp.clip(1.0 + 0.1 * jax.random.normal(key_of[3], (LAYERS, D), jnp.float32), 0.5, 1.5).astype(jnp.bfloat16)
    w_query = gaussian(key_of[4], (LAYERS, D, QW), D ** -0.5, 0.15625, ((0, 2), (1, 64)))
    w_key = gaussian(key_of[5], (LAYERS, D, KW), D ** -0.5, 0.15625, ((0, 2), (1, 64)))
    w_value = gaussian(key_of[6], (LAYERS, D, KW), D ** -0.5, 0.15625, ((0, 2), (1, 64)))
    w_out = gaussian(key_of[7], (LAYERS, QW, D), (max(1, QW * 16 // LEN)) ** -0.5, 1.75, ((0, 2), (1, 64)))
    mlp_gain = jnp.clip(1.0 + 0.1 * jax.random.normal(key_of[8], (LAYERS, D), jnp.float32), 0.5, 1.5).astype(jnp.bfloat16)
    w_gate = gaussian(key_of[9], (LAYERS, D, FF), D ** -0.5, 0.15625, ((0, 2), (1, 64)))
    w_up = gaussian(key_of[10], (LAYERS, D, FF), D ** -0.5, 0.15625, ((0, 2), (1, 64)))
    w_down = gaussian(key_of[11], (LAYERS, FF, D), FF ** -0.5, 0.09375, ((0, 2), (1, 64)))
    return dict(inputs=inputs, prefix=prefix, cotangent=cotangent, attn_gain=attn_gain, w_query=w_query, w_key=w_key, w_value=w_value, w_out=w_out, mlp_gain=mlp_gain, w_gate=w_gate, w_up=w_up, w_down=w_down)


eps_norm = 1e-05
rope_base = 100000.0
neg_fill = -1e+30
highest = lax.Precision.HIGHEST

@jax.custom_vjp
def low(v):
    return lax.optimization_barrier(v.astype(jnp.bfloat16)).astype(jnp.float32)

@jax.custom_vjp
def low_back(v):
    return v

def low_keep(v):
    return (low(v), None)

def low_pass(kept, grad):
    return (grad,)

def back_keep(v):
    return (v, None)

def back_low(kept, grad):
    return (low(grad),)
low.defvjp(low_keep, low_pass)
low_back.defvjp(back_keep, back_low)

def matmul(left, right):
    return jnp.dot(left, right, precision=highest)

def rms_scale(hidden, gain):
    inverse = lax.rsqrt(lax.optimization_barrier(jnp.mean(hidden * hidden, axis=-1, keepdims=True)) + eps_norm)
    return hidden * inverse * gain

def rotate(heads_in, positions):
    half_size = heads_in.shape[-1] // 2
    frequency = rope_base ** (-jnp.arange(half_size, dtype=jnp.float32) * 2.0 / heads_in.shape[-1])
    angles = positions.astype(jnp.float32)[:, None] * frequency[None, :]
    cosine = jnp.concatenate([jnp.cos(angles), jnp.cos(angles)], -1)[:, None, :]
    sine_table = jnp.concatenate([jnp.sin(angles), jnp.sin(angles)], -1)[:, None, :]
    first_half = heads_in[..., :half_size]
    second_half = heads_in[..., half_size:]
    turned = jnp.concatenate([-second_half, first_half], -1)
    return heads_in * cosine + turned * sine_table

def attend(queries_rot, keys_rot, values_in, prefix_len):
    length = keys_rot.shape[0]
    block_size = math.gcd(length, 512)
    block_count = length // block_size
    head_group = HEADS // KV_HEADS
    score_scale = 1.0 / math.sqrt(HEAD)
    query_blocks = queries_rot.reshape(block_count, block_size, KV_HEADS, head_group, HEAD)
    starts = jnp.arange(block_count, dtype=jnp.int32) * block_size
    key_pos = jnp.arange(length, dtype=jnp.int32)

    def one_block(query_block, start):
        scores = jnp.einsum('qgrd,kgd->grqk', query_block, keys_rot, precision=highest) * score_scale
        scores = low_back(scores)
        query_pos = start + jnp.arange(block_size, dtype=jnp.int32)
        allowed = (key_pos[None, :] <= query_pos[:, None]) | (key_pos[None, :] < prefix_len)
        scores = jnp.where(allowed, scores, neg_fill)
        soft_probs = jax.nn.softmax(scores, axis=-1)
        block_out = jnp.einsum('grqk,kgd->qgrd', low(soft_probs), values_in, precision=highest)
        return block_out.reshape(block_size, HEADS * HEAD)
    block_outs = lax.map(lambda block_pair: jax.checkpoint(one_block)(block_pair[0], block_pair[1]), (query_blocks, starts))
    return block_outs.reshape(length, HEADS * HEAD)

def layer_forward(hidden, prefix_len, weight_set):
    gain_attn, weight_query, weight_key, weight_value, weight_out, gain_mlp, weight_gate, weight_up, weight_down = weight_set
    length = hidden.shape[0]
    positions = jnp.arange(length, dtype=jnp.int32)
    normed = low(rms_scale(hidden, gain_attn))
    queries = low_back(matmul(normed, weight_query))
    keys_pre = low_back(matmul(normed, weight_key))
    values_in = low(low_back(matmul(normed, weight_value)))
    queries_rot = low(rotate(queries.reshape(length, HEADS, HEAD), positions))
    keys_rot = low(rotate(keys_pre.reshape(length, KV_HEADS, HEAD), positions))
    attended = attend(queries_rot, keys_rot, values_in.reshape(length, KV_HEADS, HEAD), prefix_len)
    attended = low(low_back(attended))
    middle = hidden + low_back(matmul(attended, weight_out))
    normed_two = low(rms_scale(middle, gain_mlp))
    gate_act = low_back(matmul(normed_two, weight_gate))
    up_act = low_back(matmul(normed_two, weight_up))
    mixed_act = low(jax.nn.silu(gate_act) * up_act)
    return middle + low_back(matmul(mixed_act, weight_down))

def reference(inputs, prefix, cotangent, attn_gain, w_query, w_key, w_value, w_out, mlp_gain, w_gate, w_up, w_down):
    params = tuple((weight.astype(jnp.float32) for weight in (attn_gain, w_query, w_key, w_value, w_out, mlp_gain, w_gate, w_up, w_down)))
    layer_params = [tuple((weight[layer_index] for weight in params)) for layer_index in range(N_SECTION)]

    def per_sequence(totals, seq_item):
        seq_in, prefix_len, seq_cot = seq_item
        hidden = seq_in.astype(jnp.float32)
        outs_list = []
        pullbacks = []
        for layer_index in range(N_SECTION):
            result, pullback = jax.vjp(lambda hidden_in, weight_set: layer_forward(hidden_in, prefix_len, weight_set), hidden, layer_params[layer_index])
            outs_list.append(result.astype(jnp.bfloat16))
            pullbacks.append(pullback)
            hidden = low(result)
        grad_now = seq_cot.astype(jnp.float32)
        in_grads = [None] * N_SECTION
        grads_list = [None] * N_SECTION
        for layer_index in reversed(range(N_SECTION)):
            grad_hidden, grad_params = pullbacks[layer_index](grad_now)
            in_grads[layer_index] = grad_hidden.astype(jnp.bfloat16)
            grad_now = low(grad_hidden)
            grads_list[layer_index] = grad_params
        stacked = tuple((jnp.stack([grads_list[layer_index][slot] for layer_index in range(N_SECTION)]) for slot in range(9)))
        totals = tuple((total + extra for total, extra in zip(totals, stacked)))
        return (totals, (jnp.stack(outs_list), jnp.stack(in_grads)))
    initial = tuple((jnp.zeros_like(weight) for weight in params))
    totals, (outs_all, grads_all) = lax.scan(per_sequence, initial, (inputs, prefix, cotangent))
    layer_outs = jnp.transpose(outs_all, (1, 0, 2, 3))
    layer_grads = jnp.transpose(grads_all, (1, 0, 2, 3))
    return (layer_outs, layer_grads, totals[0], totals[1], totals[2], totals[3], totals[4], totals[5], totals[6], totals[7], totals[8])
```

```python
import functools
import math

import jax
import jax.numpy as jnp
from jax import lax
from jax.experimental import pallas as pl
from jax.experimental.pallas import tpu as pltpu
from jax.sharding import PartitionSpec as P

HEADS = 16
KV_HEADS = 8
HEAD = 96
LANES = 128
EPS = 1e-05
ROPE_BASE = 100000.0
NEG = -1e30
PREFIX_MAX = 1024
SCALE = 1.0 / math.sqrt(HEAD)
MESH = pl.DeviceIdType.MESH
ANY = pl.BlockSpec(memory_space=pl.ANY)
VMEM = pl.BlockSpec(memory_space=pltpu.VMEM)
SMEM = pl.BlockSpec(memory_space=pltpu.SMEM)
MIB = 1 << 20

PIECES = (
    (24, 2048, "y", 1),
    (24, 2048, "y", -1),
    (24, 1536, "z", 1),
    (24, 768, "z", 1),
    (24, 128, "z", 1),
    (64, 768, "z", -1),
)
OTHER = {"y": "z", "z": "y"}


def f32dot(a, b, dims):
    return lax.dot_general(a, b, (dims, ((), ())), preferred_element_type=jnp.float32)


class Place:
    def __init__(self):
        self.s = lax.axis_index("section")
        self.d = lax.axis_index("dp")
        self.q = lax.axis_index("seq")
        self.y = lax.div(self.q, 8)
        self.z = lax.rem(lax.div(self.q, 2), 4)
        self.c = lax.rem(self.q, 2)

    def coord(self, axis):
        return self.y if axis == "y" else self.z

    def step(self, axis, by):
        y, z = self.y, self.z
        if axis == "y":
            y = lax.rem(y + by + 4, 4)
        else:
            z = lax.rem(z + by + 4, 4)
        return (self.s, self.d, y * 8 + z * 2 + self.c)

    def sibling(self):
        return (self.s, self.d, self.q + 1 - 2 * self.c)

    def dp_peer(self):
        return (self.s, 1 - self.d, self.q)


def meet(devices):
    barrier = pltpu.get_barrier_semaphore()
    for device in devices:
        pl.semaphore_signal(barrier, inc=1, device_id=device, device_id_type=MESH)
    pl.semaphore_wait(barrier, len(devices))


def remote(src, dst, send, recv, device):
    return pltpu.make_async_remote_copy(
        src_ref=src, dst_ref=dst, send_sem=send, recv_sem=recv, device_id=device, device_id_type=MESH
    )


def gather_kernel(*refs):
    n = len(PIECES)
    ins, outs = refs[:n], refs[n : 2 * n]
    give, got, chip = refs[2 * n : 3 * n], refs[3 * n : 4 * n], refs[4 * n : 5 * n]
    first, local, over, ring_s, ring_r, sib_s, sib_r = refs[5 * n :]
    me = Place()
    meet(
        [me.step("y", 1), me.step("y", -1), me.step("z", 1), me.step("z", -1), me.dp_peer(), me.sibling()]
    )
    pending = []
    swaps = []
    for i, (rows, width, _, _) in enumerate(PIECES):
        start = pl.multiple_of((1 - me.c) * width, LANES)
        give[i][...] = ins[i][:, pl.ds(start, width)].astype(jnp.float32)
        cp = remote(give[i], got[i], first.at[0, i], first.at[1, i], me.sibling())
        cp.start()
        swaps.append(cp)

    def shard(i, dp, y, z):
        width = PIECES[i][1]
        return outs[i].at[dp, y, z, :, pl.ds(pl.multiple_of(me.c * width, LANES), width)]

    def column(i, dp, pos):
        width = PIECES[i][1]
        lanes = pl.ds(pl.multiple_of(me.c * width, LANES), width)
        if PIECES[i][2] == "y":
            return outs[i].at[dp, pl.ds(0, 4), pos, :, lanes]
        return outs[i].at[dp, pos, pl.ds(0, 4), :, lanes]

    def along(i, dp, by):
        a1 = PIECES[i][2]
        pos = lax.rem(me.coord(a1) + by + 4, 4)
        return shard(i, dp, pos, me.z) if a1 == "y" else shard(i, dp, me.y, pos)

    def across(i, dp, by):
        a2 = OTHER[PIECES[i][2]]
        return column(i, dp, lax.rem(me.coord(a2) + by + 4, 4))

    def send(i, block, k, src, dst, device):
        cp = remote(src, dst, ring_s.at[i, block, k], ring_r.at[i, block, k], device)
        cp.start()
        pending.append(cp)
        return cp

    def share(i, block, k, ref):
        cp = remote(ref, ref, sib_s.at[i, block, k], sib_r.at[i, block, k], me.sibling())
        cp.start()
        pending.append(cp)
        shares.append(cp)

    shares = []
    dps = (me.d, 1 - me.d)
    one, two, locals_, overs = {}, {}, [], []
    for i, (rows, width, a1, _) in enumerate(PIECES):
        swaps[i].wait()
        start = pl.multiple_of(me.c * width, LANES)
        mine = ins[i][:, pl.ds(start, width)].astype(jnp.float32)
        theirs = got[i][...]
        low = jnp.where(me.c == 0, mine, theirs)
        high = jnp.where(me.c == 0, theirs, mine)
        chip[i][...] = jnp.concatenate([low, high], axis=0).astype(jnp.bfloat16)
        here = along(i, me.d, 0)
        one[i, 0, 1] = send(i, 0, 0, chip[i], here, me.step(a1, 1))
        one[i, 0, -1] = send(i, 0, 1, chip[i], here, me.step(a1, -1))
        cp = remote(chip[i], here, over.at[0, i], over.at[1, i], me.dp_peer())
        cp.start()
        overs.append(cp)
        cp = pltpu.make_async_copy(chip[i], here, local.at[i])
        cp.start()
        locals_.append(cp)
        cp = remote(chip[i], here, sib_s.at[i, 0, 0], sib_r.at[i, 0, 0], me.sibling())
        cp.start()
        pending.append(cp)
        shares.append(cp)

    def ring_one_end(block):
        dp = dps[block]
        for i, (_, _, a1, sign) in enumerate(PIECES):
            one[i, block, sign].wait_recv()
            came = along(i, dp, -sign)
            one[i, block, 0] = send(i, block, 2, came, came, me.step(a1, sign))
            share(i, block, 1, came)
        for i, (_, _, a1, sign) in enumerate(PIECES):
            one[i, block, -sign].wait_recv()
            share(i, block, 2, along(i, dp, sign))

    def ring_two_start(block):
        dp = dps[block]
        for i, (_, _, a1, sign) in enumerate(PIECES):
            one[i, block, 0].wait_recv()
            share(i, block, 3, along(i, dp, 2))
            if block == 0:
                locals_[i].wait()
            here = across(i, dp, 0)
            a2 = OTHER[a1]
            two[i, block, sign] = send(i, block, 3, here, here, me.step(a2, sign))
            two[i, block, -sign] = send(i, block, 4, here, here, me.step(a2, -sign))

    def ring_two_end(block):
        dp = dps[block]
        for i, (_, _, a1, sign) in enumerate(PIECES):
            two[i, block, sign].wait_recv()
            came = across(i, dp, -sign)
            two[i, block, 0] = send(i, block, 5, came, came, me.step(OTHER[a1], sign))
            share(i, block, 4, came)
        for i, (_, _, a1, sign) in enumerate(PIECES):
            two[i, block, -sign].wait_recv()
            share(i, block, 5, across(i, dp, sign))

    def finish(block):
        for i in range(n):
            two[i, block, 0].wait_recv()
            share(i, block, 6, across(i, dps[block], 2))

    ring_one_end(0)
    ring_two_start(0)
    for i, (_, _, a1, _) in enumerate(PIECES):
        overs[i].wait_recv()
        here = along(i, dps[1], 0)
        one[i, 1, 1] = send(i, 1, 0, here, here, me.step(a1, 1))
        one[i, 1, -1] = send(i, 1, 1, here, here, me.step(a1, -1))
        share(i, 1, 0, here)
    ring_two_end(0)
    ring_one_end(1)
    ring_two_start(1)
    finish(0)
    ring_two_end(1)
    finish(1)
    for cp in shares:
        cp.wait_recv()
    for cp in pending:
        cp.wait_send()
    for cp in overs:
        cp.wait_send()


def gather_weights(shards):
    n = len(PIECES)
    outs = pl.pallas_call(
        gather_kernel,
        out_shape=[
            jax.ShapeDtypeStruct((2, 4, 4, 2 * rows, 2 * width), jnp.bfloat16) for rows, width, _, _ in PIECES
        ],
        in_specs=[VMEM] * n,
        out_specs=[ANY] * n,
        scratch_shapes=[pltpu.VMEM((rows, width), jnp.float32) for rows, width, _, _ in PIECES]
        + [pltpu.VMEM((rows, width), jnp.float32) for rows, width, _, _ in PIECES]
        + [pltpu.VMEM((2 * rows, width), jnp.bfloat16) for rows, width, _, _ in PIECES]
        + [
            pltpu.SemaphoreType.DMA((2, n)),
            pltpu.SemaphoreType.DMA((n,)),
            pltpu.SemaphoreType.DMA((2, n)),
            pltpu.SemaphoreType.DMA((n, 2, 6)),
            pltpu.SemaphoreType.DMA((n, 2, 6)),
            pltpu.SemaphoreType.DMA((n, 2, 7)),
            pltpu.SemaphoreType.DMA((n, 2, 7)),
        ],
        compiler_params=pltpu.CompilerParams(
            collective_id=1, has_side_effects=True, vmem_limit_bytes=24 * MIB
        ),
        name="gather_weights",
    )(*shards)
    return [
        out.reshape(64 * rows, 2 * width) for out, (rows, width, _, _) in zip(outs, PIECES, strict=True)
    ]


def add_into(total, term):
    chunks = total.shape[1] // 16

    def step(k, carry):
        j = lax.div(k, chunks)
        rows = pl.ds(pl.multiple_of(lax.rem(k, chunks) * 16, 16), 16)
        both = total[j, rows, :].astype(jnp.float32) + term[j, rows, :].astype(jnp.float32)
        total[j, rows, :] = both.astype(jnp.bfloat16)
        return carry

    lax.fori_loop(0, total.shape[0] * chunks, step, 0)


def add_two(total, left, right):
    chunks = total.shape[1] // 16

    def step(k, carry):
        j = lax.div(k, chunks)
        rows = pl.ds(pl.multiple_of(lax.rem(k, chunks) * 16, 16), 16)
        parts = [ref[j, rows, :].astype(jnp.float32) for ref in (total, left, right)]
        total[j, rows, :] = (parts[0] + (parts[1] + parts[2])).astype(jnp.bfloat16)
        return carry

    lax.fori_loop(0, total.shape[0] * chunks, step, 0)


def scatter_kernel(*refs):
    n = len(PIECES)
    take = iter(range(0, 100 * n, n))

    def group():
        k = next(take)
        return refs[k : k + n]

    ins, outs = group(), group()
    near, far, last, mid, own = group(), group(), group(), group(), group()
    near1, far1, last1 = group(), group(), group()
    sent, came, total = group(), group(), group()
    load, ring_s, ring_r, over, fin, keep = refs[13 * n :]
    me = Place()
    meet(
        [me.step("y", 1), me.step("y", -1), me.step("z", 1), me.step("z", -1), me.dp_peer(), me.sibling()]
    )
    dps = (1 - me.d, me.d)
    pending = []

    def column(i, block, by):
        a2 = OTHER[PIECES[i][2]]
        pos = lax.rem(me.coord(a2) + by + 4, 4)
        if a2 == "y":
            return ins[i].at[dps[block], pos, pl.ds(0, 4)]
        return ins[i].at[dps[block], pl.ds(0, 4), pos]

    def send(i, block, k, src, dst, device):
        cp = remote(src, dst, ring_s.at[i, block, k], ring_r.at[i, block, k], device)
        cp.start()
        pending.append(cp)
        return cp

    loads, one, two = {}, {}, {}
    for block in range(2):
        for i, (_, _, a1, sign) in enumerate(PIECES):
            a2 = OTHER[a1]
            one[i, block, 0] = send(i, block, 0, column(i, block, 2 * sign), near[i].at[block], me.step(a2, sign))
        for i, (_, _, a1, sign) in enumerate(PIECES):
            a2 = OTHER[a1]
            one[i, block, 1] = send(i, block, 1, column(i, block, -sign), far[i].at[block], me.step(a2, -sign))
        for i, (_, _, a1, sign) in enumerate(PIECES):
            cp = pltpu.make_async_copy(column(i, block, sign), mid[i].at[block], load.at[0, i, block])
            cp.start()
            loads[i, block, 0] = cp
            cp = pltpu.make_async_copy(column(i, block, 0), own[i].at[block], load.at[1, i, block])
            cp.start()
            loads[i, block, 1] = cp
    for block in range(2):
        for i, (_, _, a1, sign) in enumerate(PIECES):
            one[i, block, 0].wait_recv()
            loads[i, block, 0].wait()
            add_into(near[i].at[block], mid[i].at[block])
            one[i, block, 2] = send(
                i, block, 2, near[i].at[block], last[i].at[block], me.step(OTHER[a1], sign)
            )
    overs = []
    for block in range(2):
        for i, (_, _, a1, sign) in enumerate(PIECES):
            one[i, block, 1].wait_recv()
            loads[i, block, 1].wait()
            one[i, block, 2].wait_recv()
            add_two(own[i].at[block], far[i].at[block], last[i].at[block])
            pos = me.coord(a1)
            far_place = lax.rem(pos + 2, 4)
            two[i, block, 0] = send(
                i, block, 3, own[i].at[block, far_place], near1[i].at[block], me.step(a1, sign)
            )
            back_place = lax.rem(pos - sign + 4, 4)
            two[i, block, 1] = send(
                i, block, 4, own[i].at[block, back_place], far1[i].at[block], me.step(a1, -sign)
            )
        for i, (_, _, a1, sign) in enumerate(PIECES):
            two[i, block, 0].wait_recv()
            place = lax.rem(me.coord(a1) + sign + 4, 4)
            add_into(near1[i].at[pl.ds(block, 1)], own[i].at[block, pl.ds(place, 1)])
            two[i, block, 2] = send(
                i, block, 5, near1[i].at[block], last1[i].at[block], me.step(a1, sign)
            )
        for i, (rows, width, a1, sign) in enumerate(PIECES):
            two[i, block, 1].wait_recv()
            two[i, block, 2].wait_recv()
            pos = me.coord(a1)
            if block == 1:
                overs[i].wait_recv()

            def step(k, carry, i=i, block=block, pos=pos):
                part = pl.ds(pl.multiple_of(k * 16, 16), 16)
                both = far1[i][block, part, :].astype(jnp.float32) + last1[i][block, part, :].astype(
                    jnp.float32
                )
                both = both + own[i][block, pos, part, :].astype(jnp.float32)
                if block == 0:
                    sent[i][part, :] = both.astype(jnp.bfloat16)
                else:
                    total[i][part, :] = both + came[i][part, :].astype(jnp.float32)
                return carry

            lax.fori_loop(0, 2 * rows // 16, step, 0)
            if block == 0:
                cp = remote(sent[i], came[i], over.at[0, i], over.at[1, i], me.dp_peer())
                cp.start()
                overs.append(cp)
            else:
                mine = total[i].at[pl.ds(pl.multiple_of(me.c * rows, 8), rows)]
                theirs = total[i].at[pl.ds(pl.multiple_of((1 - me.c) * rows, 8), rows)]
                cp = pltpu.make_async_copy(mine, outs[i].at[me.c], keep.at[i])
                cp.start()
                loads[i, "keep"] = cp
                cp = remote(theirs, outs[i].at[me.c], fin.at[0, i], fin.at[1, i], me.sibling())
                cp.start()
                loads[i, "fin"] = cp
    for i in range(n):
        loads[i, "keep"].wait()
        loads[i, "fin"].wait()
    for cp in pending:
        cp.wait_send()
    for cp in overs:
        cp.wait_send()


def scatter_grads(parts):
    n = len(PIECES)
    shapes = [(2 * rows, width) for rows, width, _, _ in PIECES]
    bf16 = jnp.bfloat16
    return pl.pallas_call(
        scatter_kernel,
        out_shape=[jax.ShapeDtypeStruct((2, rows, width), jnp.float32) for rows, width, _, _ in PIECES],
        in_specs=[ANY] * n,
        out_specs=[ANY] * n,
        scratch_shapes=[pltpu.VMEM((2, 4, *shape), bf16) for _ in range(5) for shape in shapes]
        + [pltpu.VMEM((2, *shape), bf16) for _ in range(3) for shape in shapes]
        + [pltpu.VMEM(shape, bf16) for _ in range(2) for shape in shapes]
        + [pltpu.VMEM(shape, jnp.float32) for shape in shapes]
        + [
            pltpu.SemaphoreType.DMA((2, n, 2)),
            pltpu.SemaphoreType.DMA((n, 2, 6)),
            pltpu.SemaphoreType.DMA((n, 2, 6)),
            pltpu.SemaphoreType.DMA((2, n)),
            pltpu.SemaphoreType.DMA((2, n)),
            pltpu.SemaphoreType.DMA((n,)),
        ],
        compiler_params=pltpu.CompilerParams(
            collective_id=2, has_side_effects=True, vmem_limit_bytes=56 * MIB
        ),
        name="scatter_grads",
    )(*[part.reshape(2, 4, 4, *shape) for part, shape in zip(parts, shapes, strict=True)])


def meet_plane(me, count):
    barrier = pltpu.get_barrier_semaphore()

    def greet(k, carry):
        to = lax.rem(me.q + k, count)
        pl.semaphore_signal(barrier, inc=1, device_id=(me.s, me.d, to), device_id_type=MESH)
        return carry

    lax.fori_loop(1, count, greet, 0)
    pl.semaphore_wait(barrier, count - 1)


def all_to_all(me, src, dst_of, send_sem, recv_sem, own_sem):
    count = src.shape[0]
    own = pltpu.make_async_copy(src.at[me.q], dst_of(me.q, me.q), own_sem)
    own.start()

    def out(k, carry):
        to = lax.rem(me.q + k, count)
        remote(
            src.at[to], dst_of(me.q, to), send_sem.at[to], recv_sem.at[me.q], (me.s, me.d, to)
        ).start()
        return carry

    lax.fori_loop(1, count, out, 0)

    def arrive(k, carry):
        origin = lax.rem(me.q + k, count)
        remote(
            src.at[origin],
            dst_of(origin, me.q),
            send_sem.at[origin],
            recv_sem.at[origin],
            (me.s, me.d, origin),
        ).wait()
        return carry

    lax.fori_loop(1, count, arrive, 0)
    own.wait()


def spread_kernel(src, dst, send_sem, recv_sem, own_sem, sib):
    me = Place()
    meet_plane(me, src.shape[0])
    all_to_all(
        me, src, lambda origin, to: dst.at[origin, lax.rem(to, 2)], send_sem, recv_sem, own_sem.at[0]
    )
    mine = dst.at[pl.ds(0, src.shape[0]), me.c]
    cp = remote(mine, mine, sib.at[0], sib.at[1], me.sibling())
    cp.start()
    cp.wait()


def spread(src):
    count, rows, width = src.shape
    return pl.pallas_call(
        spread_kernel,
        out_shape=jax.ShapeDtypeStruct((count, 2, rows, width), src.dtype),
        in_specs=[VMEM],
        out_specs=VMEM,
        scratch_shapes=[
            pltpu.SemaphoreType.DMA((count,)),
            pltpu.SemaphoreType.DMA((count,)),
            pltpu.SemaphoreType.DMA((1,)),
            pltpu.SemaphoreType.DMA((2,)),
        ],
        compiler_params=pltpu.CompilerParams(
            collective_id=3, has_side_effects=True, vmem_limit_bytes=16 * MIB
        ),
        name="spread",
    )(src)


def swap_kernel(src, dst, send_sem, recv_sem, own_sem):
    me = Place()
    meet_plane(me, src.shape[0])
    all_to_all(me, src, lambda origin, to: dst.at[origin], send_sem, recv_sem, own_sem.at[0])


def swap(src):
    count = src.shape[0]
    return pl.pallas_call(
        swap_kernel,
        out_shape=jax.ShapeDtypeStruct(src.shape, src.dtype),
        in_specs=[VMEM],
        out_specs=VMEM,
        scratch_shapes=[
            pltpu.SemaphoreType.DMA((count,)),
            pltpu.SemaphoreType.DMA((count,)),
            pltpu.SemaphoreType.DMA((1,)),
        ],
        compiler_params=pltpu.CompilerParams(
            collective_id=4, has_side_effects=True, vmem_limit_bytes=16 * MIB
        ),
        name="swap",
    )(src)


def return_kernel(dkv, dq, dst, got, bundle, send_sem, recv_sem, own_sem, sib):
    me = Place()
    count = dq.shape[0]
    meet_plane(me, count)
    cp = remote(dkv.at[pl.ds(0, count), 1 - me.c], got, sib.at[0], sib.at[1], me.sibling())
    cp.start()
    cp.wait()

    def step(k, carry):
        bundle[k, :, 0:256] = (dkv[k, me.c] + got[k]).astype(jnp.bfloat16)
        bundle[k, :, 256:512] = dq[k]
        return carry

    lax.fori_loop(0, count, step, 0)
    all_to_all(me, bundle, lambda origin, to: dst.at[origin], send_sem, recv_sem, own_sem.at[0])


def send_back(dkv, dq):
    count, rows, _ = dq.shape
    return pl.pallas_call(
        return_kernel,
        out_shape=jax.ShapeDtypeStruct((count, rows, 512), jnp.bfloat16),
        in_specs=[VMEM] * 2,
        out_specs=VMEM,
        scratch_shapes=[
            pltpu.VMEM((count, rows, 256), jnp.float32),
            pltpu.VMEM((count, rows, 512), jnp.bfloat16),
            pltpu.SemaphoreType.DMA((count,)),
            pltpu.SemaphoreType.DMA((count,)),
            pltpu.SemaphoreType.DMA((1,)),
            pltpu.SemaphoreType.DMA((2,)),
        ],
        compiler_params=pltpu.CompilerParams(
            collective_id=5, has_side_effects=True, vmem_limit_bytes=24 * MIB
        ),
        name="send_back",
    )(dkv, dq)


def pair_kernel(whole_count, *refs):
    n = (len(refs) - 3) // 2
    ins, outs = refs[:n], refs[n : 2 * n]
    send_sem, recv_sem, own_sem = refs[2 * n :]
    me = Place()
    meet([me.sibling()])
    copies = []
    for i in range(n):
        here = ins[i] if i < whole_count else ins[i].at[me.c]
        there = ins[i] if i < whole_count else ins[i].at[1 - me.c]
        cp = remote(there, outs[i].at[me.c], send_sem.at[i], recv_sem.at[i], me.sibling())
        cp.start()
        copies.append(cp)
        cp = pltpu.make_async_copy(here, outs[i].at[me.c], own_sem.at[i])
        cp.start()
        copies.append(cp)
    for cp in copies:
        cp.wait()


def pair_up(whole, halved):
    n = len(whole) + len(halved)
    return pl.pallas_call(
        functools.partial(pair_kernel, len(whole)),
        out_shape=[jax.ShapeDtypeStruct((2, *a.shape), a.dtype) for a in whole]
        + [jax.ShapeDtypeStruct(a.shape, a.dtype) for a in halved],
        in_specs=[ANY] * n,
        out_specs=[ANY] * n,
        scratch_shapes=[pltpu.SemaphoreType.DMA((n,))] * 3,
        compiler_params=pltpu.CompilerParams(collective_id=6, has_side_effects=True),
        name="pair_up",
    )(*whole, *halved)


ORIGINS = 32
BLOCK = 8


def block_mask(block, keys, core, prefix_len):
    rows = BLOCK * 32
    row = lax.broadcasted_iota(jnp.int32, (rows, keys), 0)
    key = lax.broadcasted_iota(jnp.int32, (rows, keys), 1)
    pos = block * BLOCK * 64 + 64 * (row // 32) + 32 * core + row % 32
    return (key <= pos) | (key < prefix_len)


def keys_of(block):
    return max((block + 1) * BLOCK * 64, PREFIX_MAX)


def attend_kernel(meta, bundle, out):
    core, prefix_len = meta[0], meta[1]
    for block in range(ORIGINS // BLOCK):
        keys = keys_of(block)
        src = pl.ds(block * BLOCK, BLOCK)
        k = bundle[pl.ds(0, keys // 64), :, :, 0:128].reshape(keys, LANES)
        v = bundle[pl.ds(0, keys // 64), :, :, 128:256].reshape(keys, LANES)
        allowed = block_mask(block, keys, core, prefix_len)
        for h in range(2):
            lanes = slice(256 + 128 * h, 384 + 128 * h)
            q = bundle[src, core, :, lanes].reshape(BLOCK * 32, LANES)
            s = jnp.where(allowed, f32dot(q, k, ((1,), (1,))) * SCALE, NEG)
            top = jnp.max(s, axis=-1, keepdims=True)
            e = jnp.exp(s - top)
            p = (e * (1.0 / jnp.sum(e, axis=-1, keepdims=True))).astype(jnp.bfloat16)
            o = f32dot(p, v, ((1,), (0,)))
            out[src, :, 128 * h : 128 * h + 128] = o.astype(jnp.bfloat16).reshape(BLOCK, 32, LANES)


def attend(meta, bundle):
    return pl.pallas_call(
        attend_kernel,
        out_shape=jax.ShapeDtypeStruct((ORIGINS, 32, 256), jnp.bfloat16),
        in_specs=[SMEM, VMEM],
        out_specs=VMEM,
        compiler_params=pltpu.CompilerParams(vmem_limit_bytes=48 * MIB),
        name="attend",
    )(meta, bundle)


def attend_back_kernel(meta, bundle, datt, dkv, dq, dk_sum, dv_sum):
    core, prefix_len = meta[0], meta[1]
    dk_sum[...] = jnp.zeros_like(dk_sum)
    dv_sum[...] = jnp.zeros_like(dv_sum)
    for block in range(ORIGINS // BLOCK):
        keys = keys_of(block)
        src = pl.ds(block * BLOCK, BLOCK)
        k = bundle[pl.ds(0, keys // 64), :, :, 0:128].reshape(keys, LANES)
        v = bundle[pl.ds(0, keys // 64), :, :, 128:256].reshape(keys, LANES)
        allowed = block_mask(block, keys, core, prefix_len)
        for h in range(2):
            lanes = slice(256 + 128 * h, 384 + 128 * h)
            q = bundle[src, core, :, lanes].reshape(BLOCK * 32, LANES)
            g = datt[src, :, 128 * h : 128 * h + 128].reshape(BLOCK * 32, LANES)
            s = jnp.where(allowed, f32dot(q, k, ((1,), (1,))) * SCALE, NEG)
            top = jnp.max(s, axis=-1, keepdims=True)
            e = jnp.exp(s - top)
            p = e * (1.0 / jnp.sum(e, axis=-1, keepdims=True))
            dp = f32dot(g, v, ((1,), (1,)))
            delta = jnp.sum(p * dp, axis=-1, keepdims=True)
            ds = (p * (dp - delta)).astype(jnp.bfloat16)
            dq[src, :, 128 * h : 128 * h + 128] = (
                (f32dot(ds, k, ((1,), (0,))) * SCALE).astype(jnp.bfloat16).reshape(BLOCK, 32, LANES)
            )
            dk_sum[pl.ds(0, keys), :] += f32dot(ds, q, ((0,), (0,)))
            dv_sum[pl.ds(0, keys), :] += f32dot(p.astype(jnp.bfloat16), g, ((0,), (0,)))
    dkv[:, :, :, 0:128] = (dk_sum[...] * SCALE).reshape(ORIGINS, 2, 32, LANES)
    dkv[:, :, :, 128:256] = dv_sum[...].reshape(ORIGINS, 2, 32, LANES)


def attend_back(meta, bundle, datt):
    return pl.pallas_call(
        attend_back_kernel,
        out_shape=[
            jax.ShapeDtypeStruct((ORIGINS, 2, 32, 256), jnp.float32),
            jax.ShapeDtypeStruct((ORIGINS, 32, 256), jnp.bfloat16),
        ],
        in_specs=[SMEM, VMEM, VMEM],
        out_specs=[VMEM, VMEM],
        scratch_shapes=[pltpu.VMEM((ORIGINS * 64, LANES), jnp.float32)] * 2,
        compiler_params=pltpu.CompilerParams(vmem_limit_bytes=56 * MIB),
        name="attend_back",
    )(meta, bundle, datt)


def mm(a, b):
    return jnp.dot(a, b, preferred_element_type=jnp.float32)


def mm_t(a, b):
    return lax.dot_general(a, b, (((1,), (1,)), ((), ())), preferred_element_type=jnp.float32)


def rope_tables(positions):
    half = HEAD // 2
    frequency = ROPE_BASE ** (-jnp.arange(half, dtype=jnp.float32) * 2.0 / HEAD)
    angles = positions.astype(jnp.float32)[:, None] * frequency[None, :]
    cos = jnp.concatenate([jnp.cos(angles)] * 2, -1)[:, None, None, :]
    sin = jnp.concatenate([jnp.sin(angles)] * 2, -1)[:, None, None, :]
    turned = (jnp.arange(4) != 1)[None, None, :, None]
    return jnp.where(turned, cos, 1.0), jnp.where(turned, sin, 0.0)


def forward(x, weights, tables, meta):
    qkv_w, o_w, gate_w, up_w, down_w, gain_attn, gain_mlp = weights
    cos, sin = tables
    tokens, width = x.shape
    hidden = x.astype(jnp.float32)
    r1 = lax.rsqrt(jnp.mean(hidden * hidden, axis=-1, keepdims=True) + EPS)
    normed = (hidden * r1 * gain_attn).astype(jnp.bfloat16)
    qkv = mm(normed, qkv_w).reshape(2, 64, KV_HEADS, 4, HEAD)
    half = HEAD // 2
    turned = jnp.concatenate([-qkv[..., half:], qkv[..., :half]], -1)
    bundle = (qkv * cos + turned * sin).astype(jnp.bfloat16)
    bundle = jnp.pad(bundle, ((0, 0),) * 4 + ((0, LANES - HEAD),))
    bundle = bundle.transpose(0, 2, 1, 3, 4).reshape(32, 32, 512)
    whole = spread(bundle)
    out = swap(attend(meta, whole))
    attended = (
        out.reshape(2, KV_HEADS, 64, 2, LANES)[..., :HEAD].transpose(0, 2, 1, 3, 4).reshape(tokens, width)
    )
    middle = hidden + mm(attended, o_w)
    r2 = lax.rsqrt(jnp.mean(middle * middle, axis=-1, keepdims=True) + EPS)
    normed_two = (middle * r2 * gain_mlp).astype(jnp.bfloat16)
    gate = mm(normed_two, gate_w)
    up = mm(normed_two, up_w)
    mixed = (jax.nn.silu(gate) * up).astype(jnp.bfloat16)
    result = (middle + mm(mixed, down_w)).astype(jnp.bfloat16)
    return result, (hidden, r1, normed, whole, attended, middle, r2, normed_two, gate, up, mixed)


def norm_back(dn, gain, u, r):
    scaled = dn * gain
    return r * (scaled - u * jnp.mean(scaled * u, axis=-1, keepdims=True))


def backward(g_low, state, weights, tables, meta):
    qkv_w, o_w, gate_w, up_w, down_w, gain_attn, gain_mlp = weights
    hidden, r1, normed, whole, attended, middle, r2, normed_two, gate, up, mixed = state
    cos, sin = tables
    tokens, width = hidden.shape
    g = g_low.astype(jnp.float32)
    gm = mm_t(g_low, down_w)
    sig = jax.nn.sigmoid(gate)
    dgate = (gm * up * sig * (1.0 + gate * (1.0 - sig))).astype(jnp.bfloat16)
    dup = (gm * (gate * sig)).astype(jnp.bfloat16)
    dn2 = mm_t(dgate, gate_w) + mm_t(dup, up_w)
    u2 = middle * r2
    dgain_mlp = jnp.sum(dn2 * u2, axis=0)
    dmiddle = g + norm_back(dn2, gain_mlp, u2, r2)
    db = dmiddle.astype(jnp.bfloat16)
    datt = mm_t(db, o_w).astype(jnp.bfloat16).reshape(2, 64, KV_HEADS, 2, HEAD)
    datt = jnp.pad(datt, ((0, 0),) * 4 + ((0, LANES - HEAD),))
    datt = swap(datt.transpose(0, 2, 1, 3, 4).reshape(32, 32, 256))
    dkv, dq = attend_back(meta, whole, datt)
    back = send_back(dkv, dq).reshape(2, KV_HEADS, 64, 4, LANES)[..., :HEAD]
    back = back.transpose(0, 2, 1, 3, 4).astype(jnp.float32)
    half = HEAD // 2
    slanted = back * sin
    turned = jnp.concatenate([slanted[..., half:], -slanted[..., :half]], -1)
    dqkv = (back * cos + turned).astype(jnp.bfloat16).reshape(tokens, 2 * width)
    dn1 = mm_t(dqkv, qkv_w)
    u1 = hidden * r1
    dgain_attn = jnp.sum(dn1 * u1, axis=0)
    dx = (dmiddle + norm_back(dn1, gain_attn, u1, r1)).astype(jnp.bfloat16)
    return dx, (g_low, dgate, dup, db, dqkv, dgain_attn, dgain_mlp)


def halves(a):
    rows, width = a.shape
    return a.reshape(rows, 2, width // 2).transpose(1, 0, 2)


def body(
    inputs, prefix, cotangent, attn_gain, w_query, w_key, w_value, w_out, mlp_gain, w_gate, w_up, w_down
):
    seqs, rows, width = inputs.shape
    tokens = seqs * rows
    section = lax.axis_index("section")
    seq = lax.axis_index("seq")
    positions = seq * rows + jnp.arange(rows, dtype=jnp.int32)
    tables = rope_tables(positions)
    meta = jnp.stack([seq % 2, lax.dynamic_index_in_dim(prefix, seq // 16, 0, keepdims=False)])

    part = w_query.shape[1]
    qkv_shard = jnp.concatenate(
        [
            w_key[0].reshape(part, KV_HEADS, HEAD),
            w_value[0].reshape(part, KV_HEADS, HEAD),
            w_query[0].reshape(part, KV_HEADS, 2 * HEAD),
        ],
        -1,
    ).reshape(part, 2 * width)
    gains = jnp.concatenate(
        [
            jnp.broadcast_to(attn_gain[0][:, None], (part, LANES)),
            jnp.broadcast_to(mlp_gain[0][:, None], (part, LANES)),
        ],
        -1,
    )
    gate_w, up_w, qkv_w, o_w, gains_w, down_w = gather_weights(
        [w_gate[0], w_up[0], qkv_shard, w_out[0], gains, w_down[0]]
    )
    gain_attn = gains_w[:, 0].astype(jnp.float32)[None, :]
    gain_mlp = gains_w[:, LANES].astype(jnp.float32)[None, :]
    weights = (qkv_w, o_w, gate_w, up_w, down_w, gain_attn, gain_mlp)

    x0 = inputs.reshape(tokens, width)
    out0, _ = forward(x0, weights, tables, meta)
    received = lax.ppermute(out0, "section", [(0, 1)])
    x1 = jnp.where(section == 0, x0, received)
    out, state = forward(x1, weights, tables, meta)

    g0 = cotangent.reshape(tokens, width)
    dx0, _ = backward(g0, state, weights, tables, meta)
    received = lax.ppermute(dx0, "section", [(1, 0)])
    g1 = jnp.where(section == 1, g0, received)
    dx, (g_low, dgate, dup, db, dqkv, dgain_attn, dgain_mlp) = backward(g1, state, weights, tables, meta)

    normed, attended, normed_two, mixed = state[2], state[4], state[7], state[10]
    dgains = jnp.broadcast_to(jnp.stack([dgain_attn, dgain_mlp])[:, None, :], (2, 8, width))
    normed, attended, normed_two, mixed, g_half, dgate, dup, db, dqkv, dgains = pair_up(
        [normed, attended, normed_two, mixed],
        [halves(g_low), halves(dgate), halves(dup), halves(db), halves(dqkv), dgains],
    )

    def outer(a, b):
        a, b = a.reshape(2 * tokens, -1), b.reshape(2 * tokens, -1)
        return lax.dot_general(
            a, b, (((0,), (0,)), ((), ())), preferred_element_type=jnp.float32
        ).astype(jnp.bfloat16)

    gain_part = jnp.broadcast_to(
        (dgains[0, 0] + dgains[1, 0]).astype(jnp.bfloat16)[:, None], (width, LANES)
    )
    sums = scatter_grads(
        [
            outer(normed_two, dgate),
            outer(normed_two, dup),
            outer(normed, dqkv),
            outer(attended, db),
            gain_part,
            outer(mixed, g_half),
        ]
    )

    def joined(a):
        return a.transpose(1, 0, 2).reshape(1, a.shape[1], -1)

    gate_g, up_g, qkv_g, o_g, gain_g, down_g = sums
    qkv_g = joined(qkv_g).reshape(1, part, KV_HEADS, 4 * HEAD)
    key_g = qkv_g[..., :HEAD].reshape(1, part, -1)
    value_g = qkv_g[..., HEAD : 2 * HEAD].reshape(1, part, -1)
    query_g = qkv_g[..., 2 * HEAD :].reshape(1, part, -1)
    return (
        out.reshape(1, seqs, rows, width),
        dx.reshape(1, seqs, rows, width),
        gain_g[0, :, 0][None],
        query_g,
        key_g,
        value_g,
        joined(o_g),
        gain_g[1, :, 0][None],
        joined(gate_g),
        joined(up_g),
        joined(down_g),
    )


def solution(mesh):
    split = ("dp", "seq")
    matrix = P("section", split, None)
    vector = P("section", split)
    rows = P("dp", "seq", None)
    layer = P("section", "dp", "seq", None)
    return jax.shard_map(
        body,
        mesh=mesh,
        in_specs=(
            rows, P("dp"), rows, vector, matrix, matrix, matrix, matrix, vector, matrix, matrix, matrix
        ),
        out_specs=(
            layer, layer, vector, matrix, matrix, matrix, matrix, vector, matrix, matrix, matrix
        ),
        check_vma=False,
    )
```

```python
import functools
import math

import jax
import jax.numpy as jnp
from jax import lax
from jax.experimental import pallas as pl
from jax.experimental.pallas import tpu as pltpu
from jax.sharding import PartitionSpec as P

HEADS = 16
KV_HEADS = 8
HEAD = 96
LANES = 128
EPS = 1e-05
ROPE_BASE = 100000.0
NEG = -1e30
PREFIX_MAX = 1024
SCALE = 1.0 / math.sqrt(HEAD)
MESH = pl.DeviceIdType.MESH
ANY = pl.BlockSpec(memory_space=pl.ANY)
VMEM = pl.BlockSpec(memory_space=pltpu.VMEM)
SMEM = pl.BlockSpec(memory_space=pltpu.SMEM)
MIB = 1 << 20

PIECES = (
    (24, 2048, "y", 1),
    (24, 2048, "y", -1),
    (24, 1536, "z", 1),
    (24, 768, "z", 1),
    (24, 128, "z", 1),
    (64, 768, "z", -1),
)
OTHER = {"y": "z", "z": "y"}


def f32dot(a, b, dims):
    return lax.dot_general(a, b, (dims, ((), ())), preferred_element_type=jnp.float32)


class Place:
    def __init__(self):
        self.s = lax.axis_index("section")
        self.d = lax.axis_index("dp")
        self.q = lax.axis_index("seq")
        self.y = lax.div(self.q, 8)
        self.z = lax.rem(lax.div(self.q, 2), 4)
        self.c = lax.rem(self.q, 2)

    def coord(self, axis):
        return self.y if axis == "y" else self.z

    def step(self, axis, by):
        y, z = self.y, self.z
        if axis == "y":
            y = lax.rem(y + by + 4, 4)
        else:
            z = lax.rem(z + by + 4, 4)
        return (self.s, self.d, y * 8 + z * 2 + self.c)

    def sibling(self):
        return (self.s, self.d, self.q + 1 - 2 * self.c)

    def dp_peer(self):
        return (self.s, 1 - self.d, self.q)


def meet(devices):
    barrier = pltpu.get_barrier_semaphore()
    for device in devices:
        pl.semaphore_signal(barrier, inc=1, device_id=device, device_id_type=MESH)
    pl.semaphore_wait(barrier, len(devices))


def remote(src, dst, send, recv, device):
    return pltpu.make_async_remote_copy(
        src_ref=src, dst_ref=dst, send_sem=send, recv_sem=recv, device_id=device, device_id_type=MESH
    )


def gather_kernel(*refs):
    n = len(PIECES)
    ins, outs = refs[:n], refs[n : 2 * n]
    give, got, chip = refs[2 * n : 3 * n], refs[3 * n : 4 * n], refs[4 * n : 5 * n]
    first, local, over, ring_s, ring_r, sib_s, sib_r = refs[5 * n :]
    me = Place()
    meet(
        [me.step("y", 1), me.step("y", -1), me.step("z", 1), me.step("z", -1), me.dp_peer(), me.sibling()]
    )
    pending = []
    swaps = []
    for i, (rows, width, _, _) in enumerate(PIECES):
        start = pl.multiple_of((1 - me.c) * width, LANES)
        give[i][...] = ins[i][:, pl.ds(start, width)].astype(jnp.float32)
        cp = remote(give[i], got[i], first.at[0, i], first.at[1, i], me.sibling())
        cp.start()
        swaps.append(cp)

    def shard(i, dp, y, z):
        width = PIECES[i][1]
        return outs[i].at[dp, y, z, :, pl.ds(pl.multiple_of(me.c * width, LANES), width)]

    def column(i, dp, pos):
        width = PIECES[i][1]
        lanes = pl.ds(pl.multiple_of(me.c * width, LANES), width)
        if PIECES[i][2] == "y":
            return outs[i].at[dp, pl.ds(0, 4), pos, :, lanes]
        return outs[i].at[dp, pos, pl.ds(0, 4), :, lanes]

    def along(i, dp, by):
        a1 = PIECES[i][2]
        pos = lax.rem(me.coord(a1) + by + 4, 4)
        return shard(i, dp, pos, me.z) if a1 == "y" else shard(i, dp, me.y, pos)

    def across(i, dp, by):
        a2 = OTHER[PIECES[i][2]]
        return column(i, dp, lax.rem(me.coord(a2) + by + 4, 4))

    def send(i, block, k, src, dst, device):
        cp = remote(src, dst, ring_s.at[i, block, k], ring_r.at[i, block, k], device)
        cp.start()
        pending.append(cp)
        return cp

    def share(i, block, k, ref):
        cp = remote(ref, ref, sib_s.at[i, block, k], sib_r.at[i, block, k], me.sibling())
        cp.start()
        pending.append(cp)
        shares.append(cp)

    shares = []
    dps = (me.d, 1 - me.d)
    one, two, locals_, overs = {}, {}, [], []
    for i, (rows, width, a1, _) in enumerate(PIECES):
        swaps[i].wait()
        start = pl.multiple_of(me.c * width, LANES)
        mine = ins[i][:, pl.ds(start, width)].astype(jnp.float32)
        theirs = got[i][...]
        low = jnp.where(me.c == 0, mine, theirs)
        high = jnp.where(me.c == 0, theirs, mine)
        chip[i][...] = jnp.concatenate([low, high], axis=0).astype(jnp.bfloat16)
        here = along(i, me.d, 0)
        one[i, 0, 1] = send(i, 0, 0, chip[i], here, me.step(a1, 1))
        one[i, 0, -1] = send(i, 0, 1, chip[i], here, me.step(a1, -1))
        cp = remote(chip[i], here, over.at[0, i], over.at[1, i], me.dp_peer())
        cp.start()
        overs.append(cp)
        cp = pltpu.make_async_copy(chip[i], here, local.at[i])
        cp.start()
        locals_.append(cp)
        cp = remote(chip[i], here, sib_s.at[i, 0, 0], sib_r.at[i, 0, 0], me.sibling())
        cp.start()
        pending.append(cp)
        shares.append(cp)

    def ring_one_end(block):
        dp = dps[block]
        for i, (_, _, a1, sign) in enumerate(PIECES):
            one[i, block, sign].wait_recv()
            came = along(i, dp, -sign)
            one[i, block, 0] = send(i, block, 2, came, came, me.step(a1, sign))
            share(i, block, 1, came)
        for i, (_, _, a1, sign) in enumerate(PIECES):
            one[i, block, -sign].wait_recv()
            share(i, block, 2, along(i, dp, sign))

    def ring_two_start(block):
        dp = dps[block]
        for i, (_, _, a1, sign) in enumerate(PIECES):
            one[i, block, 0].wait_recv()
            share(i, block, 3, along(i, dp, 2))
            if block == 0:
                locals_[i].wait()
            here = across(i, dp, 0)
            a2 = OTHER[a1]
            two[i, block, sign] = send(i, block, 3, here, here, me.step(a2, sign))
            two[i, block, -sign] = send(i, block, 4, here, here, me.step(a2, -sign))

    def ring_two_end(block):
        dp = dps[block]
        for i, (_, _, a1, sign) in enumerate(PIECES):
            two[i, block, sign].wait_recv()
            came = across(i, dp, -sign)
            two[i, block, 0] = send(i, block, 5, came, came, me.step(OTHER[a1], sign))
            share(i, block, 4, came)
        for i, (_, _, a1, sign) in enumerate(PIECES):
            two[i, block, -sign].wait_recv()
            share(i, block, 5, across(i, dp, sign))

    def finish(block):
        for i in range(n):
            two[i, block, 0].wait_recv()
            share(i, block, 6, across(i, dps[block], 2))

    ring_one_end(0)
    ring_two_start(0)
    for i, (_, _, a1, _) in enumerate(PIECES):
        overs[i].wait_recv()
        here = along(i, dps[1], 0)
        one[i, 1, 1] = send(i, 1, 0, here, here, me.step(a1, 1))
        one[i, 1, -1] = send(i, 1, 1, here, here, me.step(a1, -1))
        share(i, 1, 0, here)
    ring_two_end(0)
    ring_one_end(1)
    ring_two_start(1)
    finish(0)
    ring_two_end(1)
    finish(1)
    for cp in shares:
        cp.wait_recv()
    for cp in pending:
        cp.wait_send()
    for cp in overs:
        cp.wait_send()


def gather_weights(shards):
    n = len(PIECES)
    outs = pl.pallas_call(
        gather_kernel,
        out_shape=[
            jax.ShapeDtypeStruct((2, 4, 4, 2 * rows, 2 * width), jnp.bfloat16) for rows, width, _, _ in PIECES
        ],
        in_specs=[VMEM] * n,
        out_specs=[ANY] * n,
        scratch_shapes=[pltpu.VMEM((rows, width), jnp.float32) for rows, width, _, _ in PIECES]
        + [pltpu.VMEM((rows, width), jnp.float32) for rows, width, _, _ in PIECES]
        + [pltpu.VMEM((2 * rows, width), jnp.bfloat16) for rows, width, _, _ in PIECES]
        + [
            pltpu.SemaphoreType.DMA((2, n)),
            pltpu.SemaphoreType.DMA((n,)),
            pltpu.SemaphoreType.DMA((2, n)),
            pltpu.SemaphoreType.DMA((n, 2, 6)),
            pltpu.SemaphoreType.DMA((n, 2, 6)),
            pltpu.SemaphoreType.DMA((n, 2, 7)),
            pltpu.SemaphoreType.DMA((n, 2, 7)),
        ],
        compiler_params=pltpu.CompilerParams(
            collective_id=1, has_side_effects=True, vmem_limit_bytes=60 * MIB
        ),
        name="gather_weights",
    )(*shards)
    return [
        out.reshape(64 * rows, 2 * width) for out, (rows, width, _, _) in zip(outs, PIECES, strict=True)
    ]


def add_into(total, term):
    chunks = total.shape[1] // 16

    def step(k, carry):
        j = lax.div(k, chunks)
        rows = pl.ds(pl.multiple_of(lax.rem(k, chunks) * 16, 16), 16)
        both = total[j, rows, :].astype(jnp.float32) + term[j, rows, :].astype(jnp.float32)
        total[j, rows, :] = both.astype(jnp.bfloat16)
        return carry

    lax.fori_loop(0, total.shape[0] * chunks, step, 0)


def add_two(total, left, right):
    chunks = total.shape[1] // 16

    def step(k, carry):
        j = lax.div(k, chunks)
        rows = pl.ds(pl.multiple_of(lax.rem(k, chunks) * 16, 16), 16)
        parts = [ref[j, rows, :].astype(jnp.float32) for ref in (total, left, right)]
        total[j, rows, :] = (parts[0] + (parts[1] + parts[2])).astype(jnp.bfloat16)
        return carry

    lax.fori_loop(0, total.shape[0] * chunks, step, 0)


def scatter_kernel(*refs):
    n = len(PIECES)
    take = iter(range(0, 100 * n, n))

    def group():
        k = next(take)
        return refs[k : k + n]

    ins, outs = group(), group()
    near, far, last, mid, own = group(), group(), group(), group(), group()
    near1, far1, last1 = group(), group(), group()
    sent, came, total = group(), group(), group()
    load, ring_s, ring_r, over, fin, keep = refs[13 * n :]
    me = Place()
    meet(
        [me.step("y", 1), me.step("y", -1), me.step("z", 1), me.step("z", -1), me.dp_peer(), me.sibling()]
    )
    dps = (1 - me.d, me.d)
    pending = []

    def column(i, block, by):
        a2 = OTHER[PIECES[i][2]]
        pos = lax.rem(me.coord(a2) + by + 4, 4)
        if a2 == "y":
            return ins[i].at[dps[block], pos, pl.ds(0, 4)]
        return ins[i].at[dps[block], pl.ds(0, 4), pos]

    def send(i, block, k, src, dst, device):
        cp = remote(src, dst, ring_s.at[i, block, k], ring_r.at[i, block, k], device)
        cp.start()
        pending.append(cp)
        return cp

    loads, one, two = {}, {}, {}
    for block in range(2):
        for i, (_, _, a1, sign) in enumerate(PIECES):
            a2 = OTHER[a1]
            one[i, block, 0] = send(i, block, 0, column(i, block, 2 * sign), near[i].at[block], me.step(a2, sign))
        for i, (_, _, a1, sign) in enumerate(PIECES):
            a2 = OTHER[a1]
            one[i, block, 1] = send(i, block, 1, column(i, block, -sign), far[i].at[block], me.step(a2, -sign))
        for i, (_, _, a1, sign) in enumerate(PIECES):
            cp = pltpu.make_async_copy(column(i, block, sign), mid[i].at[block], load.at[0, i, block])
            cp.start()
            loads[i, block, 0] = cp
            cp = pltpu.make_async_copy(column(i, block, 0), own[i].at[block], load.at[1, i, block])
            cp.start()
            loads[i, block, 1] = cp
    for block in range(2):
        for i, (_, _, a1, sign) in enumerate(PIECES):
            one[i, block, 0].wait_recv()
            loads[i, block, 0].wait()
            add_into(near[i].at[block], mid[i].at[block])
            one[i, block, 2] = send(
                i, block, 2, near[i].at[block], last[i].at[block], me.step(OTHER[a1], sign)
            )
    overs = []
    for block in range(2):
        for i, (_, _, a1, sign) in enumerate(PIECES):
            one[i, block, 1].wait_recv()
            loads[i, block, 1].wait()
            one[i, block, 2].wait_recv()
            add_two(own[i].at[block], far[i].at[block], last[i].at[block])
            pos = me.coord(a1)
            far_place = lax.rem(pos + 2, 4)
            two[i, block, 0] = send(
                i, block, 3, own[i].at[block, far_place], near1[i].at[block], me.step(a1, sign)
            )
            back_place = lax.rem(pos - sign + 4, 4)
            two[i, block, 1] = send(
                i, block, 4, own[i].at[block, back_place], far1[i].at[block], me.step(a1, -sign)
            )
        for i, (_, _, a1, sign) in enumerate(PIECES):
            two[i, block, 0].wait_recv()
            place = lax.rem(me.coord(a1) + sign + 4, 4)
            add_into(near1[i].at[pl.ds(block, 1)], own[i].at[block, pl.ds(place, 1)])
            two[i, block, 2] = send(
                i, block, 5, near1[i].at[block], last1[i].at[block], me.step(a1, sign)
            )
        for i, (rows, width, a1, sign) in enumerate(PIECES):
            two[i, block, 1].wait_recv()
            two[i, block, 2].wait_recv()
            pos = me.coord(a1)
            if block == 1:
                overs[i].wait_recv()

            def step(k, carry, i=i, block=block, pos=pos):
                part = pl.ds(pl.multiple_of(k * 16, 16), 16)
                both = far1[i][block, part, :].astype(jnp.float32) + last1[i][block, part, :].astype(
                    jnp.float32
                )
                both = both + own[i][block, pos, part, :].astype(jnp.float32)
                if block == 0:
                    sent[i][part, :] = both.astype(jnp.bfloat16)
                else:
                    total[i][part, :] = both + came[i][part, :].astype(jnp.float32)
                return carry

            lax.fori_loop(0, 2 * rows // 16, step, 0)
            if block == 0:
                cp = remote(sent[i], came[i], over.at[0, i], over.at[1, i], me.dp_peer())
                cp.start()
                overs.append(cp)
            else:
                mine = total[i].at[pl.ds(pl.multiple_of(me.c * rows, 8), rows)]
                theirs = total[i].at[pl.ds(pl.multiple_of((1 - me.c) * rows, 8), rows)]
                place = outs[i].at[:, pl.ds(pl.multiple_of(me.c * width, LANES), width)]
                cp = pltpu.make_async_copy(mine, place, keep.at[i])
                cp.start()
                loads[i, "keep"] = cp
                cp = remote(theirs, place, fin.at[0, i], fin.at[1, i], me.sibling())
                cp.start()
                loads[i, "fin"] = cp
    for i in range(n):
        loads[i, "keep"].wait()
        loads[i, "fin"].wait()
    for cp in pending:
        cp.wait_send()
    for cp in overs:
        cp.wait_send()


def scatter_grads(parts):
    n = len(PIECES)
    shapes = [(2 * rows, width) for rows, width, _, _ in PIECES]
    bf16 = jnp.bfloat16
    return pl.pallas_call(
        scatter_kernel,
        out_shape=[jax.ShapeDtypeStruct((rows, 2 * width), jnp.float32) for rows, width, _, _ in PIECES],
        in_specs=[ANY] * n,
        out_specs=[ANY] * n,
        scratch_shapes=[pltpu.VMEM((2, 4, *shape), bf16) for _ in range(5) for shape in shapes]
        + [pltpu.VMEM((2, *shape), bf16) for _ in range(3) for shape in shapes]
        + [pltpu.VMEM(shape, bf16) for _ in range(2) for shape in shapes]
        + [pltpu.VMEM(shape, jnp.float32) for shape in shapes]
        + [
            pltpu.SemaphoreType.DMA((2, n, 2)),
            pltpu.SemaphoreType.DMA((n, 2, 6)),
            pltpu.SemaphoreType.DMA((n, 2, 6)),
            pltpu.SemaphoreType.DMA((2, n)),
            pltpu.SemaphoreType.DMA((2, n)),
            pltpu.SemaphoreType.DMA((n,)),
        ],
        compiler_params=pltpu.CompilerParams(
            collective_id=2, has_side_effects=True, vmem_limit_bytes=56 * MIB
        ),
        name="scatter_grads",
    )(*[part.reshape(2, 4, 4, *shape) for part, shape in zip(parts, shapes, strict=True)])


ORIGINS = 32
BLOCK = 8
BLOCKS = ORIGINS // BLOCK


def meet_plane(me):
    barrier = pltpu.get_barrier_semaphore()

    def greet(k, carry):
        to = lax.rem(me.q + k, ORIGINS)
        pl.semaphore_signal(barrier, inc=1, device_id=(me.s, me.d, to), device_id_type=MESH)
        return carry

    lax.fori_loop(1, ORIGINS, greet, 0)
    pl.semaphore_wait(barrier, ORIGINS - 1)


class Exchange:
    def __init__(self, me, src, dst_of, sems):
        self.me, self.src, self.dst_of, self.sems = me, src, dst_of, sems

    def copy(self, origin, to):
        me, (send, recv, _) = self.me, self.sems
        peer = to + origin - me.q
        return remote(
            self.src.at[to], self.dst_of(origin, to), send.at[to], recv.at[origin], (me.s, me.d, peer)
        )

    def own(self):
        q = self.me.q
        return pltpu.make_async_copy(self.src.at[q], self.dst_of(q, q), self.sems[2].at[0])

    def start_all(self):
        self.own().start()

        def step(k, carry):
            self.copy(self.me.q, lax.rem(self.me.q + k, ORIGINS)).start()
            return carry

        lax.fori_loop(1, ORIGINS, step, 0)

    def start(self, block):
        def step(k, carry):
            to = block * BLOCK + lax.rem(self.me.q + k, BLOCK)

            @pl.when(to == self.me.q)
            def _():
                self.own().start()

            @pl.when(to != self.me.q)
            def _():
                self.copy(self.me.q, to).start()

            return carry

        lax.fori_loop(0, BLOCK, step, 0)

    def arrived(self, first, count):
        def step(k, carry):
            origin = first + k

            @pl.when(origin == self.me.q)
            def _():
                self.own().wait()

            @pl.when(origin != self.me.q)
            def _():
                self.copy(origin, self.me.q).wait_recv()

            return carry

        lax.fori_loop(0, count, step, 0)

    def sent(self):
        def step(k, carry):
            self.copy(self.me.q, lax.rem(self.me.q + k, ORIGINS)).wait_send()
            return carry

        lax.fori_loop(1, ORIGINS, step, 0)


EXCHANGE_SEMS = [
    pltpu.SemaphoreType.DMA((ORIGINS,)),
    pltpu.SemaphoreType.DMA((ORIGINS,)),
    pltpu.SemaphoreType.DMA((1,)),
]


def block_mask(block, keys, core, prefix_len):
    rows = BLOCK * 32
    row = lax.broadcasted_iota(jnp.int32, (rows, keys), 0)
    key = lax.broadcasted_iota(jnp.int32, (rows, keys), 1)
    pos = block * BLOCK * 64 + 64 * (row // 32) + 32 * core + row % 32
    return (key <= pos) | (key < prefix_len)


def keys_of(block):
    return max((block + 1) * BLOCK * 64, PREFIX_MAX)


def group(block):
    return pl.ds(block * BLOCK, BLOCK)


def attend_steps(me, prefix, src, whole, dst, out, there, back, sib):
    prefix_len = prefix[0]
    coming = Exchange(me, src, lambda origin, to: whole.at[origin, lax.rem(to, 2)], there)
    going = Exchange(me, out, lambda origin, to: dst.at[origin], back)
    coming.start_all()
    yield
    shares = []
    for block in range(BLOCKS):
        coming.arrived(block * BLOCK, BLOCK)
        mine = whole.at[group(block), me.c]
        cp = remote(mine, mine, sib.at[0, block], sib.at[1, block], me.sibling())
        cp.start()
        shares.append(cp)
    ready = 0
    for block in range(BLOCKS):
        keys = keys_of(block)
        while ready * BLOCK * 64 < keys:
            shares[ready].wait_recv()
            ready += 1
        src_rows = group(block)
        k = whole[pl.ds(0, keys // 64), :, :, 0:128].reshape(keys, LANES)
        v = whole[pl.ds(0, keys // 64), :, :, 128:256].reshape(keys, LANES)
        allowed = block_mask(block, keys, me.c, prefix_len)
        for h in range(2):
            lanes = slice(256 + 128 * h, 384 + 128 * h)
            q = whole[src_rows, me.c, :, lanes].reshape(BLOCK * 32, LANES)
            s = jnp.where(allowed, f32dot(q, k, ((1,), (1,))) * SCALE, NEG)
            top = jnp.max(s, axis=-1, keepdims=True)
            e = jnp.exp(s - top)
            p = (e * (1.0 / jnp.sum(e, axis=-1, keepdims=True))).astype(jnp.bfloat16)
            o = f32dot(p, v, ((1,), (0,)))
            out[src_rows, :, 128 * h : 128 * h + 128] = o.astype(jnp.bfloat16).reshape(BLOCK, 32, LANES)
        going.start(block)
        yield
    going.arrived(0, ORIGINS)
    coming.sent()
    going.sent()
    for cp in shares:
        cp.wait_send()


ATTEND_SCRATCH = [
    pltpu.VMEM((ORIGINS, 32, 256), jnp.bfloat16),
    *EXCHANGE_SEMS,
    *EXCHANGE_SEMS,
    pltpu.SemaphoreType.DMA((2, BLOCKS)),
]


def attend_kernel(prefix, src, whole, dst, out, *sems):
    me = Place()
    meet_plane(me)
    for _ in attend_steps(me, prefix, src, whole, dst, out, sems[:3], sems[3:6], sems[6]):
        pass


def attend(prefix, src):
    _, rows, width = src.shape
    return pl.pallas_call(
        attend_kernel,
        out_shape=[
            jax.ShapeDtypeStruct((ORIGINS, 2, rows, width), jnp.bfloat16),
            jax.ShapeDtypeStruct((ORIGINS, rows, width // 2), jnp.bfloat16),
        ],
        in_specs=[SMEM, VMEM],
        out_specs=[VMEM, VMEM],
        scratch_shapes=ATTEND_SCRATCH,
        compiler_params=pltpu.CompilerParams(
            collective_id=3, has_side_effects=True, vmem_limit_bytes=56 * MIB
        ),
        name="attend",
    )(prefix, src)


def attend_back_steps(me, prefix, whole, src, dst, datt, acc, theirs, dq, bundle, there, back, sib):
    prefix_len = prefix[0]
    coming = Exchange(me, src, lambda origin, to: datt.at[origin], there)
    going = Exchange(me, bundle, lambda origin, to: dst.at[origin], back)
    coming.start_all()
    yield
    coming.arrived(0, ORIGINS)
    shares = {}

    def share(block):
        cp = remote(
            acc.at[group(block), 1 - me.c],
            theirs.at[group(block)],
            sib.at[0, block],
            sib.at[1, block],
            me.sibling(),
        )
        cp.start()
        shares[block] = cp

    def finish(block):
        shares[block].wait_recv()

        def step(i, carry):
            both = acc[block * BLOCK + i, me.c] + theirs[block * BLOCK + i]
            bundle[block * BLOCK + i, :, 0:128] = (both[:, 0:128] * SCALE).astype(jnp.bfloat16)
            bundle[block * BLOCK + i, :, 128:256] = both[:, 128:256].astype(jnp.bfloat16)
            bundle[block * BLOCK + i, :, 256:512] = dq[block * BLOCK + i]
            return carry

        lax.fori_loop(0, BLOCK, step, 0)
        going.start(block)

    for block in reversed(range(BLOCKS)):
        keys = keys_of(block)
        spread = pl.ds(0, keys // 64)
        src_rows = group(block)
        k = whole[spread, :, :, 0:128].reshape(keys, LANES)
        v = whole[spread, :, :, 128:256].reshape(keys, LANES)
        allowed = block_mask(block, keys, me.c, prefix_len)
        for h in range(2):
            lanes = slice(256 + 128 * h, 384 + 128 * h)
            q = whole[src_rows, me.c, :, lanes].reshape(BLOCK * 32, LANES)
            g = datt[src_rows, :, 128 * h : 128 * h + 128].reshape(BLOCK * 32, LANES)
            s = jnp.where(allowed, f32dot(q, k, ((1,), (1,))) * SCALE, NEG)
            top = jnp.max(s, axis=-1, keepdims=True)
            e = jnp.exp(s - top)
            p = e * (1.0 / jnp.sum(e, axis=-1, keepdims=True))
            dp = f32dot(g, v, ((1,), (1,)))
            delta = jnp.sum(p * dp, axis=-1, keepdims=True)
            ds = (p * (dp - delta)).astype(jnp.bfloat16)
            dq[src_rows, :, 128 * h : 128 * h + 128] = (
                (f32dot(ds, k, ((1,), (0,))) * SCALE).astype(jnp.bfloat16).reshape(BLOCK, 32, LANES)
            )
            dk = f32dot(ds, q, ((0,), (0,))).reshape(keys // 64, 2, 32, LANES)
            dv = f32dot(p.astype(jnp.bfloat16), g, ((0,), (0,))).reshape(keys // 64, 2, 32, LANES)
            if block == BLOCKS - 1 and h == 0:
                acc[spread, :, :, 0:128] = dk
                acc[spread, :, :, 128:256] = dv
            else:
                acc[spread, :, :, 0:128] += dk
                acc[spread, :, :, 128:256] += dv
        if block >= 2:
            share(block)
        if block == 2:
            finish(3)
        if block == 1:
            finish(2)
        if block == 0:
            share(1)
            share(0)
            finish(1)
            finish(0)
        yield
    going.arrived(0, ORIGINS)
    coming.sent()
    going.sent()
    for cp in shares.values():
        cp.wait_send()


ATTEND_BACK_SCRATCH = [
    pltpu.VMEM((ORIGINS, 32, 256), jnp.bfloat16),
    pltpu.VMEM((ORIGINS, 2, 32, 256), jnp.float32),
    pltpu.VMEM((ORIGINS, 32, 256), jnp.float32),
    pltpu.VMEM((ORIGINS, 32, 256), jnp.bfloat16),
    pltpu.VMEM((ORIGINS, 32, 512), jnp.bfloat16),
    *EXCHANGE_SEMS,
    *EXCHANGE_SEMS,
    pltpu.SemaphoreType.DMA((2, BLOCKS)),
]


def attend_back_kernel(prefix, whole, src, dst, *scratch):
    me = Place()
    meet_plane(me)
    sems = scratch[5:]
    for _ in attend_back_steps(
        me, prefix, whole, src, dst, *scratch[:5], sems[:3], sems[3:6], sems[6]
    ):
        pass


def attend_back(prefix, whole, src):
    _, rows, width = src.shape
    return pl.pallas_call(
        attend_back_kernel,
        out_shape=jax.ShapeDtypeStruct((ORIGINS, rows, 2 * width), jnp.bfloat16),
        in_specs=[SMEM, VMEM, VMEM],
        out_specs=VMEM,
        scratch_shapes=ATTEND_BACK_SCRATCH,
        compiler_params=pltpu.CompilerParams(
            collective_id=4, has_side_effects=True, vmem_limit_bytes=56 * MIB
        ),
        name="attend_back",
    )(prefix, whole, src)


def pair_kernel(whole_count, *refs):
    n = (len(refs) - 3) // 2
    ins, outs = refs[:n], refs[n : 2 * n]
    send_sem, recv_sem, own_sem = refs[2 * n :]
    me = Place()
    meet([me.sibling()])
    copies = []
    for i in range(n):
        here = there = ins[i]
        if i >= whole_count:
            width = ins[i].shape[1] // 2
            here = ins[i].at[:, pl.ds(pl.multiple_of(me.c * width, LANES), width)]
            there = ins[i].at[:, pl.ds(pl.multiple_of((1 - me.c) * width, LANES), width)]
        cp = remote(there, outs[i].at[me.c], send_sem.at[i], recv_sem.at[i], me.sibling())
        cp.start()
        copies.append(cp)
        cp = pltpu.make_async_copy(here, outs[i].at[me.c], own_sem.at[i])
        cp.start()
        copies.append(cp)
    for cp in copies:
        cp.wait()


def pair_up(whole, halved):
    n = len(whole) + len(halved)
    return pl.pallas_call(
        functools.partial(pair_kernel, len(whole)),
        out_shape=[jax.ShapeDtypeStruct((2, *a.shape), a.dtype) for a in whole]
        + [jax.ShapeDtypeStruct((2, a.shape[0], a.shape[1] // 2), a.dtype) for a in halved],
        in_specs=[VMEM] * n,
        out_specs=[VMEM] * n,
        scratch_shapes=[pltpu.SemaphoreType.DMA((n,))] * 3,
        compiler_params=pltpu.CompilerParams(
            collective_id=6, has_side_effects=True, vmem_limit_bytes=40 * MIB
        ),
        name="pair_up",
    )(*whole, *halved)


STEPS = 8
FF_BLOCK = 512
HALF = HEAD // 2


def rope_tables(positions):
    lane = jnp.arange(LANES)
    frequency = ROPE_BASE ** (-(lane % HALF).astype(jnp.float32) * 2.0 / HEAD)
    angles = positions.astype(jnp.float32)[:, None] * frequency[None, :]
    cos, sin = jnp.cos(angles), jnp.sin(angles)
    low, high = (lane < HALF)[None, :], ((lane >= HALF) & (lane < HEAD))[None, :]
    return (
        jnp.where(low | high, cos, 0.0),
        jnp.where(low, -sin, 0.0),
        jnp.where(high, sin, 0.0),
    )


def split_four(y):
    return [y[:, :LANES]] + [pltpu.roll(y, 4 * HEAD - HEAD * h, axis=1)[:, :LANES] for h in (1, 2, 3)]


def pack_four(heads):
    zero = jnp.zeros((heads[0].shape[0], 2 * LANES), jnp.float32)
    wide = [jnp.concatenate([z, zero], axis=1) for z in heads]
    total = wide[0]
    for h in (1, 2, 3):
        total = total + pltpu.roll(wide[h], HEAD * h, axis=1)
    return total


def turn(z, cos, ahead, back):
    return z * cos + pltpu.roll(z, LANES - HALF, axis=1) * ahead + pltpu.roll(z, HALF, axis=1) * back


def qkv_kernel(x, gain, w, cos, ahead, back, bundle, normed):
    @pl.when(pl.program_id(0) == 0)
    def _():
        hidden = x[...].astype(jnp.float32)
        r1 = lax.rsqrt(jnp.mean(hidden * hidden, axis=-1, keepdims=True) + EPS)
        normed[...] = (hidden * r1 * gain[...]).astype(jnp.bfloat16)

    y = f32dot(normed[...], w[...], ((1,), (0,)))
    tokens = y.shape[0] // 2
    inside = lax.broadcasted_iota(jnp.int32, (2 * tokens, LANES), 1) < HEAD
    for h, z in enumerate(split_four(y)):
        z = jnp.where(inside, z, 0.0) if h == 1 else turn(z, cos[...], ahead[...], back[...])
        z = z.astype(jnp.bfloat16)
        for s in range(2):
            bundle[s, 0, :, LANES * h : LANES * (h + 1)] = z[s * tokens : (s + 1) * tokens]


def whole_spec(a):
    return pl.BlockSpec(a.shape, lambda k: (0,) * a.ndim, pipeline_mode=pl.Buffered(1))


def project(x, gain, w, tables):
    tokens, width = x.shape
    return pl.pallas_call(
        qkv_kernel,
        grid=(KV_HEADS,),
        out_shape=[
            jax.ShapeDtypeStruct((2, KV_HEADS, tokens // 2, 4 * LANES), jnp.bfloat16),
            jax.ShapeDtypeStruct((tokens, width), jnp.bfloat16),
        ],
        in_specs=[
            whole_spec(x),
            whole_spec(gain),
            pl.BlockSpec((width, 4 * HEAD), lambda k: (0, k)),
            *[whole_spec(t) for t in tables],
        ],
        out_specs=[
            pl.BlockSpec((2, 1, tokens // 2, 4 * LANES), lambda k: (0, k, 0, 0)),
            pl.BlockSpec((tokens, width), lambda k: (0, 0)),
        ],
        compiler_params=pltpu.CompilerParams(vmem_limit_bytes=56 * MIB),
        name="project",
    )(x, gain, w, *tables)


def mlp_kernel(
    att, x, gain, o_w, gate_w, up_w, down_w, result, attended, middle, normed_two, gate, up, mixed, total
):
    k = pl.program_id(0)

    @pl.when(k == 0)
    def _():
        for pair in range(KV_HEADS // 2):
            heads = []
            for g in (2 * pair, 2 * pair + 1):
                for h in range(2):
                    lanes = slice(LANES * h, LANES * (h + 1))
                    heads.append(
                        jnp.concatenate([att[0, g, :, lanes], att[1, g, :, lanes]], axis=0).astype(jnp.float32)
                    )
            attended[:, 384 * pair : 384 * (pair + 1)] = pack_four(heads).astype(jnp.bfloat16)
        mid = x[...].astype(jnp.float32) + f32dot(attended[...], o_w[...], ((1,), (0,)))
        middle[...] = mid
        r2 = lax.rsqrt(jnp.mean(mid * mid, axis=-1, keepdims=True) + EPS)
        normed_two[...] = (mid * r2 * gain[...]).astype(jnp.bfloat16)
        total[...] = mid

    g = f32dot(normed_two[...], gate_w[...], ((1,), (0,)))
    u = f32dot(normed_two[...], up_w[...], ((1,), (0,)))
    gate[...] = g
    up[...] = u
    m = (g * jax.nn.sigmoid(g) * u).astype(jnp.bfloat16)
    mixed[...] = m
    total[...] += f32dot(m, down_w[...], ((1,), (0,)))

    @pl.when(k == STEPS - 1)
    def _():
        result[...] = total[...].astype(jnp.bfloat16)


def mlp(att, x, gain, o_w, gate_w, up_w, down_w):
    tokens, width = x.shape
    ff = gate_w.shape[1]
    in_block = pl.BlockSpec((width, FF_BLOCK), lambda k: (0, k))
    ff_block = pl.BlockSpec((tokens, FF_BLOCK), lambda k: (0, k))
    fixed = pl.BlockSpec((tokens, width), lambda k: (0, 0))
    return pl.pallas_call(
        mlp_kernel,
        grid=(STEPS,),
        out_shape=[
            jax.ShapeDtypeStruct((tokens, width), jnp.bfloat16),
            jax.ShapeDtypeStruct((tokens, width), jnp.bfloat16),
            jax.ShapeDtypeStruct((tokens, width), jnp.float32),
            jax.ShapeDtypeStruct((tokens, width), jnp.bfloat16),
            jax.ShapeDtypeStruct((tokens, ff), jnp.float32),
            jax.ShapeDtypeStruct((tokens, ff), jnp.float32),
            jax.ShapeDtypeStruct((tokens, ff), jnp.bfloat16),
        ],
        in_specs=[
            whole_spec(att),
            whole_spec(x),
            whole_spec(gain),
            whole_spec(o_w),
            in_block,
            in_block,
            pl.BlockSpec((FF_BLOCK, width), lambda k: (k, 0)),
        ],
        out_specs=[fixed, fixed, fixed, fixed, ff_block, ff_block, ff_block],
        scratch_shapes=[pltpu.VMEM((tokens, width), jnp.float32)],
        compiler_params=pltpu.CompilerParams(vmem_limit_bytes=48 * MIB),
        name="mlp",
    )(att, x, gain, o_w, gate_w, up_w, down_w)


def norm_back(dn, gain, u, r):
    scaled = dn * gain
    return r * (scaled - u * jnp.mean(scaled * u, axis=-1, keepdims=True))


def mlp_back_kernel(
    g_low, gate, up, middle, gain, o_w, gate_w, up_w, down_w, dgate, dup, dmiddle, db, dgain, datt, total
):
    k = pl.program_id(0)

    @pl.when(k == 0)
    def _():
        total[...] = jnp.zeros_like(total)

    gm = f32dot(g_low[...], down_w[...], ((1,), (1,)))
    sig = jax.nn.sigmoid(gate[...])
    dg = (gm * up[...] * sig * (1.0 + gate[...] * (1.0 - sig))).astype(jnp.bfloat16)
    du = (gm * (gate[...] * sig)).astype(jnp.bfloat16)
    dgate[...] = dg
    dup[...] = du
    total[...] += f32dot(dg, gate_w[...], ((1,), (1,))) + f32dot(du, up_w[...], ((1,), (1,)))

    @pl.when(k == STEPS - 1)
    def _():
        mid, dn2 = middle[...], total[...]
        r2 = lax.rsqrt(jnp.mean(mid * mid, axis=-1, keepdims=True) + EPS)
        u2 = mid * r2
        dgain[...] = jnp.broadcast_to(jnp.sum(dn2 * u2, axis=0, keepdims=True), dgain.shape)
        dm = g_low[...].astype(jnp.float32) + norm_back(dn2, gain[...], u2, r2)
        dmiddle[...] = dm
        low = dm.astype(jnp.bfloat16)
        db[...] = low
        tokens = low.shape[0] // 2
        inside = lax.broadcasted_iota(jnp.int32, (2 * tokens, LANES), 1) < HEAD
        for pair in range(KV_HEADS // 2):
            y = f32dot(low, o_w[384 * pair : 384 * (pair + 1), :], ((1,), (1,)))
            for i, z in enumerate(split_four(y)):
                z = jnp.where(inside, z, 0.0).astype(jnp.bfloat16)
                lanes = slice(LANES * (i % 2), LANES * (i % 2 + 1))
                for s in range(2):
                    datt[s, 2 * pair + i // 2, :, lanes] = z[s * tokens : (s + 1) * tokens]


def mlp_back(g_low, gate, up, middle, gain, o_w, gate_w, up_w, down_w):
    tokens, width = g_low.shape
    ff = gate_w.shape[1]
    in_block = pl.BlockSpec((width, FF_BLOCK), lambda k: (0, k))
    ff_block = pl.BlockSpec((tokens, FF_BLOCK), lambda k: (0, k))
    fixed = pl.BlockSpec((tokens, width), lambda k: (0, 0))
    datt_shape = (2, KV_HEADS, tokens // 2, 2 * LANES)
    return pl.pallas_call(
        mlp_back_kernel,
        grid=(STEPS,),
        out_shape=[
            jax.ShapeDtypeStruct((tokens, ff), jnp.bfloat16),
            jax.ShapeDtypeStruct((tokens, ff), jnp.bfloat16),
            jax.ShapeDtypeStruct((tokens, width), jnp.float32),
            jax.ShapeDtypeStruct((tokens, width), jnp.bfloat16),
            jax.ShapeDtypeStruct((8, width), jnp.float32),
            jax.ShapeDtypeStruct(datt_shape, jnp.bfloat16),
        ],
        in_specs=[
            whole_spec(g_low),
            ff_block,
            ff_block,
            whole_spec(middle),
            whole_spec(gain),
            whole_spec(o_w),
            in_block,
            in_block,
            pl.BlockSpec((FF_BLOCK, width), lambda k: (k, 0)),
        ],
        out_specs=[
            ff_block,
            ff_block,
            fixed,
            fixed,
            pl.BlockSpec((8, width), lambda k: (0, 0)),
            pl.BlockSpec(datt_shape, lambda k: (0, 0, 0, 0)),
        ],
        scratch_shapes=[pltpu.VMEM((tokens, width), jnp.float32)],
        compiler_params=pltpu.CompilerParams(vmem_limit_bytes=48 * MIB),
        name="mlp_back",
    )(g_low, gate, up, middle, gain, o_w, gate_w, up_w, down_w)


def qkv_back_kernel(back_in, cos, ahead, back, w, x, dmiddle, gain, dqkv, dx, dgain, total):
    k = pl.program_id(0)

    @pl.when(k == 0)
    def _():
        total[...] = jnp.zeros_like(total)

    heads = []
    for h in range(4):
        lanes = slice(LANES * h, LANES * (h + 1))
        z = jnp.concatenate([back_in[0, 0, :, lanes], back_in[1, 0, :, lanes]], axis=0).astype(jnp.float32)
        heads.append(z if h == 1 else turn(z, cos[...], -ahead[...], -back[...]))
    packed = pack_four(heads).astype(jnp.bfloat16)
    dqkv[...] = packed
    total[...] += f32dot(packed, w[...], ((1,), (1,)))

    @pl.when(k == KV_HEADS - 1)
    def _():
        hidden, dn1 = x[...].astype(jnp.float32), total[...]
        r1 = lax.rsqrt(jnp.mean(hidden * hidden, axis=-1, keepdims=True) + EPS)
        u1 = hidden * r1
        dgain[...] = jnp.broadcast_to(jnp.sum(dn1 * u1, axis=0, keepdims=True), dgain.shape)
        dx[...] = (dmiddle[...] + norm_back(dn1, gain[...], u1, r1)).astype(jnp.bfloat16)


def project_back(back_in, tables, w, x, dmiddle, gain):
    tokens, width = x.shape
    return pl.pallas_call(
        qkv_back_kernel,
        grid=(KV_HEADS,),
        out_shape=[
            jax.ShapeDtypeStruct((tokens, 2 * width), jnp.bfloat16),
            jax.ShapeDtypeStruct((tokens, width), jnp.bfloat16),
            jax.ShapeDtypeStruct((8, width), jnp.float32),
        ],
        in_specs=[
            pl.BlockSpec((2, 1, tokens // 2, 4 * LANES), lambda k: (0, k, 0, 0)),
            *[whole_spec(t) for t in tables],
            pl.BlockSpec((width, 4 * HEAD), lambda k: (0, k)),
            whole_spec(x),
            whole_spec(dmiddle),
            whole_spec(gain),
        ],
        out_specs=[
            pl.BlockSpec((tokens, 4 * HEAD), lambda k: (0, k)),
            pl.BlockSpec((tokens, width), lambda k: (0, 0)),
            pl.BlockSpec((8, width), lambda k: (0, 0)),
        ],
        scratch_shapes=[pltpu.VMEM((tokens, width), jnp.float32)],
        compiler_params=pltpu.CompilerParams(vmem_limit_bytes=56 * MIB),
        name="project_back",
    )(back_in, *tables, w, x, dmiddle, gain)


def forward(x, weights, tables, prefix):
    qkv_w, o_w, gate_w, up_w, down_w, gain_attn, gain_mlp = weights
    bundle, normed = project(x, gain_attn, qkv_w, tables)
    seqs, heads, rows, wide = bundle.shape
    whole, out = attend(prefix, bundle.reshape(2 * seqs * heads, rows // 2, wide))
    out = out.reshape(seqs, heads, rows, 2 * LANES)
    result, attended, middle, normed_two, gate, up, mixed = mlp(
        out, x, gain_mlp, o_w, gate_w, up_w, down_w
    )
    return result, (x, normed, whole, attended, middle, normed_two, gate, up, mixed)


def backward(g_low, state, weights, tables, prefix):
    qkv_w, o_w, gate_w, up_w, down_w, gain_attn, gain_mlp = weights
    x, normed, whole, attended, middle, normed_two, gate, up, mixed = state
    dgate, dup, dmiddle, db, dgain_mlp, datt = mlp_back(
        g_low, gate, up, middle, gain_mlp, o_w, gate_w, up_w, down_w
    )
    seqs, heads, rows, wide = datt.shape
    back = attend_back(prefix, whole, datt.reshape(2 * seqs * heads, rows // 2, wide))
    back = back.reshape(seqs, heads, rows, 4 * LANES)
    dqkv, dx, dgain_attn = project_back(back, tables, qkv_w, x, dmiddle, gain_attn)
    return dx, (g_low, dgate, dup, db, dqkv, dgain_attn, dgain_mlp)


def body(
    inputs, prefix, cotangent, attn_gain, w_query, w_key, w_value, w_out, mlp_gain, w_gate, w_up, w_down
):
    seqs, rows, width = inputs.shape
    tokens = seqs * rows
    section = lax.axis_index("section")
    seq = lax.axis_index("seq")
    positions = seq * rows + jnp.arange(rows, dtype=jnp.int32)
    tables = rope_tables(jnp.concatenate([positions, positions]))
    own_prefix = lax.dynamic_slice_in_dim(prefix, seq // 16, 1)

    part = w_query.shape[1]
    qkv_shard = jnp.concatenate(
        [
            w_key[0].reshape(part, KV_HEADS, HEAD),
            w_value[0].reshape(part, KV_HEADS, HEAD),
            w_query[0].reshape(part, KV_HEADS, 2 * HEAD),
        ],
        -1,
    ).reshape(part, 2 * width)
    gains = jnp.concatenate(
        [
            jnp.broadcast_to(attn_gain[0][:, None], (part, LANES)),
            jnp.broadcast_to(mlp_gain[0][:, None], (part, LANES)),
        ],
        -1,
    )
    gate_w, up_w, qkv_w, o_w, gains_w, down_w = gather_weights(
        [w_gate[0], w_up[0], qkv_shard, w_out[0], gains, w_down[0]]
    )
    gain_attn = gains_w[:, 0].astype(jnp.float32)[None, :]
    gain_mlp = gains_w[:, LANES].astype(jnp.float32)[None, :]
    weights = (qkv_w, o_w, gate_w, up_w, down_w, gain_attn, gain_mlp)

    x0 = inputs.reshape(tokens, width)
    out0, _ = forward(x0, weights, tables, own_prefix)
    received = lax.ppermute(out0, "section", [(0, 1)])
    x1 = jnp.where(section == 0, x0, received)
    out, state = forward(x1, weights, tables, own_prefix)

    g0 = cotangent.reshape(tokens, width)
    dx0, _ = backward(g0, state, weights, tables, own_prefix)
    received = lax.ppermute(dx0, "section", [(1, 0)])
    g1 = jnp.where(section == 1, g0, received)
    dx, (g_low, dgate, dup, db, dqkv, dgain_attn, dgain_mlp) = backward(g1, state, weights, tables, own_prefix)

    _, normed, _, attended, _, normed_two, _, _, mixed = state
    dgains = jnp.concatenate([dgain_attn, dgain_mlp], axis=1)
    normed, attended, normed_two, mixed, g_half, dgate, dup, db, dqkv, dgains = pair_up(
        [normed, attended, normed_two, mixed], [g_low, dgate, dup, db, dqkv, dgains]
    )

    def outer(a, b):
        a, b = a.reshape(2 * tokens, -1), b.reshape(2 * tokens, -1)
        return lax.dot_general(
            a, b, (((0,), (0,)), ((), ())), preferred_element_type=jnp.float32
        ).astype(jnp.bfloat16)

    gain_part = jnp.broadcast_to(
        (dgains[0, 0] + dgains[1, 0]).astype(jnp.bfloat16)[:, None], (width, LANES)
    )
    gate_g, up_g, qkv_g, o_g, gain_g, down_g = scatter_grads(
        [
            outer(normed_two, dgate),
            outer(normed_two, dup),
            outer(normed, dqkv),
            outer(attended, db),
            gain_part,
            outer(mixed, g_half),
        ]
    )
    qkv_g = qkv_g.reshape(1, part, KV_HEADS, 4 * HEAD)
    key_g = qkv_g[..., :HEAD].reshape(1, part, -1)
    value_g = qkv_g[..., HEAD : 2 * HEAD].reshape(1, part, -1)
    query_g = qkv_g[..., 2 * HEAD :].reshape(1, part, -1)
    return (
        out.reshape(1, seqs, rows, width),
        dx.reshape(1, seqs, rows, width),
        gain_g[:, 0][None],
        query_g,
        key_g,
        value_g,
        o_g[None],
        gain_g[:, LANES][None],
        gate_g[None],
        up_g[None],
        down_g[None],
    )


def solution(mesh):
    split = ("dp", "seq")
    matrix = P("section", split, None)
    vector = P("section", split)
    rows = P("dp", "seq", None)
    layer = P("section", "dp", "seq", None)
    return jax.shard_map(
        body,
        mesh=mesh,
        in_specs=(
            rows, P("dp"), rows, vector, matrix, matrix, matrix, matrix, vector, matrix, matrix, matrix
        ),
        out_specs=(
            layer, layer, vector, matrix, matrix, matrix, matrix, vector, matrix, matrix, matrix
        ),
        check_vma=False,
    )
```

```python
import functools
import math

import jax
import jax.numpy as jnp
from jax import lax
from jax.experimental import pallas as pl
from jax.experimental.pallas import tpu as pltpu
from jax.sharding import PartitionSpec as P

HEADS = 16
KV_HEADS = 8
HEAD = 96
LANES = 128
HALF = HEAD // 2
PACKED = 4 * HEAD
EPS = 1e-05
ROPE_BASE = 100000.0
NEG = -1e30
PREFIX_MAX = 1024
SCALE = 1.0 / math.sqrt(HEAD)
MESH = pl.DeviceIdType.MESH
ANY = pl.BlockSpec(memory_space=pl.ANY)
VMEM = pl.BlockSpec(memory_space=pltpu.VMEM)
SMEM = pl.BlockSpec(memory_space=pltpu.SMEM)
MIB = 1 << 20

ARRAYS = ((24, 2048), (24, 2048), (24, 1536), (24, 768), (24, 128), (64, 768))
GATE, UP, QKV, OUT, GAIN, DOWN = range(6)
QKV_PIECES = (
    (QKV, 0, 512, "y", 1, -1),
    (QKV, 512, 256, "y", -1, -1),
    (QKV, 768, 512, "z", 1, -1),
    (QKV, 1280, 256, "z", -1, -1),
    (GAIN, 0, 128, "y", 1, -1),
)
GATHER_PIECES = QKV_PIECES + (
    (OUT, 0, 384, "y", -1, 1),
    (OUT, 384, 384, "z", -1, 1),
    (GATE, 0, 512, "y", 1, -1),
    (GATE, 512, 1536, "y", -1, None),
    (UP, 0, 512, "z", 1, -1),
    (UP, 512, 1536, "z", -1, None),
    (DOWN, 0, 384, "y", 1, 1),
    (DOWN, 384, 384, "z", 1, 1),
)
ATTN_PIECES = (
    (QKV, 0, 512, "y", 1, 1),
    (QKV, 512, 256, "y", -1, -1),
    (QKV, 768, 512, "z", 1, 1),
    (QKV, 1280, 256, "z", -1, -1),
    (GAIN, 0, 128, "y", -1, -1),
    (OUT, 0, 384, "y", -1, None),
    (OUT, 384, 384, "z", -1, None),
)
MLP_PIECES = (
    (GATE, 0, 1024, "y", 1, 1),
    (UP, 0, 1024, "z", 1, 1),
    (DOWN, 0, 384, "y", -1, -1),
    (DOWN, 384, 384, "z", -1, -1),
    (GATE, 1024, 512, "y", 1, None),
    (GATE, 1536, 512, "y", -1, None),
    (UP, 1024, 512, "z", 1, None),
    (UP, 1536, 512, "z", -1, None),
)
OTHER = {"y": "z", "z": "y"}


def f32dot(a, b, dims):
    return lax.dot_general(a, b, (dims, ((), ())), preferred_element_type=jnp.float32)


class Place:
    def __init__(self):
        self.s = lax.axis_index("section")
        self.d = lax.axis_index("dp")
        self.q = lax.axis_index("seq")
        self.y = lax.div(self.q, 8)
        self.z = lax.rem(lax.div(self.q, 2), 4)
        self.c = lax.rem(self.q, 2)

    def coord(self, axis):
        return self.y if axis == "y" else self.z

    def step(self, axis, by):
        y, z = self.y, self.z
        if axis == "y":
            y = lax.rem(y + by + 4, 4)
        else:
            z = lax.rem(z + by + 4, 4)
        return (self.s, self.d, y * 8 + z * 2 + self.c)

    def sibling(self):
        return (self.s, self.d, self.q + 1 - 2 * self.c)

    def dp_peer(self):
        return (self.s, 1 - self.d, self.q)


def meet(devices):
    barrier = pltpu.get_barrier_semaphore()
    for device in devices:
        pl.semaphore_signal(barrier, inc=1, device_id=device, device_id_type=MESH)
    pl.semaphore_wait(barrier, len(devices))


def remote(src, dst, send, recv, device):
    return pltpu.make_async_remote_copy(
        src_ref=src, dst_ref=dst, send_sem=send, recv_sem=recv, device_id=device, device_id_type=MESH
    )


EARLY = len(QKV_PIECES)


class Gather:
    def __init__(self, me, ins, outs, scratch):
        n = len(ARRAYS)
        self.me, self.ins, self.outs = me, ins, outs
        self.give, self.got, self.chip = scratch[:n], scratch[n : 2 * n], scratch[2 * n : 3 * n]
        self.first, self.local, self.over, self.ring_s, self.ring_r, self.sib_s, self.sib_r = scratch[3 * n :]
        self.dps = (me.d, 1 - me.d)
        self.one, self.two, self.held, self.overs, self.swaps = {}, {}, {}, {}, {}
        self.shares, self.pending = {}, []

    def neighbours(self):
        me = self.me
        near = [me.step(axis, by) for axis in "yz" for by in (1, -1)]
        return near + [me.dp_peer(), me.sibling()]

    def lanes(self, i):
        array, start, width = GATHER_PIECES[i][:3]
        return pl.ds(pl.multiple_of(self.me.c * ARRAYS[array][1] + start, LANES), width)

    def along(self, i, dp, by):
        array, _, _, a1 = GATHER_PIECES[i][:4]
        pos = lax.rem(self.me.coord(a1) + by + 4, 4)
        y, z = (pos, self.me.z) if a1 == "y" else (self.me.y, pos)
        return self.outs[array].at[dp, y, z, :, self.lanes(i)]

    def across(self, i, dp, by):
        array, _, _, a1 = GATHER_PIECES[i][:4]
        pos = lax.rem(self.me.coord(OTHER[a1]) + by + 4, 4)
        if a1 == "y":
            return self.outs[array].at[dp, pl.ds(0, 4), pos, :, self.lanes(i)]
        return self.outs[array].at[dp, pos, pl.ds(0, 4), :, self.lanes(i)]

    def send(self, i, block, k, src, dst, device):
        cp = remote(src, dst, self.ring_s.at[i, block, k], self.ring_r.at[i, block, k], device)
        cp.start()
        self.pending.append(cp)
        return cp

    def share(self, i, block, k, ref, src=None):
        src = ref if src is None else src
        cp = remote(src, ref, self.sib_s.at[i, block, k], self.sib_r.at[i, block, k], self.me.sibling())
        cp.start()
        self.pending.append(cp)
        self.shares.setdefault(i, []).append(cp)
        if block == 0 and (k == 0 or self.crosses(i)):
            cp = remote(src, ref, self.over.at[0, i, k], self.over.at[1, i, k], self.me.dp_peer())
            cp.start()
            self.pending.append(cp)
            self.overs[i, k] = cp

    def crosses(self, i):
        return GATHER_PIECES[i][5] is None

    def way(self, i, block):
        return GATHER_PIECES[i][4 + block]

    def both(self, pieces):
        return [i for i in pieces if not self.crosses(i)]

    def cross(self, pieces, spots):
        for k in spots:
            for i in pieces:
                if self.crosses(i):
                    way = self.way(i, 0)
                    by = (0, -way, way, 2, -way, way, 2)[k]
                    place = self.along if k < 4 else self.across
                    self.overs[i, k].wait_recv()
                    self.share(i, 1, k, place(i, self.dps[1], by))

    def swap(self):
        me = self.me
        for a, (_, width) in enumerate(ARRAYS):
            start = pl.multiple_of((1 - me.c) * width, LANES)
            self.give[a][...] = self.ins[a][:, pl.ds(start, width)].astype(jnp.float32)
            cp = remote(self.give[a], self.got[a], self.first.at[0, a], self.first.at[1, a], me.sibling())
            cp.start()
            self.swaps[a] = cp

    def join(self, a):
        me, width = self.me, ARRAYS[a][1]
        self.swaps[a].wait()
        start = pl.multiple_of(me.c * width, LANES)
        mine = self.ins[a][:, pl.ds(start, width)].astype(jnp.float32)
        theirs = self.got[a][...]
        low = jnp.where(me.c == 0, mine, theirs)
        high = jnp.where(me.c == 0, theirs, mine)
        self.chip[a][...] = jnp.concatenate([low, high], axis=0).astype(jnp.bfloat16)

    def start(self, pieces):
        me = self.me
        for i in pieces:
            array, start, width, a1 = GATHER_PIECES[i][:4]
            src = self.chip[array].at[:, pl.ds(start, width)]
            here = self.along(i, me.d, 0)
            self.one[i, 0, 1] = self.send(i, 0, 0, src, here, me.step(a1, 1))
            self.one[i, 0, -1] = self.send(i, 0, 1, src, here, me.step(a1, -1))
            cp = pltpu.make_async_copy(src, here, self.local.at[i])
            cp.start()
            self.held[i] = cp
            self.share(i, 0, 0, here, src)

    def start_other(self, pieces):
        me = self.me
        for i in self.both(pieces):
            a1 = GATHER_PIECES[i][3]
            self.overs[i, 0].wait_recv()
            here = self.along(i, self.dps[1], 0)
            self.one[i, 1, 1] = self.send(i, 1, 0, here, here, me.step(a1, 1))
            self.one[i, 1, -1] = self.send(i, 1, 1, here, here, me.step(a1, -1))
            self.share(i, 1, 0, here)

    def hop(self, pieces, block, second):
        kept, place, base = (self.two, self.across, 3) if second else (self.one, self.along, 0)
        dp = self.dps[block]
        pieces = self.both(pieces) if block else pieces
        for i in pieces:
            axis, way = GATHER_PIECES[i][3], self.way(i, block)
            axis = OTHER[axis] if second else axis
            kept[i, block, way].wait_recv()
            came = place(i, dp, -way)
            kept[i, block, 0] = self.send(i, block, base + 2, came, came, self.me.step(axis, way))
            self.share(i, block, base + 1, came)
        for i in pieces:
            way = self.way(i, block)
            kept[i, block, -way].wait_recv()
            self.share(i, block, base + 2, place(i, dp, way))

    def turn(self, pieces, block):
        dp = self.dps[block]
        for i in self.both(pieces) if block else pieces:
            a2 = OTHER[GATHER_PIECES[i][3]]
            self.one[i, block, 0].wait_recv()
            self.share(i, block, 3, self.along(i, dp, 2))
            if block == 0:
                self.held[i].wait()
            here = self.across(i, dp, 0)
            self.two[i, block, 1] = self.send(i, block, 3, here, here, self.me.step(a2, 1))
            self.two[i, block, -1] = self.send(i, block, 4, here, here, self.me.step(a2, -1))

    def finish(self, pieces, block):
        for i in self.both(pieces) if block else pieces:
            self.two[i, block, 0].wait_recv()
            self.share(i, block, 6, self.across(i, self.dps[block], 2))

    def shown(self, pieces):
        for i in pieces:
            for cp in self.shares[i]:
                cp.wait_recv()

    def drain(self):
        for cp in self.pending:
            cp.wait_send()


GATHER_SCRATCH = (
    [pltpu.VMEM(shape, jnp.float32) for shape in ARRAYS]
    + [pltpu.VMEM(shape, jnp.float32) for shape in ARRAYS]
    + [pltpu.VMEM((2 * rows, width), jnp.bfloat16) for rows, width in ARRAYS]
    + [
        pltpu.SemaphoreType.DMA((2, len(ARRAYS))),
        pltpu.SemaphoreType.DMA((len(GATHER_PIECES),)),
        pltpu.SemaphoreType.DMA((2, len(GATHER_PIECES), 7)),
        pltpu.SemaphoreType.DMA((len(GATHER_PIECES), 2, 6)),
        pltpu.SemaphoreType.DMA((len(GATHER_PIECES), 2, 6)),
        pltpu.SemaphoreType.DMA((len(GATHER_PIECES), 2, 7)),
        pltpu.SemaphoreType.DMA((len(GATHER_PIECES), 2, 7)),
    ]
)


def gather_steps(gather):
    early = range(EARLY)
    late = range(EARLY, len(GATHER_PIECES))
    gather.swap()
    for a in (QKV, GAIN):
        gather.join(a)
    gather.start(early)
    for a in (OUT, GATE, UP, DOWN):
        gather.join(a)
    gather.start(late)
    gather.hop(early, 0, False)
    gather.turn(early, 0)
    gather.start_other(early)
    gather.hop(late, 0, False)
    gather.hop(early, 1, False)
    gather.turn(early, 1)
    gather.turn(late, 0)
    gather.start_other(late)
    gather.hop(early, 0, True)
    gather.hop(late, 1, False)
    gather.hop(early, 1, True)
    gather.finish(early, 0)
    gather.hop(late, 0, True)
    gather.turn(late, 1)
    gather.finish(early, 1)
    gather.shown(early)
    yield
    gather.finish(late, 0)
    gather.cross(late, range(4))
    gather.hop(late, 1, True)
    yield
    gather.finish(late, 1)
    gather.cross(late, range(4, 7))
    gather.shown(late)
    gather.drain()


def add_into(total, term):
    chunks = total.shape[1] // 16

    def step(k, carry):
        j = lax.div(k, chunks)
        rows = pl.ds(pl.multiple_of(lax.rem(k, chunks) * 16, 16), 16)
        both = total[j, rows, :].astype(jnp.float32) + term[j, rows, :].astype(jnp.float32)
        total[j, rows, :] = both.astype(jnp.bfloat16)
        return carry

    lax.fori_loop(0, total.shape[0] * chunks, step, 0)


def add_two(total, left, right):
    chunks = total.shape[1] // 16

    def step(k, carry):
        j = lax.div(k, chunks)
        rows = pl.ds(pl.multiple_of(lax.rem(k, chunks) * 16, 16), 16)
        parts = [ref[j, rows, :].astype(jnp.float32) for ref in (total, left, right)]
        total[j, rows, :] = (parts[0] + (parts[1] + parts[2])).astype(jnp.bfloat16)
        return carry

    lax.fori_loop(0, total.shape[0] * chunks, step, 0)


class Scatter:
    def __init__(self, me, pieces, arrays, ins, outs, scratch):
        n, m = len(pieces), len(arrays)
        self.me, self.pieces, self.ins, self.outs = me, pieces, ins, outs
        self.at = {a: k for k, a in enumerate(arrays)}
        names = ("near", "far", "last", "mid", "own", "near1", "far1", "last1", "sent", "came")
        for k, name in enumerate(names):
            setattr(self, name, scratch[k * n : (k + 1) * n])
        rest = scratch[len(names) * n :]
        whole = [i for i in range(n) if self.crosses(i)]
        self.ours, rest = dict(zip(whole, rest)), rest[len(whole) :]
        self.theirs, rest = dict(zip(whole, rest)), rest[len(whole) :]
        self.total, rest = rest[:m], rest[m:]
        self.load, self.ring_s, self.ring_r, self.over, self.fin, self.keep = rest
        self.dps = (1 - me.d, me.d)
        self.loads, self.one, self.two, self.overs, self.pending = {}, {}, {}, {}, []

    def neighbours(self):
        me = self.me
        near = [me.step(axis, by) for axis in "yz" for by in (1, -1)]
        return near + [me.dp_peer(), me.sibling()]

    def crosses(self, i):
        return self.pieces[i][5] is None

    def way(self, i, block):
        return self.pieces[i][5 - block]

    def of(self, block, crossing=None):
        picked = [i for i in range(len(self.pieces)) if block or not self.crosses(i)]
        return [i for i in picked if crossing is None or self.crosses(i) == crossing]

    def slot(self, i, block):
        return 0 if self.crosses(i) else block

    def column(self, i, block, by):
        array, start, width, a1 = self.pieces[i][:4]
        pos = lax.rem(self.me.coord(OTHER[a1]) + by + 4, 4)
        ref, dp, lanes = self.ins[self.at[array]], self.dps[block], pl.ds(start, width)
        if a1 == "z":
            return ref.at[dp, pos, pl.ds(0, 4), :, lanes]
        return ref.at[dp, pl.ds(0, 4), pos, :, lanes]

    def send(self, i, block, k, src, dst, device):
        cp = remote(src, dst, self.ring_s.at[i, block, k], self.ring_r.at[i, block, k], device)
        cp.start()
        self.pending.append(cp)
        return cp

    def start_crossing(self):
        for k in range(4):
            for i in self.of(1, True):
                way = self.way(i, 1)
                by = (2 * way, -way, way, 0)[k]
                there = self.theirs[i].at[k]
                cp = remote(
                    self.column(i, 0, by), there, self.over.at[0, i, k], self.over.at[1, i, k], self.me.dp_peer()
                )
                cp.start()
                self.pending.append(cp)
                self.overs[i, k] = cp
                cp = pltpu.make_async_copy(self.column(i, 1, by), self.ours[i].at[k], self.load.at[k, i, 0])
                cp.start()
                self.loads[i, k] = cp

    def add_crossed(self, i, k):
        self.overs[i, k].wait_recv()
        self.loads[i, k].wait()
        add_into(self.ours[i].at[k], self.theirs[i].at[k])

    def start(self, block):
        for i in self.of(block, False):
            way = self.way(i, block)
            there = self.me.step(OTHER[self.pieces[i][3]], way)
            self.one[i, block, 0] = self.send(
                i, block, 0, self.column(i, block, 2 * way), self.near[i].at[block], there
            )
        for i in self.of(block, False):
            way = self.way(i, block)
            there = self.me.step(OTHER[self.pieces[i][3]], -way)
            self.one[i, block, 1] = self.send(
                i, block, 1, self.column(i, block, -way), self.far[i].at[block], there
            )
        for i in self.of(block, False):
            way = self.way(i, block)
            for k, (by, ref) in enumerate(((way, self.mid[i]), (0, self.own[i]))):
                cp = pltpu.make_async_copy(self.column(i, block, by), ref.at[block], self.load.at[k, i, block])
                cp.start()
                self.loads[i, block, k] = cp

    def start_crossed(self):
        for k in range(2):
            for i in self.of(1, True):
                way = self.way(i, 1)
                self.add_crossed(i, k)
                there = self.me.step(OTHER[self.pieces[i][3]], -way if k else way)
                dst = (self.far if k else self.near)[i].at[0]
                self.one[i, 1, k] = self.send(i, 1, k, self.ours[i].at[k], dst, there)

    def hop(self, block, crossing):
        for i in self.of(block, crossing):
            slot = self.slot(i, block)
            self.one[i, block, 0].wait_recv()
            if crossing:
                self.add_crossed(i, 2)
                mid = self.ours[i].at[2]
            else:
                self.loads[i, block, 0].wait()
                mid = self.mid[i].at[block]
            near = self.near[i].at[slot]
            add_into(near, mid)
            there = self.me.step(OTHER[self.pieces[i][3]], self.way(i, block))
            self.one[i, block, 2] = self.send(i, block, 2, near, self.last[i].at[slot], there)

    def own_of(self, i, block):
        return self.ours[i].at[3] if self.crosses(i) else self.own[i].at[block]

    def turn(self, block, crossing):
        me = self.me
        for i in self.of(block, crossing):
            slot, a1, way = self.slot(i, block), self.pieces[i][3], self.way(i, block)
            if crossing:
                self.add_crossed(i, 3)
            else:
                self.loads[i, block, 1].wait()
            self.one[i, block, 1].wait_recv()
            self.one[i, block, 2].wait_recv()
            own = self.own_of(i, block)
            add_two(own, self.far[i].at[slot], self.last[i].at[slot])
            pos = me.coord(a1)
            self.two[i, block, 0] = self.send(
                i, block, 3, own.at[lax.rem(pos + 2, 4)], self.near1[i].at[slot], me.step(a1, way)
            )
            self.two[i, block, 1] = self.send(
                i, block, 4, own.at[lax.rem(pos - way + 4, 4)], self.far1[i].at[slot], me.step(a1, -way)
            )

    def hop_two(self, block, crossing):
        me = self.me
        for i in self.of(block, crossing):
            slot, a1, way = self.slot(i, block), self.pieces[i][3], self.way(i, block)
            self.two[i, block, 0].wait_recv()
            place = lax.rem(me.coord(a1) + way + 4, 4)
            add_into(self.near1[i].at[pl.ds(slot, 1)], self.own_of(i, block).at[pl.ds(place, 1)])
            self.two[i, block, 2] = self.send(
                i, block, 5, self.near1[i].at[slot], self.last1[i].at[slot], me.step(a1, way)
            )

    def finish(self, block, crossing):
        me = self.me
        for i in self.of(block, crossing):
            array, start, width, a1 = self.pieces[i][:4]
            slot, pos = self.slot(i, block), me.coord(a1)
            self.two[i, block, 1].wait_recv()
            self.two[i, block, 2].wait_recv()
            if block == 1 and not crossing:
                self.overs[i, 0].wait_recv()
            far1, last1, sent, came = (ref[i] for ref in (self.far1, self.last1, self.sent, self.came))
            own = self.own_of(i, block)
            total = self.total[self.at[array]]

            def step(k, carry):
                part = pl.ds(pl.multiple_of(k * 16, 16), 16)
                both = far1[slot, part, :].astype(jnp.float32) + last1[slot, part, :].astype(jnp.float32)
                both = both + own[pos, part, :].astype(jnp.float32)
                if block == 0:
                    sent[part, :] = both.astype(jnp.bfloat16)
                elif crossing:
                    total[part, start : start + width] = both
                else:
                    total[part, start : start + width] = both + came[part, :].astype(jnp.float32)
                return carry

            lax.fori_loop(0, 2 * ARRAYS[array][0] // 16, step, 0)
            if block == 0:
                cp = remote(sent, came, self.over.at[0, i, 0], self.over.at[1, i, 0], me.dp_peer())
                cp.start()
                self.pending.append(cp)
                self.overs[i, 0] = cp

    def hand_out(self):
        me = self.me
        copies = []
        for array, k in self.at.items():
            rows, width = ARRAYS[array]
            mine = self.total[k].at[pl.ds(pl.multiple_of(me.c * rows, 8), rows)]
            theirs = self.total[k].at[pl.ds(pl.multiple_of((1 - me.c) * rows, 8), rows)]
            place = self.outs[k].at[:, pl.ds(pl.multiple_of(me.c * width, LANES), width)]
            copies.append(pltpu.make_async_copy(mine, place, self.keep.at[k]))
            copies.append(remote(theirs, place, self.fin.at[0, k], self.fin.at[1, k], me.sibling()))
        for cp in copies:
            cp.start()
        for cp in copies:
            cp.wait()
        for cp in self.pending:
            cp.wait_send()


def scatter_steps(scatter):
    scatter.start_crossing()
    scatter.start(0)
    scatter.start(1)
    yield
    scatter.hop(0, False)
    scatter.start_crossed()
    scatter.hop(1, False)
    scatter.turn(0, False)
    scatter.hop_two(0, False)
    scatter.hop(1, True)
    scatter.finish(0, False)
    scatter.turn(1, False)
    scatter.hop_two(1, False)
    scatter.turn(1, True)
    scatter.finish(1, False)
    scatter.hop_two(1, True)
    scatter.finish(1, True)
    scatter.hand_out()


def scatter_scratch(pieces, arrays):
    n, m = len(pieces), len(arrays)
    bf16 = jnp.bfloat16
    shapes = [(2 * ARRAYS[piece[0]][0], piece[2]) for piece in pieces]
    crossing = [piece[5] is None for piece in pieces]

    def buffers(count, *lead):
        return [pltpu.VMEM((1 if one else 2, *lead, *shape), bf16) for _ in range(count) for shape, one in zip(shapes, crossing)]

    held = [
        pltpu.VMEM((1, 16, LANES) if one else (2, 4, *shape), bf16)
        for _ in range(2)
        for shape, one in zip(shapes, crossing)
    ]
    whole = [pltpu.VMEM((4, 4, *shape), bf16) for _ in range(2) for shape, one in zip(shapes, crossing) if one]
    return (
        buffers(3, 4)
        + held
        + buffers(3)
        + [pltpu.VMEM((16, LANES) if one else shape, bf16) for _ in range(2) for shape, one in zip(shapes, crossing)]
        + whole
        + [pltpu.VMEM((2 * ARRAYS[a][0], ARRAYS[a][1]), jnp.float32) for a in arrays]
        + [
            pltpu.SemaphoreType.DMA((4, n, 2)),
            pltpu.SemaphoreType.DMA((n, 2, 6)),
            pltpu.SemaphoreType.DMA((n, 2, 6)),
            pltpu.SemaphoreType.DMA((2, n, 4)),
            pltpu.SemaphoreType.DMA((2, m)),
            pltpu.SemaphoreType.DMA((m,)),
        ]
    )


def scatter_shapes(arrays):
    return [jax.ShapeDtypeStruct((ARRAYS[a][0], 2 * ARRAYS[a][1]), jnp.float32) for a in arrays]


def in_shards(parts, arrays):
    return [part.reshape(2, 4, 4, 2 * ARRAYS[a][0], ARRAYS[a][1]) for part, a in zip(parts, arrays, strict=True)]


ATTN_ARRAYS = (QKV, OUT, GAIN)
MLP_ARRAYS = (GATE, UP, DOWN)


def scatter_kernel(pieces, arrays, *refs):
    m = len(arrays)
    me = Place()
    scatter = Scatter(me, pieces, arrays, refs[:m], refs[m : 2 * m], refs[2 * m :])
    meet(scatter.neighbours())
    for _ in scatter_steps(scatter):
        pass


def scatter_attn(parts):
    pieces, arrays = ATTN_PIECES, ATTN_ARRAYS
    return pl.pallas_call(
        functools.partial(scatter_kernel, pieces, arrays),
        out_shape=scatter_shapes(arrays),
        in_specs=[ANY] * len(arrays),
        out_specs=[ANY] * len(arrays),
        scratch_shapes=scatter_scratch(pieces, arrays),
        compiler_params=pltpu.CompilerParams(
            collective_id=2, has_side_effects=True, vmem_limit_bytes=56 * MIB
        ),
        name="scatter_attn",
    )(*in_shards(parts, arrays))


ORIGINS = 32
BLOCK = 8
BLOCKS = ORIGINS // BLOCK


def meet_plane(me, others=()):
    barrier = pltpu.get_barrier_semaphore()
    for device in others:
        pl.semaphore_signal(barrier, inc=1, device_id=device, device_id_type=MESH)

    def greet(k, carry):
        to = lax.rem(me.q + k, ORIGINS)
        pl.semaphore_signal(barrier, inc=1, device_id=(me.s, me.d, to), device_id_type=MESH)
        return carry

    lax.fori_loop(1, ORIGINS, greet, 0)
    pl.semaphore_wait(barrier, ORIGINS - 1 + len(others))


class Exchange:
    def __init__(self, me, src, dst_of, sems):
        self.me, self.src, self.dst_of, self.sems = me, src, dst_of, sems

    def copy(self, origin, to):
        me, (send, recv, _) = self.me, self.sems
        peer = to + origin - me.q
        return remote(
            self.src.at[to], self.dst_of(origin, to), send.at[to], recv.at[origin], (me.s, me.d, peer)
        )

    def own(self):
        q = self.me.q
        return pltpu.make_async_copy(self.src.at[q], self.dst_of(q, q), self.sems[2].at[0])

    def start_all(self):
        self.own().start()

        def step(k, carry):
            by = (k + 1) // 2
            by = jnp.where(lax.rem(k, 2) == 1, by, ORIGINS - by)
            self.copy(self.me.q, lax.rem(self.me.q + by, ORIGINS)).start()
            return carry

        lax.fori_loop(1, ORIGINS, step, 0)

    def start_one(self, to):
        @pl.when(to == self.me.q)
        def _():
            self.own().start()

        @pl.when(to != self.me.q)
        def _():
            self.copy(self.me.q, to).start()

    def start(self, block):
        def step(k, carry):
            self.start_one(block * BLOCK + lax.rem(self.me.q + k, BLOCK))
            return carry

        lax.fori_loop(0, BLOCK, step, 0)

    def arrived(self, first, count):
        def step(k, carry):
            origin = first + k

            @pl.when(origin == self.me.q)
            def _():
                self.own().wait()

            @pl.when(origin != self.me.q)
            def _():
                self.copy(origin, self.me.q).wait_recv()

            return carry

        lax.fori_loop(0, count, step, 0)

    def sent(self):
        def step(k, carry):
            self.copy(self.me.q, lax.rem(self.me.q + k, ORIGINS)).wait_send()
            return carry

        lax.fori_loop(1, ORIGINS, step, 0)


EXCHANGE_SEMS = [
    pltpu.SemaphoreType.DMA((ORIGINS,)),
    pltpu.SemaphoreType.DMA((ORIGINS,)),
    pltpu.SemaphoreType.DMA((1,)),
]


def block_mask(block, keys, core, prefix_len):
    rows = BLOCK * 32
    row = lax.broadcasted_iota(jnp.int32, (rows, keys), 0)
    key = lax.broadcasted_iota(jnp.int32, (rows, keys), 1)
    pos = block * BLOCK * 64 + 64 * (row // 32) + 32 * core + row % 32
    return (key <= pos) | (key < prefix_len)


def keys_of(block):
    return max((block + 1) * BLOCK * 64, PREFIX_MAX)


def group(block):
    return pl.ds(block * BLOCK, BLOCK)


def split_four(y):
    inside = lax.broadcasted_iota(jnp.int32, (y.shape[0], LANES), 1) < HEAD
    heads = [y[:, :LANES]] + [pltpu.roll(y, PACKED - HEAD * h, axis=1)[:, :LANES] for h in (1, 2, 3)]
    return [jnp.where(inside, z, 0.0) for z in heads]


def pack_four(heads):
    zero = jnp.zeros((heads[0].shape[0], 2 * LANES), jnp.float32)
    wide = [jnp.concatenate([z, zero], axis=1) for z in heads]
    total = wide[0]
    for h in (1, 2, 3):
        total = total + pltpu.roll(wide[h], HEAD * h, axis=1)
    return total


def turn_heads(z, cos, ahead, back):
    return z * cos + pltpu.roll(z, PACKED - HALF, axis=1) * ahead + pltpu.roll(z, HALF, axis=1) * back


def project_and_send(x, gain, w, tables, normed, bundle, held, held_sem, coming):
    cos, ahead, back = tables
    tokens = x.shape[0]

    def fetch(g, slot):
        lanes = pl.ds(pl.multiple_of(g * PACKED, LANES), PACKED)
        return pltpu.make_async_copy(w.at[:, :, :, :, lanes], held.at[slot], held_sem.at[slot])

    begin = lax.rem(coming.me.q // 2, KV_HEADS)
    fetch(begin, 0).start()
    hidden = x[...].astype(jnp.float32)
    r1 = lax.rsqrt(jnp.mean(hidden * hidden, axis=-1, keepdims=True) + EPS)
    normed[...] = (hidden * r1 * gain).astype(jnp.bfloat16)

    def step(k, carry):
        slot = lax.rem(k, 2)
        g = lax.rem(begin + k, KV_HEADS)
        fetch(g, slot).wait()

        @pl.when(k + 1 < KV_HEADS)
        def _():
            fetch(lax.rem(g + 1, KV_HEADS), 1 - slot).start()

        y = f32dot(normed[...], held[slot].reshape(x.shape[1], PACKED), ((1,), (0,)))
        z = turn_heads(y, cos[...], ahead[...], back[...]).astype(jnp.bfloat16)
        for part in range(4):
            to = (part // 2) * 16 + g * 2 + part % 2
            bundle[to] = z[part * 32 : (part + 1) * 32]
            coming.start_one(to)
        return carry

    lax.fori_loop(0, KV_HEADS, step, 0)


PROJECT_SCRATCH = [
    pltpu.VMEM((ORIGINS, 32, PACKED), jnp.bfloat16),
    pltpu.VMEM((2, 2, 4, 4, 48, PACKED), jnp.bfloat16),
    pltpu.SemaphoreType.DMA((2,)),
]


class Attend:
    def __init__(self, me, prefix, bundle, dst, keys, values, queries, scratch):
        self.me, self.prefix, self.keys, self.values, self.queries = me, prefix, keys, values, queries
        self.whole, self.out = scratch[:2]
        self.sib = scratch[8]
        self.coming = Exchange(
            me, bundle, lambda origin, to: self.whole.at[origin, lax.rem(to, 2)], scratch[2:5]
        )
        self.going = Exchange(me, self.out, lambda origin, to: dst.at[origin], scratch[5:8])
        self.shares = []

    def receive(self):
        for block in range(BLOCKS):
            self.coming.arrived(block * BLOCK, BLOCK)
            mine = self.whole.at[group(block), self.me.c, :, pl.ds(0, 2 * LANES)]
            cp = remote(mine, mine, self.sib.at[0, block], self.sib.at[1, block], self.me.sibling())
            cp.start()
            self.shares.append(cp)
            y = self.whole[group(block), self.me.c].reshape(BLOCK * 32, PACKED).astype(jnp.float32)
            heads = split_four(y)
            for h in range(2):
                self.queries[h, pl.ds(block * BLOCK * 32, BLOCK * 32), :] = heads[2 + h].astype(jnp.bfloat16)

    def unpack(self, block):
        self.shares[block].wait_recv()
        rows = BLOCK * 64
        both = self.whole[group(block), :, :, 0 : 2 * LANES].reshape(rows, 2 * LANES)
        at = pl.ds(block * rows, rows)
        self.keys[at, :] = both[:, :LANES]
        turned = pltpu.roll(both.astype(jnp.float32), 2 * LANES - HEAD, axis=1)
        self.values[at, :] = turned[:, :LANES].astype(jnp.bfloat16)

    def compute(self):
        ready = 0
        for block in range(BLOCKS):
            count = keys_of(block)
            while ready * BLOCK * 64 < count:
                self.unpack(ready)
                ready += 1
            k = self.keys[pl.ds(0, count), :]
            v = self.values[pl.ds(0, count), :]
            allowed = block_mask(block, count, self.me.c, self.prefix[0])
            quarters = []
            for h in range(2):
                q = self.queries[h, pl.ds(block * BLOCK * 32, BLOCK * 32), :]
                s = jnp.where(allowed, f32dot(q, k, ((1,), (1,))) * SCALE, NEG)
                top = jnp.max(s, axis=-1, keepdims=True)
                e = jnp.exp(s - top)
                p = (e * (1.0 / jnp.sum(e, axis=-1, keepdims=True))).astype(jnp.bfloat16)
                quarters.append(f32dot(p, v, ((1,), (0,))).reshape(BLOCK, 32, LANES))
            inside = lax.broadcasted_iota(jnp.int32, (BLOCK * 16, LANES), 1) < HEAD
            heads = [
                jnp.where(inside, o[:, r * 16 : r * 16 + 16].reshape(BLOCK * 16, LANES), 0.0)
                for r in range(2)
                for o in quarters
            ]
            packed = pack_four(heads).astype(jnp.bfloat16)
            self.out[group(block)] = packed.reshape(BLOCK, 16, PACKED)
        self.going.start_all()

    def drain(self):
        self.going.arrived(0, ORIGINS)
        self.coming.sent()
        self.going.sent()
        for cp in self.shares:
            cp.wait_send()


ATTEND_SCRATCH = [
    pltpu.VMEM((ORIGINS, 2, 32, PACKED), jnp.bfloat16),
    pltpu.VMEM((ORIGINS, 16, PACKED), jnp.bfloat16),
    *EXCHANGE_SEMS,
    *EXCHANGE_SEMS,
    pltpu.SemaphoreType.DMA((2, BLOCKS)),
]
KEPT = [
    ((ORIGINS * 64, LANES), jnp.bfloat16),
    ((ORIGINS * 64, LANES), jnp.bfloat16),
    ((2, ORIGINS * 32, LANES), jnp.bfloat16),
]
ATTENDED = ((ORIGINS, 16, PACKED), jnp.bfloat16)


def attend_kernel(prefix, x, gain, cos, ahead, back, w, normed, keys, values, queries, dst, *scratch):
    me = Place()
    meet_plane(me)
    bundle, held, held_sem = scratch[:3]
    attention = Attend(me, prefix, bundle, dst, keys, values, queries, scratch[3:])
    project_and_send(
        x, gain[0:1, :], w, (cos, ahead, back), normed, bundle, held, held_sem, attention.coming
    )
    attention.receive()
    attention.compute()
    attention.drain()


def attend(prefix, x, gain, tables, w):
    return pl.pallas_call(
        attend_kernel,
        out_shape=[jax.ShapeDtypeStruct(x.shape, jnp.bfloat16)]
        + [jax.ShapeDtypeStruct(*kept) for kept in KEPT]
        + [jax.ShapeDtypeStruct(*ATTENDED)],
        in_specs=[SMEM] + [VMEM] * 5 + [ANY],
        out_specs=[VMEM] * 5,
        scratch_shapes=PROJECT_SCRATCH + ATTEND_SCRATCH,
        compiler_params=pltpu.CompilerParams(
            collective_id=3, has_side_effects=True, vmem_limit_bytes=60 * MIB
        ),
        name="attend",
    )(prefix, x, gain, *tables, w)


def enter_kernel(prefix, x, cos, ahead, back, *refs):
    n = len(ARRAYS)
    ins, outs = refs[:n], refs[n : 2 * n]
    gains, dst = refs[2 * n : 2 * n + 2]
    normed, keys, values, queries, column, column_sem = refs[2 * n + 2 : 2 * n + 8]
    rest = refs[2 * n + 8 :]
    bundle, held, held_sem = rest[:3]
    k = 3 + len(ATTEND_SCRATCH)
    me = Place()
    attention = Attend(me, prefix, bundle, dst, keys, values, queries, rest[3:k])
    gather = Gather(me, ins, outs, rest[k:])
    meet_plane(me, [me.dp_peer()])
    steps = gather_steps(gather)
    next(steps)
    cp = pltpu.make_async_copy(outs[GAIN], column, column_sem.at[0])
    cp.start()
    cp.wait()
    first = (lax.broadcasted_iota(jnp.int32, (8, LANES), 1) == 0).astype(jnp.bfloat16)
    for half in range(2):
        one = column[:, :, :, :, half * LANES : (half + 1) * LANES].reshape(x.shape[1], LANES)
        gains[half] = f32dot(first, one, ((1,), (1,)))
    project_and_send(
        x, gains[0, 0:1, :], outs[QKV], (cos, ahead, back), normed, bundle, held, held_sem, attention.coming
    )
    attention.receive()
    next(steps)
    attention.compute()
    for _ in steps:
        pass
    attention.drain()


def enter(prefix, x, tables, shards):
    n = len(ARRAYS)
    width = x.shape[1]
    return pl.pallas_call(
        enter_kernel,
        out_shape=[jax.ShapeDtypeStruct((2, 4, 4, 2 * r, 2 * w), jnp.bfloat16) for r, w in ARRAYS]
        + [jax.ShapeDtypeStruct((2, 8, width), jnp.float32), jax.ShapeDtypeStruct(*ATTENDED)],
        in_specs=[SMEM] + [VMEM] * (4 + n),
        out_specs=[ANY] * n + [VMEM] * 2,
        scratch_shapes=[pltpu.VMEM(x.shape, jnp.bfloat16)]
        + [pltpu.VMEM(*kept) for kept in KEPT]
        + [pltpu.VMEM((2, 4, 4, 48, 2 * LANES), jnp.bfloat16), pltpu.SemaphoreType.DMA((1,))]
        + PROJECT_SCRATCH
        + ATTEND_SCRATCH
        + GATHER_SCRATCH,
        compiler_params=pltpu.CompilerParams(
            collective_id=1, has_side_effects=True, vmem_limit_bytes=60 * MIB
        ),
        name="enter",
    )(prefix, x, *tables, *shards)


class AttendBack:
    def __init__(self, me, prefix, keys, values, queries, src, dst, scratch):
        self.me, self.prefix, self.keys, self.values, self.queries = me, prefix, keys, values, queries
        self.datt, self.acc, self.theirs, self.dq, self.bundle = scratch[:5]
        self.sib = scratch[11]
        self.coming = Exchange(me, src, lambda origin, to: self.datt.at[origin], scratch[5:8])
        self.going = Exchange(me, self.bundle, lambda origin, to: dst.at[origin], scratch[8:11])
        self.shares = {}

    def share(self, block):
        cp = remote(
            self.acc.at[group(block), 1 - self.me.c],
            self.theirs.at[group(block)],
            self.sib.at[0, block],
            self.sib.at[1, block],
            self.me.sibling(),
        )
        cp.start()
        self.shares[block] = cp

    def finish(self, block):
        self.shares[block].wait_recv()
        rows = BLOCK * 32
        both = self.acc[group(block), self.me.c] + self.theirs[group(block)]
        both = both.reshape(rows, 2 * LANES)
        dq = self.dq[group(block)].reshape(rows, 2 * LANES)
        heads = [both[:, :LANES] * SCALE, both[:, LANES:], dq[:, :LANES], dq[:, LANES:]]
        self.bundle[group(block)] = pack_four(heads).astype(jnp.bfloat16).reshape(BLOCK, 32, PACKED)
        self.going.start(block)

    def block(self, block):
        count = keys_of(block)
        spread = pl.ds(0, count // 64)
        k = self.keys[pl.ds(0, count), :]
        v = self.values[pl.ds(0, count), :]
        allowed = block_mask(block, count, self.me.c, self.prefix[0])
        quarters = split_four(self.datt[group(block)].reshape(BLOCK * 16, PACKED).astype(jnp.float32))
        inside = lax.broadcasted_iota(jnp.int32, (BLOCK * 32, LANES), 1) < HEAD
        for h in range(2):
            q = self.queries[h, pl.ds(block * BLOCK * 32, BLOCK * 32), :]
            g = jnp.concatenate([quarters[2 * r + h].reshape(BLOCK, 16, LANES) for r in range(2)], axis=1)
            g = g.reshape(BLOCK * 32, LANES).astype(jnp.bfloat16)
            s = jnp.where(allowed, f32dot(q, k, ((1,), (1,))) * SCALE, NEG)
            top = jnp.max(s, axis=-1, keepdims=True)
            e = jnp.exp(s - top)
            p = e * (1.0 / jnp.sum(e, axis=-1, keepdims=True))
            dp = f32dot(g, v, ((1,), (1,)))
            delta = jnp.sum(p * dp, axis=-1, keepdims=True)
            ds = (p * (dp - delta)).astype(jnp.bfloat16)
            dq = jnp.where(inside, f32dot(ds, k, ((1,), (0,))) * SCALE, 0.0)
            self.dq[group(block), :, LANES * h : LANES * (h + 1)] = dq.reshape(BLOCK, 32, LANES)
            dk = f32dot(ds, q, ((0,), (0,))).reshape(count // 64, 2, 32, LANES)
            dv = f32dot(p.astype(jnp.bfloat16), g, ((0,), (0,))).reshape(count // 64, 2, 32, LANES)
            if block == BLOCKS - 1 and h == 0:
                self.acc[spread, :, :, 0:LANES] = dk
                self.acc[spread, :, :, LANES : 2 * LANES] = dv
            else:
                self.acc[spread, :, :, 0:LANES] += dk
                self.acc[spread, :, :, LANES : 2 * LANES] += dv

    def steps(self):
        self.coming.start_all()
        yield
        self.coming.arrived(0, ORIGINS)
        self.block(3)
        self.share(3)
        self.block(2)
        self.share(2)
        self.finish(3)
        self.block(1)
        self.finish(2)
        self.block(0)
        self.share(1)
        self.share(0)
        self.finish(1)
        self.finish(0)
        yield
        self.going.arrived(0, ORIGINS)
        self.coming.sent()
        self.going.sent()
        for cp in self.shares.values():
            cp.wait_send()


ATTEND_BACK_SCRATCH = [
    pltpu.VMEM((ORIGINS, 16, PACKED), jnp.bfloat16),
    pltpu.VMEM((ORIGINS, 2, 32, 2 * LANES), jnp.float32),
    pltpu.VMEM((ORIGINS, 32, 2 * LANES), jnp.float32),
    pltpu.VMEM((ORIGINS, 32, 2 * LANES), jnp.float32),
    pltpu.VMEM((ORIGINS, 32, PACKED), jnp.bfloat16),
    *EXCHANGE_SEMS,
    *EXCHANGE_SEMS,
    pltpu.SemaphoreType.DMA((2, BLOCKS)),
]
RETURNED = ((ORIGINS, 32, PACKED), jnp.bfloat16)


def attend_back_kernel(prefix, keys, values, queries, src, dst, *scratch):
    me = Place()
    meet_plane(me)
    for _ in AttendBack(me, prefix, keys, values, queries, src, dst, scratch).steps():
        pass


def attend_back(prefix, kept, src):
    return pl.pallas_call(
        attend_back_kernel,
        out_shape=jax.ShapeDtypeStruct(*RETURNED),
        in_specs=[SMEM] + [VMEM] * 4,
        out_specs=VMEM,
        scratch_shapes=ATTEND_BACK_SCRATCH,
        compiler_params=pltpu.CompilerParams(
            collective_id=4, has_side_effects=True, vmem_limit_bytes=60 * MIB
        ),
        name="attend_back",
    )(prefix, *kept, src)


def leave_kernel(prefix, keys, values, queries, src, *refs):
    m, n = len(MLP_ARRAYS), len(ATTEND_BACK_SCRATCH)
    ins, outs, dst = refs[:m], refs[m : 2 * m], refs[2 * m]
    scratch = refs[2 * m + 1 :]
    me = Place()
    scatter = Scatter(me, MLP_PIECES, MLP_ARRAYS, ins, outs, scratch[n:])
    attention = AttendBack(me, prefix, keys, values, queries, src, dst, scratch[:n]).steps()
    meet_plane(me, [me.dp_peer()])
    sums = scatter_steps(scatter)
    next(attention)
    next(sums)
    next(attention)
    for _ in sums:
        pass
    for _ in attention:
        pass


def leave(prefix, kept, src, parts):
    m = len(MLP_ARRAYS)
    return pl.pallas_call(
        leave_kernel,
        out_shape=scatter_shapes(MLP_ARRAYS) + [jax.ShapeDtypeStruct(*RETURNED)],
        in_specs=[SMEM] + [VMEM] * 4 + [ANY] * m,
        out_specs=[ANY] * m + [VMEM],
        scratch_shapes=ATTEND_BACK_SCRATCH + scatter_scratch(MLP_PIECES, MLP_ARRAYS),
        compiler_params=pltpu.CompilerParams(
            collective_id=5, has_side_effects=True, vmem_limit_bytes=62 * MIB
        ),
        name="leave",
    )(prefix, *kept, src, *in_shards(parts, MLP_ARRAYS))


def pair_kernel(whole_count, *refs):
    n = (len(refs) - 3) // 2
    ins, outs = refs[:n], refs[n : 2 * n]
    send_sem, recv_sem, own_sem = refs[2 * n :]
    me = Place()
    meet([me.sibling()])
    copies = []
    for i in range(n):
        here = there = ins[i]
        if i >= whole_count:
            width = ins[i].shape[1] // 2
            here = ins[i].at[:, pl.ds(pl.multiple_of(me.c * width, LANES), width)]
            there = ins[i].at[:, pl.ds(pl.multiple_of((1 - me.c) * width, LANES), width)]
        cp = remote(there, outs[i].at[me.c], send_sem.at[i], recv_sem.at[i], me.sibling())
        cp.start()
        copies.append(cp)
        cp = pltpu.make_async_copy(here, outs[i].at[me.c], own_sem.at[i])
        cp.start()
        copies.append(cp)
    for cp in copies:
        cp.wait()


def pair_up(collective_id, whole, halved):
    n = len(whole) + len(halved)
    return pl.pallas_call(
        functools.partial(pair_kernel, len(whole)),
        out_shape=[jax.ShapeDtypeStruct((2, *a.shape), a.dtype) for a in whole]
        + [jax.ShapeDtypeStruct((2, a.shape[0], a.shape[1] // 2), a.dtype) for a in halved],
        in_specs=[VMEM] * n,
        out_specs=[VMEM] * n,
        scratch_shapes=[pltpu.SemaphoreType.DMA((n,))] * 3,
        compiler_params=pltpu.CompilerParams(
            collective_id=collective_id, has_side_effects=True, vmem_limit_bytes=40 * MIB
        ),
        name="pair_up",
    )(*whole, *halved)


STEPS = 8
FF_BLOCK = 512


def rope_tables(positions):
    lane = jnp.arange(PACKED)
    head, spot = lane // HEAD, lane % HEAD
    frequency = ROPE_BASE ** (-(lane % HALF).astype(jnp.float32) * 2.0 / HEAD)
    angles = positions.astype(jnp.float32)[:, None] * frequency[None, :]
    cos, sin = jnp.cos(angles), jnp.sin(angles)
    still, low = (head == 1)[None, :], (spot < HALF)[None, :]
    return (
        jnp.where(still, 1.0, cos),
        jnp.where(still | ~low, 0.0, -sin),
        jnp.where(still | low, 0.0, sin),
    )


def whole_spec(a):
    return pl.BlockSpec(a.shape, lambda k: (0,) * a.ndim, pipeline_mode=pl.Buffered(1))


def mlp_kernel(
    att, x, gain, o_w, gate_w, up_w, down_w, result, attended, middle, normed_two, gate, up, mixed, total
):
    k = pl.program_id(0)

    @pl.when(k == 0)
    def _():
        low_half = lax.broadcasted_iota(jnp.int32, (64, PACKED), 1) < 2 * HEAD
        for pair in range(KV_HEADS // 2):
            even, odd = (
                att[:, 2 * pair + j].reshape(64, PACKED).astype(jnp.float32) for j in range(2)
            )
            upper = jnp.where(low_half, even, pltpu.roll(odd, 2 * HEAD, axis=1))
            lower = jnp.where(low_half, pltpu.roll(even, 2 * HEAD, axis=1), odd)
            rows = jnp.concatenate([upper.reshape(4, 16, PACKED), lower.reshape(4, 16, PACKED)], axis=1)
            attended[:, PACKED * pair : PACKED * (pair + 1)] = rows.reshape(128, PACKED).astype(jnp.bfloat16)
        mid = x[...].astype(jnp.float32) + f32dot(attended[...], o_w[...], ((1,), (0,)))
        middle[...] = mid
        r2 = lax.rsqrt(jnp.mean(mid * mid, axis=-1, keepdims=True) + EPS)
        normed_two[...] = (mid * r2 * gain[0:1, :]).astype(jnp.bfloat16)
        total[...] = mid

    g = f32dot(normed_two[...], gate_w[...], ((1,), (0,)))
    u = f32dot(normed_two[...], up_w[...], ((1,), (0,)))
    gate[...] = g
    up[...] = u
    m = (g * jax.nn.sigmoid(g) * u).astype(jnp.bfloat16)
    mixed[...] = m
    total[...] += f32dot(m, down_w[...], ((1,), (0,)))

    @pl.when(k == STEPS - 1)
    def _():
        result[...] = total[...].astype(jnp.bfloat16)


def mlp(att, x, gain, o_w, gate_w, up_w, down_w):
    tokens, width = x.shape
    ff = gate_w.shape[1]
    in_block = pl.BlockSpec((width, FF_BLOCK), lambda k: (0, k))
    ff_block = pl.BlockSpec((tokens, FF_BLOCK), lambda k: (0, k))
    fixed = pl.BlockSpec((tokens, width), lambda k: (0, 0))
    return pl.pallas_call(
        mlp_kernel,
        grid=(STEPS,),
        out_shape=[
            jax.ShapeDtypeStruct((tokens, width), jnp.bfloat16),
            jax.ShapeDtypeStruct((tokens, width), jnp.bfloat16),
            jax.ShapeDtypeStruct((tokens, width), jnp.float32),
            jax.ShapeDtypeStruct((tokens, width), jnp.bfloat16),
            jax.ShapeDtypeStruct((tokens, ff), jnp.float32),
            jax.ShapeDtypeStruct((tokens, ff), jnp.float32),
            jax.ShapeDtypeStruct((tokens, ff), jnp.bfloat16),
        ],
        in_specs=[
            whole_spec(att),
            whole_spec(x),
            whole_spec(gain),
            whole_spec(o_w),
            in_block,
            in_block,
            pl.BlockSpec((FF_BLOCK, width), lambda k: (k, 0)),
        ],
        out_specs=[fixed, fixed, fixed, fixed, ff_block, ff_block, ff_block],
        scratch_shapes=[pltpu.VMEM((tokens, width), jnp.float32)],
        compiler_params=pltpu.CompilerParams(vmem_limit_bytes=48 * MIB),
        name="mlp",
    )(att, x, gain, o_w, gate_w, up_w, down_w)


def norm_back(dn, gain, u, r):
    scaled = dn * gain
    return r * (scaled - u * jnp.mean(scaled * u, axis=-1, keepdims=True))


def mlp_back_kernel(
    g_low, gate, up, middle, gain, o_w, gate_w, up_w, down_w, dgate, dup, dmiddle, db, dgain, datt, total
):
    k = pl.program_id(0)

    @pl.when(k == 0)
    def _():
        total[...] = jnp.zeros_like(total)

    gm = f32dot(g_low[...], down_w[...], ((1,), (1,)))
    sig = jax.nn.sigmoid(gate[...])
    dg = (gm * up[...] * sig * (1.0 + gate[...] * (1.0 - sig))).astype(jnp.bfloat16)
    du = (gm * (gate[...] * sig)).astype(jnp.bfloat16)
    dgate[...] = dg
    dup[...] = du
    total[...] += f32dot(dg, gate_w[...], ((1,), (1,))) + f32dot(du, up_w[...], ((1,), (1,)))

    @pl.when(k == STEPS - 1)
    def _():
        mid, dn2 = middle[...], total[...]
        r2 = lax.rsqrt(jnp.mean(mid * mid, axis=-1, keepdims=True) + EPS)
        u2 = mid * r2
        dgain[...] = jnp.broadcast_to(jnp.sum(dn2 * u2, axis=0, keepdims=True), dgain.shape)
        dm = g_low[...].astype(jnp.float32) + norm_back(dn2, gain[0:1, :], u2, r2)
        dmiddle[...] = dm
        low = dm.astype(jnp.bfloat16)
        db[...] = low
        low_half = lax.broadcasted_iota(jnp.int32, (4, 16, PACKED), 2) < 2 * HEAD
        for pair in range(KV_HEADS // 2):
            y = f32dot(low, o_w[PACKED * pair : PACKED * (pair + 1), :], ((1,), (1,)))
            turned = pltpu.roll(y, 2 * HEAD, axis=1).reshape(4, 32, PACKED)
            y = y.reshape(4, 32, PACKED)
            even = jnp.where(low_half, y[:, :16], turned[:, 16:])
            odd = jnp.where(low_half, turned[:, :16], y[:, 16:])
            for j, z in enumerate((even, odd)):
                datt[:, 2 * pair + j] = z.astype(jnp.bfloat16).reshape(2, 2, 16, PACKED)


def mlp_back(g_low, gate, up, middle, gain, o_w, gate_w, up_w, down_w):
    tokens, width = g_low.shape
    ff = gate_w.shape[1]
    in_block = pl.BlockSpec((width, FF_BLOCK), lambda k: (0, k))
    ff_block = pl.BlockSpec((tokens, FF_BLOCK), lambda k: (0, k))
    fixed = pl.BlockSpec((tokens, width), lambda k: (0, 0))
    datt_shape = (2, KV_HEADS, 2, 16, PACKED)
    return pl.pallas_call(
        mlp_back_kernel,
        grid=(STEPS,),
        out_shape=[
            jax.ShapeDtypeStruct((tokens, ff), jnp.bfloat16),
            jax.ShapeDtypeStruct((tokens, ff), jnp.bfloat16),
            jax.ShapeDtypeStruct((tokens, width), jnp.float32),
            jax.ShapeDtypeStruct((tokens, width), jnp.bfloat16),
            jax.ShapeDtypeStruct((8, width), jnp.float32),
            jax.ShapeDtypeStruct(datt_shape, jnp.bfloat16),
        ],
        in_specs=[
            whole_spec(g_low),
            ff_block,
            ff_block,
            whole_spec(middle),
            whole_spec(gain),
            whole_spec(o_w),
            in_block,
            in_block,
            pl.BlockSpec((FF_BLOCK, width), lambda k: (k, 0)),
        ],
        out_specs=[
            ff_block,
            ff_block,
            fixed,
            fixed,
            pl.BlockSpec((8, width), lambda k: (0, 0)),
            pl.BlockSpec(datt_shape, lambda k: (0,) * 5),
        ],
        scratch_shapes=[pltpu.VMEM((tokens, width), jnp.float32)],
        compiler_params=pltpu.CompilerParams(vmem_limit_bytes=48 * MIB),
        name="mlp_back",
    )(g_low, gate, up, middle, gain, o_w, gate_w, up_w, down_w)


def qkv_back_kernel(back_in, cos, ahead, back, w, x, dmiddle, gain, dqkv, dx, dgain, total):
    k = pl.program_id(0)

    @pl.when(k == 0)
    def _():
        total[...] = jnp.zeros_like(total)

    z = back_in[...].reshape(128, PACKED).astype(jnp.float32)
    packed = turn_heads(z, cos[...], -ahead[...], -back[...]).astype(jnp.bfloat16)
    dqkv[...] = packed
    total[...] += f32dot(packed, w[...], ((1,), (1,)))

    @pl.when(k == KV_HEADS - 1)
    def _():
        hidden, dn1 = x[...].astype(jnp.float32), total[...]
        r1 = lax.rsqrt(jnp.mean(hidden * hidden, axis=-1, keepdims=True) + EPS)
        u1 = hidden * r1
        dgain[...] = jnp.broadcast_to(jnp.sum(dn1 * u1, axis=0, keepdims=True), dgain.shape)
        dx[...] = (dmiddle[...] + norm_back(dn1, gain[0:1, :], u1, r1)).astype(jnp.bfloat16)


def project_back(back_in, tables, w, x, dmiddle, gain):
    tokens, width = x.shape
    return pl.pallas_call(
        qkv_back_kernel,
        grid=(KV_HEADS,),
        out_shape=[
            jax.ShapeDtypeStruct((tokens, 2 * width), jnp.bfloat16),
            jax.ShapeDtypeStruct((tokens, width), jnp.bfloat16),
            jax.ShapeDtypeStruct((8, width), jnp.float32),
        ],
        in_specs=[
            pl.BlockSpec((2, 1, tokens // 2, PACKED), lambda k: (0, k, 0, 0)),
            *[whole_spec(t) for t in tables],
            pl.BlockSpec((width, 4 * HEAD), lambda k: (0, k)),
            whole_spec(x),
            whole_spec(dmiddle),
            whole_spec(gain),
        ],
        out_specs=[
            pl.BlockSpec((tokens, 4 * HEAD), lambda k: (0, k)),
            pl.BlockSpec((tokens, width), lambda k: (0, 0)),
            pl.BlockSpec((8, width), lambda k: (0, 0)),
        ],
        scratch_shapes=[pltpu.VMEM((tokens, width), jnp.float32)],
        compiler_params=pltpu.CompilerParams(vmem_limit_bytes=56 * MIB),
        name="project_back",
    )(back_in, *tables, w, x, dmiddle, gain)


def body(
    inputs, prefix, cotangent, attn_gain, w_query, w_key, w_value, w_out, mlp_gain, w_gate, w_up, w_down
):
    seqs, rows, width = inputs.shape
    tokens = seqs * rows
    section = lax.axis_index("section")
    seq = lax.axis_index("seq")
    positions = seq * rows + jnp.arange(rows, dtype=jnp.int32)
    tables = rope_tables(jnp.concatenate([positions, positions]))
    own_prefix = lax.dynamic_slice_in_dim(prefix, seq // 16, 1)

    part = w_query.shape[1]
    qkv_shard = jnp.concatenate(
        [
            w_key[0].reshape(part, KV_HEADS, HEAD),
            w_value[0].reshape(part, KV_HEADS, HEAD),
            w_query[0].reshape(part, KV_HEADS, 2 * HEAD),
        ],
        -1,
    ).reshape(part, 2 * width)
    gain_shard = jnp.concatenate(
        [
            jnp.broadcast_to(attn_gain[0][:, None], (part, LANES)),
            jnp.broadcast_to(mlp_gain[0][:, None], (part, LANES)),
        ],
        -1,
    )
    x0 = inputs.reshape(tokens, width)
    gate_w, up_w, qkv_split, o_w, _, down_w, gains, att = enter(
        own_prefix, x0, tables, [w_gate[0], w_up[0], qkv_shard, w_out[0], gain_shard, w_down[0]]
    )
    gate_w, up_w, qkv_w, o_w, down_w = (
        w.reshape(-1, w.shape[-1]) for w in (gate_w, up_w, qkv_split, o_w, down_w)
    )
    gain_attn, gain_mlp = gains[0], gains[1]

    def feed_forward(att, x):
        return mlp(att.reshape(2, KV_HEADS, 2, 16, PACKED), x, gain_mlp, o_w, gate_w, up_w, down_w)

    out0 = feed_forward(att, x0)[0]
    received = lax.ppermute(out0, "section", [(0, 1)])
    x = jnp.where(section == 0, x0, received)
    normed, *kept, att = attend(own_prefix, x, gain_attn, tables, qkv_split)
    out, attended, middle, normed_two, gate, up, mixed = feed_forward(att, x)

    def feed_forward_back(g_low):
        return mlp_back(g_low, gate, up, middle, gain_mlp, o_w, gate_w, up_w, down_w)

    def attention_back(back, dmiddle):
        back = back.reshape(2, KV_HEADS, rows, PACKED)
        return project_back(back, tables, qkv_w, x, dmiddle, gain_attn)

    g0 = cotangent.reshape(tokens, width)
    _, _, dmiddle, _, _, datt = feed_forward_back(g0)
    back = attend_back(own_prefix, kept, datt.reshape(ORIGINS, 16, PACKED))
    _, dx0, _ = attention_back(back, dmiddle)
    received = lax.ppermute(dx0, "section", [(1, 0)])
    g_low = jnp.where(section == 1, g0, received)

    def outer(a, b):
        a, b = a.reshape(2 * tokens, -1), b.reshape(2 * tokens, -1)
        return lax.dot_general(
            a, b, (((0,), (0,)), ((), ())), preferred_element_type=jnp.float32
        ).astype(jnp.bfloat16)

    dgate, dup, dmiddle, db, dgain_mlp, datt = feed_forward_back(g_low)
    normed_two, mixed, g_half, dgate, dup = pair_up(6, [normed_two, mixed], [g_low, dgate, dup])
    gate_g, up_g, down_g, back = leave(
        own_prefix,
        kept,
        datt.reshape(ORIGINS, 16, PACKED),
        [outer(normed_two, dgate), outer(normed_two, dup), outer(mixed, g_half)],
    )
    dqkv, dx, dgain_attn = attention_back(back, dmiddle)
    dgains = jnp.concatenate([dgain_attn, dgain_mlp], axis=1)
    normed, attended, db, dqkv, dgains = pair_up(7, [normed, attended], [db, dqkv, dgains])
    gain_part = jnp.broadcast_to(
        (dgains[0, 0] + dgains[1, 0]).astype(jnp.bfloat16)[:, None], (width, LANES)
    )
    qkv_g, o_g, gain_g = scatter_attn([outer(normed, dqkv), outer(attended, db), gain_part])
    qkv_g = qkv_g.reshape(1, part, KV_HEADS, PACKED)
    key_g = qkv_g[..., :HEAD].reshape(1, part, -1)
    value_g = qkv_g[..., HEAD : 2 * HEAD].reshape(1, part, -1)
    query_g = qkv_g[..., 2 * HEAD :].reshape(1, part, -1)
    return (
        out.reshape(1, seqs, rows, width),
        dx.reshape(1, seqs, rows, width),
        gain_g[:, 0][None],
        query_g,
        key_g,
        value_g,
        o_g[None],
        gain_g[:, LANES][None],
        gate_g[None],
        up_g[None],
        down_g[None],
    )


def solution(mesh):
    split = ("dp", "seq")
    matrix = P("section", split, None)
    vector = P("section", split)
    rows = P("dp", "seq", None)
    layer = P("section", "dp", "seq", None)
    return jax.shard_map(
        body,
        mesh=mesh,
        in_specs=(
            rows, P("dp"), rows, vector, matrix, matrix, matrix, matrix, vector, matrix, matrix, matrix
        ),
        out_specs=(
            layer, layer, vector, matrix, matrix, matrix, matrix, vector, matrix, matrix, matrix
        ),
        check_vma=False,
    )
```

```python
import functools
import math

import jax
import jax.numpy as jnp
from jax import lax
from jax.experimental import pallas as pl
from jax.experimental.pallas import tpu as pltpu
from jax.sharding import PartitionSpec as P

HEADS = 16
KV_HEADS = 8
HEAD = 96
LANES = 128
HALF = HEAD // 2
PACKED = 4 * HEAD
EPS = 1e-05
ROPE_BASE = 100000.0
NEG = -1e30
PREFIX_MAX = 1024
SCALE = 1.0 / math.sqrt(HEAD)
MESH = pl.DeviceIdType.MESH
ANY = pl.BlockSpec(memory_space=pl.ANY)
VMEM = pl.BlockSpec(memory_space=pltpu.VMEM)
SMEM = pl.BlockSpec(memory_space=pltpu.SMEM)
MIB = 1 << 20

ARRAYS = ((24, 2048), (24, 2048), (24, 1536), (24, 768), (24, 128), (64, 768))
GATE, UP, QKV, OUT, GAIN, DOWN = range(6)
QKV_PIECES = (
    (QKV, 0, 512, "y", 1, -1),
    (QKV, 512, 256, "y", -1, -1),
    (QKV, 768, 512, "z", 1, -1),
    (QKV, 1280, 256, "z", -1, -1),
    (GAIN, 0, 128, "y", 1, -1),
)
GATHER_PIECES = QKV_PIECES + (
    (GATE, 1024, 1024, "y", -1, None),
    (UP, 1024, 1024, "z", -1, None),
    (OUT, 0, 384, "y", -1, 1),
    (OUT, 384, 384, "z", -1, 1),
    (GATE, 0, 1024, "y", 1, -1),
    (UP, 0, 1024, "z", 1, -1),
    (DOWN, 0, 384, "y", 1, 1),
    (DOWN, 384, 384, "z", 1, 1),
)
LAST_ARRAYS = (QKV, GAIN)
LAST_PIECES = (
    (QKV, 0, 256, "y", 1, 1),
    (QKV, 768, 256, "z", 1, 1),
    (QKV, 256, 256, "y", -1, -1),
    (QKV, 1024, 256, "z", -1, -1),
    (GAIN, 0, 128, "y", -1, -1),
    (QKV, 512, 256, "y", 1, None),
    (QKV, 1280, 256, "z", 1, None),
)
MAIN_ARRAYS = (GATE, UP, OUT, DOWN)
MAIN_PIECES = (
    (GATE, 0, 1024, "y", 1, 1),
    (UP, 0, 1024, "z", 1, 1),
    (DOWN, 0, 384, "y", -1, -1),
    (DOWN, 384, 384, "z", -1, -1),
    (OUT, 0, 384, "y", -1, None),
    (OUT, 384, 384, "z", -1, None),
    (GATE, 1024, 1024, "y", 1, None),
    (UP, 1024, 1024, "z", 1, None),
)
OTHER = {"y": "z", "z": "y"}


def f32dot(a, b, dims):
    return lax.dot_general(a, b, (dims, ((), ())), preferred_element_type=jnp.float32)


class Place:
    def __init__(self):
        self.s = lax.axis_index("section")
        self.d = lax.axis_index("dp")
        self.q = lax.axis_index("seq")
        self.y = lax.div(self.q, 8)
        self.z = lax.rem(lax.div(self.q, 2), 4)
        self.c = lax.rem(self.q, 2)

    def coord(self, axis):
        return self.y if axis == "y" else self.z

    def step(self, axis, by):
        y, z = self.y, self.z
        if axis == "y":
            y = lax.rem(y + by + 4, 4)
        else:
            z = lax.rem(z + by + 4, 4)
        return (self.s, self.d, y * 8 + z * 2 + self.c)

    def sibling(self):
        return (self.s, self.d, self.q + 1 - 2 * self.c)

    def dp_peer(self):
        return (self.s, 1 - self.d, self.q)


def meet(devices):
    barrier = pltpu.get_barrier_semaphore()
    for device in devices:
        pl.semaphore_signal(barrier, inc=1, device_id=device, device_id_type=MESH)
    pl.semaphore_wait(barrier, len(devices))


def remote(src, dst, send, recv, device):
    return pltpu.make_async_remote_copy(
        src_ref=src, dst_ref=dst, send_sem=send, recv_sem=recv, device_id=device, device_id_type=MESH
    )


EARLY = len(QKV_PIECES)


class Gather:
    def __init__(self, me, ins, outs, scratch):
        n = len(ARRAYS)
        self.me, self.ins, self.outs = me, ins, outs
        self.give, self.got, self.chip = scratch[:n], scratch[n : 2 * n], scratch[2 * n : 3 * n]
        self.first, self.local, self.over, self.ring_s, self.ring_r, self.sib_s, self.sib_r = scratch[3 * n :]
        self.dps = (me.d, 1 - me.d)
        self.one, self.two, self.held, self.overs, self.swaps = {}, {}, {}, {}, {}
        self.shares, self.pending = {}, []

    def neighbours(self):
        me = self.me
        near = [me.step(axis, by) for axis in "yz" for by in (1, -1)]
        return near + [me.dp_peer(), me.sibling()]

    def lanes(self, i):
        array, start, width = GATHER_PIECES[i][:3]
        return pl.ds(pl.multiple_of(self.me.c * ARRAYS[array][1] + start, LANES), width)

    def along(self, i, dp, by):
        array, _, _, a1 = GATHER_PIECES[i][:4]
        pos = lax.rem(self.me.coord(a1) + by + 4, 4)
        y, z = (pos, self.me.z) if a1 == "y" else (self.me.y, pos)
        return self.outs[array].at[dp, y, z, :, self.lanes(i)]

    def across(self, i, dp, by):
        array, _, _, a1 = GATHER_PIECES[i][:4]
        pos = lax.rem(self.me.coord(OTHER[a1]) + by + 4, 4)
        if a1 == "y":
            return self.outs[array].at[dp, pl.ds(0, 4), pos, :, self.lanes(i)]
        return self.outs[array].at[dp, pos, pl.ds(0, 4), :, self.lanes(i)]

    def send(self, i, block, k, src, dst, device):
        cp = remote(src, dst, self.ring_s.at[i, block, k], self.ring_r.at[i, block, k], device)
        cp.start()
        self.pending.append(cp)
        return cp

    def share(self, i, block, k, ref, src=None):
        src = ref if src is None else src
        cp = remote(src, ref, self.sib_s.at[i, block, k], self.sib_r.at[i, block, k], self.me.sibling())
        cp.start()
        self.pending.append(cp)
        self.shares.setdefault(i, []).append(cp)
        if block == 0 and (k == 0 or self.crosses(i)):
            cp = remote(src, ref, self.over.at[0, i, k], self.over.at[1, i, k], self.me.dp_peer())
            cp.start()
            self.pending.append(cp)
            self.overs[i, k] = cp

    def crosses(self, i):
        return GATHER_PIECES[i][5] is None

    def way(self, i, block):
        return GATHER_PIECES[i][4 + block]

    def both(self, pieces):
        return [i for i in pieces if not self.crosses(i)]

    def cross(self, pieces, spots):
        for k in spots:
            for i in pieces:
                if self.crosses(i):
                    way = self.way(i, 0)
                    by = (0, -way, way, 2, -way, way, 2)[k]
                    place = self.along if k < 4 else self.across
                    self.overs[i, k].wait_recv()
                    self.share(i, 1, k, place(i, self.dps[1], by))

    def swap(self):
        me = self.me
        for a, (_, width) in enumerate(ARRAYS):
            start = pl.multiple_of((1 - me.c) * width, LANES)
            self.give[a][...] = self.ins[a][:, pl.ds(start, width)].astype(jnp.float32)
            cp = remote(self.give[a], self.got[a], self.first.at[0, a], self.first.at[1, a], me.sibling())
            cp.start()
            self.swaps[a] = cp

    def join(self, a):
        me, width = self.me, ARRAYS[a][1]
        self.swaps[a].wait()
        start = pl.multiple_of(me.c * width, LANES)
        mine = self.ins[a][:, pl.ds(start, width)].astype(jnp.float32)
        theirs = self.got[a][...]
        low = jnp.where(me.c == 0, mine, theirs)
        high = jnp.where(me.c == 0, theirs, mine)
        self.chip[a][...] = jnp.concatenate([low, high], axis=0).astype(jnp.bfloat16)

    def start(self, pieces):
        me = self.me
        for i in pieces:
            array, start, width, a1 = GATHER_PIECES[i][:4]
            src = self.chip[array].at[:, pl.ds(start, width)]
            here = self.along(i, me.d, 0)
            self.one[i, 0, 1] = self.send(i, 0, 0, src, here, me.step(a1, 1))
            self.one[i, 0, -1] = self.send(i, 0, 1, src, here, me.step(a1, -1))
            cp = pltpu.make_async_copy(src, here, self.local.at[i])
            cp.start()
            self.held[i] = cp
            self.share(i, 0, 0, here, src)

    def start_other(self, pieces):
        me = self.me
        for i in self.both(pieces):
            a1 = GATHER_PIECES[i][3]
            self.overs[i, 0].wait_recv()
            here = self.along(i, self.dps[1], 0)
            self.one[i, 1, 1] = self.send(i, 1, 0, here, here, me.step(a1, 1))
            self.one[i, 1, -1] = self.send(i, 1, 1, here, here, me.step(a1, -1))
            self.share(i, 1, 0, here)

    def hop(self, pieces, block, second):
        kept, place, base = (self.two, self.across, 3) if second else (self.one, self.along, 0)
        dp = self.dps[block]
        pieces = self.both(pieces) if block else pieces
        for i in pieces:
            axis, way = GATHER_PIECES[i][3], self.way(i, block)
            axis = OTHER[axis] if second else axis
            kept[i, block, way].wait_recv()
            came = place(i, dp, -way)
            kept[i, block, 0] = self.send(i, block, base + 2, came, came, self.me.step(axis, way))
            self.share(i, block, base + 1, came)
        for i in pieces:
            way = self.way(i, block)
            kept[i, block, -way].wait_recv()
            self.share(i, block, base + 2, place(i, dp, way))

    def turn(self, pieces, block):
        dp = self.dps[block]
        for i in self.both(pieces) if block else pieces:
            a2 = OTHER[GATHER_PIECES[i][3]]
            self.one[i, block, 0].wait_recv()
            self.share(i, block, 3, self.along(i, dp, 2))
            if block == 0:
                self.held[i].wait()
            here = self.across(i, dp, 0)
            self.two[i, block, 1] = self.send(i, block, 3, here, here, self.me.step(a2, 1))
            self.two[i, block, -1] = self.send(i, block, 4, here, here, self.me.step(a2, -1))

    def finish(self, pieces, block):
        for i in self.both(pieces) if block else pieces:
            self.two[i, block, 0].wait_recv()
            self.share(i, block, 6, self.across(i, self.dps[block], 2))

    def shown(self, pieces):
        for i in pieces:
            for cp in self.shares[i]:
                cp.wait_recv()

    def drain(self):
        for cp in self.pending:
            cp.wait_send()


GATHER_SCRATCH = (
    [pltpu.VMEM(shape, jnp.float32) for shape in ARRAYS]
    + [pltpu.VMEM(shape, jnp.float32) for shape in ARRAYS]
    + [pltpu.VMEM((2 * rows, width), jnp.bfloat16) for rows, width in ARRAYS]
    + [
        pltpu.SemaphoreType.DMA((2, len(ARRAYS))),
        pltpu.SemaphoreType.DMA((len(GATHER_PIECES),)),
        pltpu.SemaphoreType.DMA((2, len(GATHER_PIECES), 7)),
        pltpu.SemaphoreType.DMA((len(GATHER_PIECES), 2, 6)),
        pltpu.SemaphoreType.DMA((len(GATHER_PIECES), 2, 6)),
        pltpu.SemaphoreType.DMA((len(GATHER_PIECES), 2, 7)),
        pltpu.SemaphoreType.DMA((len(GATHER_PIECES), 2, 7)),
    ]
)


def gather_steps(gather):
    early = range(EARLY)
    late = range(EARLY, len(GATHER_PIECES))
    gather.swap()
    for a in (QKV, GAIN):
        gather.join(a)
    gather.start(early)
    for a in (OUT, GATE, UP, DOWN):
        gather.join(a)
    gather.start(late)
    gather.hop(early, 0, False)
    gather.turn(early, 0)
    gather.start_other(early)
    gather.hop(late, 0, False)
    gather.hop(early, 1, False)
    gather.turn(early, 1)
    gather.turn(late, 0)
    gather.start_other(late)
    gather.hop(early, 0, True)
    gather.hop(late, 1, False)
    gather.hop(early, 1, True)
    gather.finish(early, 0)
    gather.hop(late, 0, True)
    gather.turn(late, 1)
    gather.finish(early, 1)
    gather.shown(early)
    yield
    gather.finish(late, 0)
    gather.cross(late, range(4))
    gather.hop(late, 1, True)
    yield
    gather.finish(late, 1)
    gather.cross(late, range(4, 7))
    gather.shown(late)
    gather.drain()


def add_into(total, term):
    chunks = total.shape[1] // 16

    def step(k, carry):
        j = lax.div(k, chunks)
        rows = pl.ds(pl.multiple_of(lax.rem(k, chunks) * 16, 16), 16)
        both = total[j, rows, :].astype(jnp.float32) + term[j, rows, :].astype(jnp.float32)
        total[j, rows, :] = both.astype(jnp.bfloat16)
        return carry

    lax.fori_loop(0, total.shape[0] * chunks, step, 0)


def add_two(total, left, right):
    chunks = total.shape[1] // 16

    def step(k, carry):
        j = lax.div(k, chunks)
        rows = pl.ds(pl.multiple_of(lax.rem(k, chunks) * 16, 16), 16)
        parts = [ref[j, rows, :].astype(jnp.float32) for ref in (total, left, right)]
        total[j, rows, :] = (parts[0] + (parts[1] + parts[2])).astype(jnp.bfloat16)
        return carry

    lax.fori_loop(0, total.shape[0] * chunks, step, 0)


class Scatter:
    def __init__(self, me, pieces, arrays, ins, outs, scratch):
        n, m = len(pieces), len(arrays)
        self.me, self.pieces, self.ins, self.outs = me, pieces, ins, outs
        self.at = {a: k for k, a in enumerate(arrays)}
        names = ("near", "far", "last", "mid", "own", "near1", "far1", "last1", "sent", "came")
        for k, name in enumerate(names):
            setattr(self, name, scratch[k * n : (k + 1) * n])
        rest = scratch[len(names) * n :]
        whole = [i for i in range(n) if self.crosses(i)]
        self.ours, rest = dict(zip(whole, rest)), rest[len(whole) :]
        self.theirs, rest = dict(zip(whole, rest)), rest[len(whole) :]
        self.total, rest = rest[:m], rest[m:]
        self.load, self.ring_s, self.ring_r, self.over, self.fin, self.keep = rest
        self.dps = (1 - me.d, me.d)
        self.loads, self.one, self.two, self.overs, self.pending = {}, {}, {}, {}, []

    def neighbours(self):
        me = self.me
        near = [me.step(axis, by) for axis in "yz" for by in (1, -1)]
        return near + [me.dp_peer(), me.sibling()]

    def crosses(self, i):
        return self.pieces[i][5] is None

    def way(self, i, block):
        return self.pieces[i][5 - block]

    def of(self, block, crossing=None):
        picked = [i for i in range(len(self.pieces)) if block or not self.crosses(i)]
        return [i for i in picked if crossing is None or self.crosses(i) == crossing]

    def slot(self, i, block):
        return 0 if self.crosses(i) else block

    def column(self, i, block, by):
        array, start, width, a1 = self.pieces[i][:4]
        pos = lax.rem(self.me.coord(OTHER[a1]) + by + 4, 4)
        ref, dp, lanes = self.ins[self.at[array]], self.dps[block], pl.ds(start, width)
        if a1 == "z":
            return ref.at[dp, pos, pl.ds(0, 4), :, lanes]
        return ref.at[dp, pl.ds(0, 4), pos, :, lanes]

    def send(self, i, block, k, src, dst, device):
        cp = remote(src, dst, self.ring_s.at[i, block, k], self.ring_r.at[i, block, k], device)
        cp.start()
        self.pending.append(cp)
        return cp

    def start_crossing(self):
        for k in range(4):
            for i in self.of(1, True):
                way = self.way(i, 1)
                by = (2 * way, -way, way, 0)[k]
                there = self.theirs[i].at[k]
                cp = remote(
                    self.column(i, 0, by), there, self.over.at[0, i, k], self.over.at[1, i, k], self.me.dp_peer()
                )
                cp.start()
                self.pending.append(cp)
                self.overs[i, k] = cp
                cp = pltpu.make_async_copy(self.column(i, 1, by), self.ours[i].at[k], self.load.at[k, i, 0])
                cp.start()
                self.loads[i, k] = cp

    def add_crossed(self, i, k):
        self.overs[i, k].wait_recv()
        self.loads[i, k].wait()
        add_into(self.ours[i].at[k], self.theirs[i].at[k])

    def start(self, block):
        for i in self.of(block, False):
            way = self.way(i, block)
            there = self.me.step(OTHER[self.pieces[i][3]], way)
            self.one[i, block, 0] = self.send(
                i, block, 0, self.column(i, block, 2 * way), self.near[i].at[block], there
            )
        for i in self.of(block, False):
            way = self.way(i, block)
            there = self.me.step(OTHER[self.pieces[i][3]], -way)
            self.one[i, block, 1] = self.send(
                i, block, 1, self.column(i, block, -way), self.far[i].at[block], there
            )
        for i in self.of(block, False):
            way = self.way(i, block)
            self.fetch(i, block, 1, 0, self.own[i].at[block])
            if block == 0:
                self.fetch(i, block, 0, way, self.mid[i])

    def fetch(self, i, block, k, by, ref):
        cp = pltpu.make_async_copy(self.column(i, block, by), ref, self.load.at[k, i, block])
        cp.start()
        self.loads[i, block, k] = cp

    def start_crossed(self):
        for k in range(2):
            for i in self.of(1, True):
                way = self.way(i, 1)
                self.add_crossed(i, k)
                there = self.me.step(OTHER[self.pieces[i][3]], -way if k else way)
                dst = (self.far if k else self.near)[i].at[0]
                self.one[i, 1, k] = self.send(i, 1, k, self.ours[i].at[k], dst, there)

    def hop(self, block, crossing):
        for i in self.of(block, crossing):
            slot = self.slot(i, block)
            self.one[i, block, 0].wait_recv()
            if crossing:
                self.add_crossed(i, 2)
                mid = self.ours[i].at[2]
            else:
                self.loads[i, block, 0].wait()
                mid = self.mid[i]
            near = self.near[i].at[slot]
            add_into(near, mid)
            if block == 0:
                self.fetch(i, 1, 0, self.way(i, 1), mid)
            there = self.me.step(OTHER[self.pieces[i][3]], self.way(i, block))
            self.one[i, block, 2] = self.send(i, block, 2, near, self.last[i].at[slot], there)

    def own_of(self, i, block):
        return self.ours[i].at[3] if self.crosses(i) else self.own[i].at[block]

    def turn(self, block, crossing):
        me = self.me
        for i in self.of(block, crossing):
            slot, a1, way = self.slot(i, block), self.pieces[i][3], self.way(i, block)
            if crossing:
                self.add_crossed(i, 3)
            else:
                self.loads[i, block, 1].wait()
            self.one[i, block, 1].wait_recv()
            self.one[i, block, 2].wait_recv()
            own = self.own_of(i, block)
            add_two(own, self.far[i].at[slot], self.last[i].at[slot])
            pos = me.coord(a1)
            self.two[i, block, 0] = self.send(
                i, block, 3, own.at[lax.rem(pos + 2, 4)], self.near1[i].at[slot], me.step(a1, way)
            )
            self.two[i, block, 1] = self.send(
                i, block, 4, own.at[lax.rem(pos - way + 4, 4)], self.far1[i].at[slot], me.step(a1, -way)
            )

    def hop_two(self, block, crossing):
        me = self.me
        for i in self.of(block, crossing):
            slot, a1, way = self.slot(i, block), self.pieces[i][3], self.way(i, block)
            self.two[i, block, 0].wait_recv()
            place = lax.rem(me.coord(a1) + way + 4, 4)
            add_into(self.near1[i].at[pl.ds(slot, 1)], self.own_of(i, block).at[pl.ds(place, 1)])
            self.two[i, block, 2] = self.send(
                i, block, 5, self.near1[i].at[slot], self.last1[i].at[slot], me.step(a1, way)
            )

    def finish(self, block, crossing):
        me = self.me
        for i in self.of(block, crossing):
            array, start, width, a1 = self.pieces[i][:4]
            slot, pos = self.slot(i, block), me.coord(a1)
            self.two[i, block, 1].wait_recv()
            self.two[i, block, 2].wait_recv()
            if block == 1 and not crossing:
                self.overs[i, 0].wait_recv()
            far1, last1, sent, came = (ref[i] for ref in (self.far1, self.last1, self.sent, self.came))
            own = self.own_of(i, block)
            total = self.total[self.at[array]]

            def step(k, carry):
                part = pl.ds(pl.multiple_of(k * 16, 16), 16)
                both = far1[slot, part, :].astype(jnp.float32) + last1[slot, part, :].astype(jnp.float32)
                both = both + own[pos, part, :].astype(jnp.float32)
                if block == 0:
                    sent[part, :] = both.astype(jnp.bfloat16)
                elif crossing:
                    total[part, start : start + width] = both
                else:
                    total[part, start : start + width] = both + came[part, :].astype(jnp.float32)
                return carry

            lax.fori_loop(0, 2 * ARRAYS[array][0] // 16, step, 0)
            if block == 0:
                cp = remote(sent, came, self.over.at[0, i, 0], self.over.at[1, i, 0], me.dp_peer())
                cp.start()
                self.pending.append(cp)
                self.overs[i, 0] = cp

    def hand_out(self):
        me = self.me
        copies = []

        def give(k, first, width, out):
            rows = out.shape[0]
            lanes = pl.ds(first, width)
            mine = self.total[k].at[pl.ds(pl.multiple_of(me.c * rows, 8), rows), lanes]
            theirs = self.total[k].at[pl.ds(pl.multiple_of((1 - me.c) * rows, 8), rows), lanes]
            place = out.at[:, pl.ds(pl.multiple_of(me.c * width, LANES), width)]
            n = len(copies) // 2
            copies.append(pltpu.make_async_copy(mine, place, self.keep.at[n]))
            copies.append(remote(theirs, place, self.fin.at[0, n], self.fin.at[1, n], me.sibling()))

        for array, k in self.at.items():
            width = ARRAYS[array][1]
            if array == QKV:
                total = self.total[k]
                groups = [split_four(total[:, PACKED * g : PACKED * (g + 1)]) for g in range(4)]
                total[:, 0:PACKED] = pack_four([heads[0] for heads in groups])
                total[:, PACKED : 2 * PACKED] = pack_four([heads[1] for heads in groups])
                for pair in range(2):
                    queries = [heads[h] for heads in groups[2 * pair : 2 * pair + 2] for h in (2, 3)]
                    total[:, PACKED * (2 + pair) : PACKED * (3 + pair)] = pack_four(queries)
                for j, (first, part) in enumerate(((0, PACKED), (PACKED, PACKED), (2 * PACKED, 2 * PACKED))):
                    give(k, first, part, self.outs[k][j])
            else:
                give(k, 0, width, self.outs[k])
        for cp in copies:
            cp.start()
        for cp in copies:
            cp.wait()
        for cp in self.pending:
            cp.wait_send()


def scatter_steps(scatter):
    scatter.start_crossing()
    scatter.start(0)
    scatter.start(1)
    yield
    for stage in (
        lambda: scatter.hop(0, False),
        scatter.start_crossed,
        lambda: scatter.hop(1, False),
        lambda: scatter.turn(0, False),
        lambda: scatter.hop_two(0, False),
        lambda: scatter.hop(1, True),
        lambda: scatter.finish(0, False),
        lambda: scatter.turn(1, False),
        lambda: scatter.hop_two(1, False),
        lambda: scatter.turn(1, True),
        lambda: scatter.finish(1, False),
        lambda: scatter.hop_two(1, True),
        lambda: scatter.finish(1, True),
        scatter.hand_out,
    ):
        stage()
        yield


def advance(steps, count):
    for _ in range(count):
        next(steps)


def scatter_scratch(pieces, arrays):
    n, m = len(pieces), len(arrays)
    bf16 = jnp.bfloat16
    shapes = [(2 * ARRAYS[piece[0]][0], piece[2]) for piece in pieces]
    crossing = [piece[5] is None for piece in pieces]

    def buffers(count, *lead):
        return [pltpu.VMEM((1 if one else 2, *lead, *shape), bf16) for _ in range(count) for shape, one in zip(shapes, crossing)]

    held = [
        pltpu.VMEM((1, 16, LANES) if one else (*lead, *shape), bf16)
        for lead in ((4,), (2, 4))
        for shape, one in zip(shapes, crossing)
    ]
    whole = [pltpu.VMEM((4, 4, *shape), bf16) for _ in range(2) for shape, one in zip(shapes, crossing) if one]
    return (
        buffers(3, 4)
        + held
        + buffers(3)
        + [pltpu.VMEM((16, LANES) if one else shape, bf16) for _ in range(2) for shape, one in zip(shapes, crossing)]
        + whole
        + [pltpu.VMEM((2 * ARRAYS[a][0], ARRAYS[a][1]), jnp.float32) for a in arrays]
        + [
            pltpu.SemaphoreType.DMA((4, n, 2)),
            pltpu.SemaphoreType.DMA((n, 2, 6)),
            pltpu.SemaphoreType.DMA((n, 2, 6)),
            pltpu.SemaphoreType.DMA((2, n, 4)),
            pltpu.SemaphoreType.DMA((2, m + 2)),
            pltpu.SemaphoreType.DMA((m + 2,)),
        ]
    )


def scatter_shapes(arrays):
    return [jax.ShapeDtypeStruct((ARRAYS[a][0], 2 * ARRAYS[a][1]), jnp.float32) for a in arrays]


def in_shards(parts, arrays):
    return [part.reshape(2, 4, 4, 2 * ARRAYS[a][0], ARRAYS[a][1]) for part, a in zip(parts, arrays, strict=True)]


ORIGINS = 32
BLOCK = 8
BLOCKS = ORIGINS // BLOCK


def meet_plane(me, others=()):
    barrier = pltpu.get_barrier_semaphore()
    for device in others:
        pl.semaphore_signal(barrier, inc=1, device_id=device, device_id_type=MESH)

    def greet(k, carry):
        to = lax.rem(me.q + k, ORIGINS)
        pl.semaphore_signal(barrier, inc=1, device_id=(me.s, me.d, to), device_id_type=MESH)
        return carry

    lax.fori_loop(1, ORIGINS, greet, 0)
    pl.semaphore_wait(barrier, ORIGINS - 1 + len(others))


class Exchange:
    def __init__(self, me, src, dst_of, sems):
        self.me, self.src, self.dst_of, self.sems = me, src, dst_of, sems

    def copy(self, origin, to):
        me, (send, recv, _) = self.me, self.sems
        peer = to + origin - me.q
        return remote(
            self.src.at[to], self.dst_of(origin, to), send.at[to], recv.at[origin], (me.s, me.d, peer)
        )

    def own(self):
        q = self.me.q
        return pltpu.make_async_copy(self.src.at[q], self.dst_of(q, q), self.sems[2].at[0])

    def start_all(self):
        self.own().start()

        def step(k, carry):
            by = (k + 1) // 2
            by = jnp.where(lax.rem(k, 2) == 1, by, ORIGINS - by)
            self.copy(self.me.q, lax.rem(self.me.q + by, ORIGINS)).start()
            return carry

        lax.fori_loop(1, ORIGINS, step, 0)

    def start_one(self, to):
        @pl.when(to == self.me.q)
        def _():
            self.own().start()

        @pl.when(to != self.me.q)
        def _():
            self.copy(self.me.q, to).start()

    def start(self, block):
        def step(k, carry):
            self.start_one(block * BLOCK + lax.rem(self.me.q + k, BLOCK))
            return carry

        lax.fori_loop(0, BLOCK, step, 0)

    def arrived(self, first, count):
        def step(k, carry):
            origin = first + k

            @pl.when(origin == self.me.q)
            def _():
                self.own().wait()

            @pl.when(origin != self.me.q)
            def _():
                self.copy(origin, self.me.q).wait_recv()

            return carry

        lax.fori_loop(0, count, step, 0)

    def sent(self):
        def step(k, carry):
            self.copy(self.me.q, lax.rem(self.me.q + k, ORIGINS)).wait_send()
            return carry

        lax.fori_loop(1, ORIGINS, step, 0)


EXCHANGE_SEMS = [
    pltpu.SemaphoreType.DMA((ORIGINS,)),
    pltpu.SemaphoreType.DMA((ORIGINS,)),
    pltpu.SemaphoreType.DMA((1,)),
]


def block_mask(block, keys, core, prefix_len):
    rows = BLOCK * 32
    row = lax.broadcasted_iota(jnp.int32, (rows, keys), 0)
    key = lax.broadcasted_iota(jnp.int32, (rows, keys), 1)
    pos = block * BLOCK * 64 + 64 * (row // 32) + 32 * core + row % 32
    return (key <= pos) | (key < prefix_len)


def keys_of(block):
    return max((block + 1) * BLOCK * 64, PREFIX_MAX)


def group(block):
    return pl.ds(block * BLOCK, BLOCK)


def split_four(y):
    inside = lax.broadcasted_iota(jnp.int32, (y.shape[0], LANES), 1) < HEAD
    heads = [y[:, :LANES]] + [pltpu.roll(y, PACKED - HEAD * h, axis=1)[:, :LANES] for h in (1, 2, 3)]
    return [jnp.where(inside, z, 0.0) for z in heads]


def pack_four(heads):
    zero = jnp.zeros((heads[0].shape[0], 2 * LANES), jnp.float32)
    wide = [jnp.concatenate([z, zero], axis=1) for z in heads]
    total = wide[0]
    for h in (1, 2, 3):
        total = total + pltpu.roll(wide[h], HEAD * h, axis=1)
    return total


def turn_heads(z, cos, ahead, back):
    return z * cos + pltpu.roll(z, PACKED - HALF, axis=1) * ahead + pltpu.roll(z, HALF, axis=1) * back


def project_and_send(x, gain, w, tables, normed, bundle, held, held_sem, coming):
    cos, ahead, back = tables
    tokens = x.shape[0]

    def fetch(g, slot):
        lanes = pl.ds(pl.multiple_of(g * PACKED, LANES), PACKED)
        return pltpu.make_async_copy(w.at[:, :, :, :, lanes], held.at[slot], held_sem.at[slot])

    begin = lax.rem(coming.me.q // 2, KV_HEADS)
    fetch(begin, 0).start()
    hidden = x[...].astype(jnp.float32)
    r1 = lax.rsqrt(jnp.mean(hidden * hidden, axis=-1, keepdims=True) + EPS)
    normed[...] = (hidden * r1 * gain).astype(jnp.bfloat16)

    def step(k, carry):
        slot = lax.rem(k, 2)
        g = lax.rem(begin + k, KV_HEADS)
        fetch(g, slot).wait()

        @pl.when(k + 1 < KV_HEADS)
        def _():
            fetch(lax.rem(g + 1, KV_HEADS), 1 - slot).start()

        y = f32dot(normed[...], held[slot].reshape(x.shape[1], PACKED), ((1,), (0,)))
        z = turn_heads(y, cos[...], ahead[...], back[...]).astype(jnp.bfloat16)
        for part in range(4):
            to = (part // 2) * 16 + g * 2 + part % 2
            bundle[to] = z[part * 32 : (part + 1) * 32]
            coming.start_one(to)
        return carry

    lax.fori_loop(0, KV_HEADS, step, 0)


PROJECT_SCRATCH = [
    pltpu.VMEM((ORIGINS, 32, PACKED), jnp.bfloat16),
    pltpu.VMEM((2, 2, 4, 4, 48, PACKED), jnp.bfloat16),
    pltpu.SemaphoreType.DMA((2,)),
]


class Attend:
    def __init__(self, me, prefix, bundle, dst, keys, values, queries, scratch):
        self.me, self.prefix, self.keys, self.values, self.queries = me, prefix, keys, values, queries
        self.whole, self.out = scratch[:2]
        self.sib = scratch[8]
        self.coming = Exchange(
            me, bundle, lambda origin, to: self.whole.at[origin, lax.rem(to, 2)], scratch[2:5]
        )
        self.going = Exchange(me, self.out, lambda origin, to: dst.at[origin], scratch[5:8])
        self.shares = []

    def receive(self):
        for block in range(BLOCKS):
            self.coming.arrived(block * BLOCK, BLOCK)
            mine = self.whole.at[group(block), self.me.c, :, pl.ds(0, 2 * LANES)]
            cp = remote(mine, mine, self.sib.at[0, block], self.sib.at[1, block], self.me.sibling())
            cp.start()
            self.shares.append(cp)
            y = self.whole[group(block), self.me.c].reshape(BLOCK * 32, PACKED).astype(jnp.float32)
            heads = split_four(y)
            for h in range(2):
                self.queries[h, pl.ds(block * BLOCK * 32, BLOCK * 32), :] = heads[2 + h].astype(jnp.bfloat16)

    def unpack(self, block):
        self.shares[block].wait_recv()
        rows = BLOCK * 64
        both = self.whole[group(block), :, :, 0 : 2 * LANES].reshape(rows, 2 * LANES)
        at = pl.ds(block * rows, rows)
        self.keys[at, :] = both[:, :LANES]
        turned = pltpu.roll(both.astype(jnp.float32), 2 * LANES - HEAD, axis=1)
        self.values[at, :] = turned[:, :LANES].astype(jnp.bfloat16)

    def compute(self):
        ready = 0
        for block in range(BLOCKS):
            count = keys_of(block)
            while ready * BLOCK * 64 < count:
                self.unpack(ready)
                ready += 1
            k = self.keys[pl.ds(0, count), :]
            v = self.values[pl.ds(0, count), :]
            allowed = block_mask(block, count, self.me.c, self.prefix[0])
            quarters = []
            for h in range(2):
                q = self.queries[h, pl.ds(block * BLOCK * 32, BLOCK * 32), :]
                s = jnp.where(allowed, f32dot(q, k, ((1,), (1,))) * SCALE, NEG)
                top = jnp.max(s, axis=-1, keepdims=True)
                e = jnp.exp(s - top)
                p = (e * (1.0 / jnp.sum(e, axis=-1, keepdims=True))).astype(jnp.bfloat16)
                quarters.append(f32dot(p, v, ((1,), (0,))).reshape(BLOCK, 32, LANES))
            inside = lax.broadcasted_iota(jnp.int32, (BLOCK * 16, LANES), 1) < HEAD
            heads = [
                jnp.where(inside, o[:, r * 16 : r * 16 + 16].reshape(BLOCK * 16, LANES), 0.0)
                for r in range(2)
                for o in quarters
            ]
            packed = pack_four(heads).astype(jnp.bfloat16)
            self.out[group(block)] = packed.reshape(BLOCK, 16, PACKED)
        self.going.start_all()

    def drain(self):
        self.going.arrived(0, ORIGINS)
        self.coming.sent()
        self.going.sent()
        for cp in self.shares:
            cp.wait_send()


ATTEND_SCRATCH = [
    pltpu.VMEM((ORIGINS, 2, 32, PACKED), jnp.bfloat16),
    pltpu.VMEM((ORIGINS, 16, PACKED), jnp.bfloat16),
    *EXCHANGE_SEMS,
    *EXCHANGE_SEMS,
    pltpu.SemaphoreType.DMA((2, BLOCKS)),
]
KEPT = [
    ((ORIGINS * 64, LANES), jnp.bfloat16),
    ((ORIGINS * 64, LANES), jnp.bfloat16),
    ((2, ORIGINS * 32, LANES), jnp.bfloat16),
]
ATTENDED = ((ORIGINS, 16, PACKED), jnp.bfloat16)


def attend_kernel(prefix, x, gain, cos, ahead, back, w, normed, keys, values, queries, dst, *scratch):
    me = Place()
    meet_plane(me)
    bundle, held, held_sem = scratch[:3]
    attention = Attend(me, prefix, bundle, dst, keys, values, queries, scratch[3:])
    project_and_send(
        x, gain[0:1, :], w, (cos, ahead, back), normed, bundle, held, held_sem, attention.coming
    )
    attention.receive()
    attention.compute()
    attention.drain()


def attend(prefix, x, gain, tables, w):
    return pl.pallas_call(
        attend_kernel,
        out_shape=[jax.ShapeDtypeStruct(x.shape, jnp.bfloat16)]
        + [jax.ShapeDtypeStruct(*kept) for kept in KEPT]
        + [jax.ShapeDtypeStruct(*ATTENDED)],
        in_specs=[SMEM] + [VMEM] * 5 + [ANY],
        out_specs=[VMEM] * 5,
        scratch_shapes=PROJECT_SCRATCH + ATTEND_SCRATCH,
        compiler_params=pltpu.CompilerParams(
            collective_id=3, has_side_effects=True, vmem_limit_bytes=60 * MIB
        ),
        name="attend",
    )(prefix, x, gain, *tables, w)


def enter_kernel(prefix, x, cos, ahead, back, *refs):
    n = len(ARRAYS)
    ins, outs = refs[:n], refs[n : 2 * n]
    gains, dst = refs[2 * n : 2 * n + 2]
    normed, keys, values, queries, column, column_sem = refs[2 * n + 2 : 2 * n + 8]
    rest = refs[2 * n + 8 :]
    bundle, held, held_sem = rest[:3]
    k = 3 + len(ATTEND_SCRATCH)
    me = Place()
    attention = Attend(me, prefix, bundle, dst, keys, values, queries, rest[3:k])
    gather = Gather(me, ins, outs, rest[k:])
    meet_plane(me, [me.dp_peer()])
    steps = gather_steps(gather)
    next(steps)
    cp = pltpu.make_async_copy(outs[GAIN], column, column_sem.at[0])
    cp.start()
    cp.wait()
    first = (lax.broadcasted_iota(jnp.int32, (8, LANES), 1) == 0).astype(jnp.bfloat16)
    for half in range(2):
        one = column[:, :, :, :, half * LANES : (half + 1) * LANES].reshape(x.shape[1], LANES)
        gains[half] = f32dot(first, one, ((1,), (1,)))
    project_and_send(
        x, gains[0, 0:1, :], outs[QKV], (cos, ahead, back), normed, bundle, held, held_sem, attention.coming
    )
    attention.receive()
    next(steps)
    attention.compute()
    for _ in steps:
        pass
    attention.drain()


def enter(prefix, x, tables, shards):
    n = len(ARRAYS)
    width = x.shape[1]
    return pl.pallas_call(
        enter_kernel,
        out_shape=[jax.ShapeDtypeStruct((2, 4, 4, 2 * r, 2 * w), jnp.bfloat16) for r, w in ARRAYS]
        + [jax.ShapeDtypeStruct((2, 8, width), jnp.float32), jax.ShapeDtypeStruct(*ATTENDED)],
        in_specs=[SMEM] + [VMEM] * (4 + n),
        out_specs=[ANY] * n + [VMEM] * 2,
        scratch_shapes=[pltpu.VMEM(x.shape, jnp.bfloat16)]
        + [pltpu.VMEM(*kept) for kept in KEPT]
        + [pltpu.VMEM((2, 4, 4, 48, 2 * LANES), jnp.bfloat16), pltpu.SemaphoreType.DMA((1,))]
        + PROJECT_SCRATCH
        + ATTEND_SCRATCH
        + GATHER_SCRATCH,
        compiler_params=pltpu.CompilerParams(
            collective_id=1, has_side_effects=True, vmem_limit_bytes=60 * MIB
        ),
        name="enter",
    )(prefix, x, *tables, *shards)


class AttendBack:
    def __init__(self, me, prefix, keys, values, queries, src, dst, scratch):
        self.me, self.prefix, self.keys, self.values, self.queries = me, prefix, keys, values, queries
        self.datt, self.acc, self.theirs, self.dq, self.bundle = scratch[:5]
        self.sib = scratch[11]
        self.coming = Exchange(me, src, lambda origin, to: self.datt.at[origin], scratch[5:8])
        self.going = Exchange(me, self.bundle, lambda origin, to: dst.at[origin], scratch[8:11])
        self.shares = {}

    def share(self, block):
        cp = remote(
            self.acc.at[group(block), 1 - self.me.c],
            self.theirs.at[group(block)],
            self.sib.at[0, block],
            self.sib.at[1, block],
            self.me.sibling(),
        )
        cp.start()
        self.shares[block] = cp

    def finish(self, block):
        self.shares[block].wait_recv()
        rows = BLOCK * 32
        both = self.acc[group(block), self.me.c] + self.theirs[group(block)]
        both = both.reshape(rows, 2 * LANES)
        dq = self.dq[group(block)].reshape(rows, 2 * LANES)
        heads = [both[:, :LANES] * SCALE, both[:, LANES:], dq[:, :LANES], dq[:, LANES:]]
        self.bundle[group(block)] = pack_four(heads).astype(jnp.bfloat16).reshape(BLOCK, 32, PACKED)
        self.going.start(block)

    def block(self, block):
        count = keys_of(block)
        spread = pl.ds(0, count // 64)
        k = self.keys[pl.ds(0, count), :]
        v = self.values[pl.ds(0, count), :]
        allowed = block_mask(block, count, self.me.c, self.prefix[0])
        quarters = split_four(self.datt[group(block)].reshape(BLOCK * 16, PACKED).astype(jnp.float32))
        inside = lax.broadcasted_iota(jnp.int32, (BLOCK * 32, LANES), 1) < HEAD
        for h in range(2):
            q = self.queries[h, pl.ds(block * BLOCK * 32, BLOCK * 32), :]
            g = jnp.concatenate([quarters[2 * r + h].reshape(BLOCK, 16, LANES) for r in range(2)], axis=1)
            g = g.reshape(BLOCK * 32, LANES).astype(jnp.bfloat16)
            s = jnp.where(allowed, f32dot(q, k, ((1,), (1,))) * SCALE, NEG)
            top = jnp.max(s, axis=-1, keepdims=True)
            e = jnp.exp(s - top)
            p = e * (1.0 / jnp.sum(e, axis=-1, keepdims=True))
            dp = f32dot(g, v, ((1,), (1,)))
            delta = jnp.sum(p * dp, axis=-1, keepdims=True)
            ds = (p * (dp - delta)).astype(jnp.bfloat16)
            dq = jnp.where(inside, f32dot(ds, k, ((1,), (0,))) * SCALE, 0.0)
            self.dq[group(block), :, LANES * h : LANES * (h + 1)] = dq.reshape(BLOCK, 32, LANES)
            dk = f32dot(ds, q, ((0,), (0,))).reshape(count // 64, 2, 32, LANES)
            dv = f32dot(p.astype(jnp.bfloat16), g, ((0,), (0,))).reshape(count // 64, 2, 32, LANES)
            if block == BLOCKS - 1 and h == 0:
                self.acc[spread, :, :, 0:LANES] = dk
                self.acc[spread, :, :, LANES : 2 * LANES] = dv
            else:
                self.acc[spread, :, :, 0:LANES] += dk
                self.acc[spread, :, :, LANES : 2 * LANES] += dv

    def steps(self):
        self.coming.start_all()
        yield
        self.coming.arrived(0, ORIGINS)
        self.block(3)
        self.share(3)
        self.block(2)
        self.share(2)
        self.finish(3)
        self.block(1)
        self.finish(2)
        self.block(0)
        self.share(1)
        self.share(0)
        self.finish(1)
        self.finish(0)
        yield
        self.going.arrived(0, ORIGINS)
        self.coming.sent()
        self.going.sent()
        for cp in self.shares.values():
            cp.wait_send()


ATTEND_BACK_SCRATCH = [
    pltpu.VMEM((ORIGINS, 16, PACKED), jnp.bfloat16),
    pltpu.VMEM((ORIGINS, 2, 32, 2 * LANES), jnp.float32),
    pltpu.VMEM((ORIGINS, 32, 2 * LANES), jnp.float32),
    pltpu.VMEM((ORIGINS, 32, 2 * LANES), jnp.float32),
    pltpu.VMEM((ORIGINS, 32, PACKED), jnp.bfloat16),
    *EXCHANGE_SEMS,
    *EXCHANGE_SEMS,
    pltpu.SemaphoreType.DMA((2, BLOCKS)),
]
RETURNED = ((ORIGINS, 32, PACKED), jnp.bfloat16)


def attend_back_kernel(prefix, keys, values, queries, src, dst, *scratch):
    me = Place()
    meet_plane(me)
    for _ in AttendBack(me, prefix, keys, values, queries, src, dst, scratch).steps():
        pass


def attend_back(prefix, kept, src):
    return pl.pallas_call(
        attend_back_kernel,
        out_shape=jax.ShapeDtypeStruct(*RETURNED),
        in_specs=[SMEM] + [VMEM] * 4,
        out_specs=VMEM,
        scratch_shapes=ATTEND_BACK_SCRATCH,
        compiler_params=pltpu.CompilerParams(
            collective_id=4, has_side_effects=True, vmem_limit_bytes=60 * MIB
        ),
        name="attend_back",
    )(prefix, *kept, src)


def norm_back(dn, gain, u, r):
    scaled = dn * gain
    return r * (scaled - u * jnp.mean(scaled * u, axis=-1, keepdims=True))


def projections_back(me, back, tables, w, x, dmiddle, gain, dqkv, dx, total, held, held_sem):
    cos, ahead, behind = tables

    def fetch(g, slot):
        lanes = pl.ds(pl.multiple_of(g * PACKED, LANES), PACKED)
        return pltpu.make_async_copy(w.at[:, :, :, :, lanes], held.at[slot], held_sem.at[slot])

    fetch(0, 0).start()
    total[...] = jnp.zeros_like(total)

    def step(g, carry):
        slot = lax.rem(g, 2)
        fetch(g, slot).wait()

        @pl.when(g + 1 < KV_HEADS)
        def _():
            fetch(g + 1, 1 - slot).start()

        parts = [back[(part // 2) * 16 + g * 2 + part % 2] for part in range(4)]
        z = jnp.concatenate(parts, axis=0).astype(jnp.float32)
        z = turn_heads(z, cos[...], -ahead[...], -behind[...]).astype(jnp.bfloat16)
        dqkv[g] = z
        total[...] += f32dot(z, held[slot].reshape(x.shape[1], PACKED), ((1,), (1,)))
        return carry

    lax.fori_loop(0, KV_HEADS, step, 0)
    hidden, dn1 = x[...].astype(jnp.float32), total[...]
    r1 = lax.rsqrt(jnp.mean(hidden * hidden, axis=-1, keepdims=True) + EPS)
    u1 = hidden * r1
    dx[...] = (dmiddle[...] + norm_back(dn1, gain[0:1, :], u1, r1)).astype(jnp.bfloat16)
    return jnp.sum(dn1 * u1, axis=0, keepdims=True)


def leave_kernel(
    prefix, keys, values, queries, src, x, dmiddle, normed, gain, dgain_mlp, cos, ahead, behind, w, *refs
):
    m = len(MAIN_ARRAYS)
    ins, refs = refs[:m], refs[m:]
    outs, refs = refs[:m], refs[m:]
    last_outs, gain_out, dx, qkv_part, gain_part = refs[:3], refs[3], refs[4], refs[5], refs[6]
    scratch = refs[7:]
    (back, dqkv, total, held, held_sem, normed_s, dqkv_s, dgain_give, dgain_got, stage, column) = scratch[:11]
    pair, out_sem = scratch[11:13]
    scratch = scratch[13:]
    n = len(ATTEND_BACK_SCRATCH)
    k = n + len(scatter_scratch(MAIN_PIECES, MAIN_ARRAYS))
    me = Place()
    main = scatter_steps(Scatter(me, MAIN_PIECES, MAIN_ARRAYS, ins, outs, scratch[n:k]))
    last = scatter_steps(
        Scatter(me, LAST_PIECES, LAST_ARRAYS, (qkv_part, gain_part), (last_outs, gain_out), scratch[k:])
    )
    attention = AttendBack(me, prefix, keys, values, queries, src, back, scratch[:n]).steps()
    meet_plane(me, [me.dp_peer()])
    next(attention)
    next(main)
    next(attention)
    advance(main, 2)
    for _ in attention:
        pass
    dgain = projections_back(
        me, back, (cos, ahead, behind), w, x, dmiddle, gain, dqkv, dx, total, held, held_sem
    )
    half = KV_HEADS // 2
    dgain = jnp.broadcast_to(dgain, dgain_give.shape)
    dgain_give[...] = jnp.where(me.c == 0, dgain_mlp[...], dgain)
    copies = [
        remote(normed, normed_s, pair.at[0, 0], pair.at[1, 0], me.sibling()),
        remote(dqkv.at[pl.ds((1 - me.c) * half, half)], dqkv_s, pair.at[0, 1], pair.at[1, 1], me.sibling()),
        remote(dgain_give, dgain_got, pair.at[0, 2], pair.at[1, 2], me.sibling()),
    ]
    for cp in copies:
        cp.start()
    next(main)
    for cp in copies:
        cp.wait()
    rows = jnp.where(me.c == 0, dgain, dgain_mlp[...]) + dgain_got[...]
    first = (lax.broadcasted_iota(jnp.int32, (8, LANES), 0) == 0).astype(jnp.bfloat16)
    gains = f32dot(rows.astype(jnp.bfloat16), first, ((0,), (0,))).astype(jnp.bfloat16)
    column[...] = gains.reshape(column.shape)
    writes = [pltpu.make_async_copy(column, gain_part, out_sem.at[2])]
    writes[0].start()
    right = jnp.concatenate(
        [jnp.concatenate([dqkv[me.c * half + g], dqkv_s[g]], axis=0) for g in range(half)], axis=1
    )
    for r in range(4):
        lanes = slice(PACKED * r, PACKED * (r + 1))
        left = jnp.concatenate([normed[:, lanes], normed_s[:, lanes]], axis=0)
        sums = f32dot(left, right, ((0,), (0,))).astype(jnp.bfloat16)
        if r:
            writes[r].wait()
        stage[...] = sums.reshape(stage.shape)
        cp = pltpu.make_async_copy(stage, qkv_part.at[r // 2, pl.ds(2 * (r % 2), 2)], out_sem.at[r % 2])
        cp.start()
        writes.append(cp)
    for cp in (writes[0], writes[4]):
        cp.wait()
    next(last)
    advance(main, 2)
    advance(last, 2)
    advance(main, 2)
    advance(last, 2)
    advance(main, 2)
    advance(last, 2)
    advance(main, 2)
    advance(last, 2)
    advance(main, 2)
    advance(last, 6)
    advance(main, 1)


def leave(prefix, kept, src, x, dmiddle, normed, gain, dgain_mlp, tables, w, parts):
    m = len(MAIN_ARRAYS)
    width = x.shape[1]
    bf16, f32 = jnp.bfloat16, jnp.float32
    rows, half = ARRAYS[QKV]
    return pl.pallas_call(
        leave_kernel,
        out_shape=scatter_shapes(MAIN_ARRAYS)
        + [jax.ShapeDtypeStruct((rows, size), f32) for size in (half // 2, half // 2, half)]
        + scatter_shapes((GAIN,))
        + [jax.ShapeDtypeStruct(x.shape, bf16)]
        + [jax.ShapeDtypeStruct((2, 4, 4, 2 * rows, size), bf16) for size in (half, LANES)],
        in_specs=[SMEM] + [VMEM] * 12 + [ANY] * (1 + m),
        out_specs=[ANY] * (m + 4) + [VMEM] + [ANY] * 2,
        scratch_shapes=[
            pltpu.VMEM(*RETURNED),
            pltpu.VMEM((KV_HEADS, x.shape[0], PACKED), bf16),
            pltpu.VMEM(x.shape, f32),
            pltpu.VMEM((2, 2, 4, 4, 48, PACKED), bf16),
            pltpu.SemaphoreType.DMA((2,)),
            pltpu.VMEM(x.shape, bf16),
            pltpu.VMEM((KV_HEADS // 2, x.shape[0], PACKED), bf16),
            pltpu.VMEM((8, width), f32),
            pltpu.VMEM((8, width), f32),
            pltpu.VMEM((2, 4, 48, half), bf16),
            pltpu.VMEM((2, 4, 4, 48, LANES), bf16),
            pltpu.SemaphoreType.DMA((2, 3)),
            pltpu.SemaphoreType.DMA((3,)),
        ]
        + ATTEND_BACK_SCRATCH
        + scatter_scratch(MAIN_PIECES, MAIN_ARRAYS)
        + scatter_scratch(LAST_PIECES, LAST_ARRAYS),
        compiler_params=pltpu.CompilerParams(
            collective_id=5, has_side_effects=True, vmem_limit_bytes=62 * MIB
        ),
        name="leave",
    )(prefix, *kept, src, x, dmiddle, normed, gain, dgain_mlp, *tables, w, *in_shards(parts, MAIN_ARRAYS))


def pair_kernel(whole_count, *refs):
    n = (len(refs) - 3) // 2
    ins, outs = refs[:n], refs[n : 2 * n]
    send_sem, recv_sem, own_sem = refs[2 * n :]
    me = Place()
    meet([me.sibling()])
    copies = []
    for i in range(n):
        here = there = ins[i]
        if i >= whole_count:
            width = ins[i].shape[1] // 2
            here = ins[i].at[:, pl.ds(pl.multiple_of(me.c * width, LANES), width)]
            there = ins[i].at[:, pl.ds(pl.multiple_of((1 - me.c) * width, LANES), width)]
        cp = remote(there, outs[i].at[me.c], send_sem.at[i], recv_sem.at[i], me.sibling())
        cp.start()
        copies.append(cp)
        cp = pltpu.make_async_copy(here, outs[i].at[me.c], own_sem.at[i])
        cp.start()
        copies.append(cp)
    for cp in copies:
        cp.wait()


def pair_up(collective_id, whole, halved):
    n = len(whole) + len(halved)
    return pl.pallas_call(
        functools.partial(pair_kernel, len(whole)),
        out_shape=[jax.ShapeDtypeStruct((2, *a.shape), a.dtype) for a in whole]
        + [jax.ShapeDtypeStruct((2, a.shape[0], a.shape[1] // 2), a.dtype) for a in halved],
        in_specs=[VMEM] * n,
        out_specs=[VMEM] * n,
        scratch_shapes=[pltpu.SemaphoreType.DMA((n,))] * 3,
        compiler_params=pltpu.CompilerParams(
            collective_id=collective_id, has_side_effects=True, vmem_limit_bytes=40 * MIB
        ),
        name="pair_up",
    )(*whole, *halved)


STEPS = 8
FF_BLOCK = 512


def rope_tables(positions):
    lane = jnp.arange(PACKED)
    head, spot = lane // HEAD, lane % HEAD
    frequency = ROPE_BASE ** (-(lane % HALF).astype(jnp.float32) * 2.0 / HEAD)
    angles = positions.astype(jnp.float32)[:, None] * frequency[None, :]
    cos, sin = jnp.cos(angles), jnp.sin(angles)
    still, low = (head == 1)[None, :], (spot < HALF)[None, :]
    return (
        jnp.where(still, 1.0, cos),
        jnp.where(still | ~low, 0.0, -sin),
        jnp.where(still | low, 0.0, sin),
    )


def whole_spec(a):
    return pl.BlockSpec(a.shape, lambda k: (0,) * a.ndim, pipeline_mode=pl.Buffered(1))


def mlp_kernel(
    att, x, gain, o_w, gate_w, up_w, down_w, result, attended, middle, normed_two, gate, up, mixed, total
):
    k = pl.program_id(0)

    @pl.when(k == 0)
    def _():
        low_half = lax.broadcasted_iota(jnp.int32, (64, PACKED), 1) < 2 * HEAD
        for pair in range(KV_HEADS // 2):
            even, odd = (
                att[:, 2 * pair + j].reshape(64, PACKED).astype(jnp.float32) for j in range(2)
            )
            upper = jnp.where(low_half, even, pltpu.roll(odd, 2 * HEAD, axis=1))
            lower = jnp.where(low_half, pltpu.roll(even, 2 * HEAD, axis=1), odd)
            rows = jnp.concatenate([upper.reshape(4, 16, PACKED), lower.reshape(4, 16, PACKED)], axis=1)
            attended[:, PACKED * pair : PACKED * (pair + 1)] = rows.reshape(128, PACKED).astype(jnp.bfloat16)
        mid = x[...].astype(jnp.float32) + f32dot(attended[...], o_w[...], ((1,), (0,)))
        middle[...] = mid
        r2 = lax.rsqrt(jnp.mean(mid * mid, axis=-1, keepdims=True) + EPS)
        normed_two[...] = (mid * r2 * gain[0:1, :]).astype(jnp.bfloat16)
        total[...] = mid

    g = f32dot(normed_two[...], gate_w[...], ((1,), (0,)))
    u = f32dot(normed_two[...], up_w[...], ((1,), (0,)))
    gate[...] = g
    up[...] = u
    m = (g * jax.nn.sigmoid(g) * u).astype(jnp.bfloat16)
    mixed[...] = m
    total[...] += f32dot(m, down_w[...], ((1,), (0,)))

    @pl.when(k == STEPS - 1)
    def _():
        result[...] = total[...].astype(jnp.bfloat16)


def mlp(att, x, gain, o_w, gate_w, up_w, down_w):
    tokens, width = x.shape
    ff = gate_w.shape[1]
    in_block = pl.BlockSpec((width, FF_BLOCK), lambda k: (0, k))
    ff_block = pl.BlockSpec((tokens, FF_BLOCK), lambda k: (0, k))
    fixed = pl.BlockSpec((tokens, width), lambda k: (0, 0))
    return pl.pallas_call(
        mlp_kernel,
        grid=(STEPS,),
        out_shape=[
            jax.ShapeDtypeStruct((tokens, width), jnp.bfloat16),
            jax.ShapeDtypeStruct((tokens, width), jnp.bfloat16),
            jax.ShapeDtypeStruct((tokens, width), jnp.float32),
            jax.ShapeDtypeStruct((tokens, width), jnp.bfloat16),
            jax.ShapeDtypeStruct((tokens, ff), jnp.float32),
            jax.ShapeDtypeStruct((tokens, ff), jnp.float32),
            jax.ShapeDtypeStruct((tokens, ff), jnp.bfloat16),
        ],
        in_specs=[
            whole_spec(att),
            whole_spec(x),
            whole_spec(gain),
            whole_spec(o_w),
            in_block,
            in_block,
            pl.BlockSpec((FF_BLOCK, width), lambda k: (k, 0)),
        ],
        out_specs=[fixed, fixed, fixed, fixed, ff_block, ff_block, ff_block],
        scratch_shapes=[pltpu.VMEM((tokens, width), jnp.float32)],
        compiler_params=pltpu.CompilerParams(vmem_limit_bytes=48 * MIB),
        name="mlp",
    )(att, x, gain, o_w, gate_w, up_w, down_w)


def mlp_back_kernel(
    g_low, gate, up, middle, gain, o_w, gate_w, up_w, down_w, dgate, dup, dmiddle, db, dgain, datt, total
):
    k = pl.program_id(0)

    @pl.when(k == 0)
    def _():
        total[...] = jnp.zeros_like(total)

    gm = f32dot(g_low[...], down_w[...], ((1,), (1,)))
    sig = jax.nn.sigmoid(gate[...])
    dg = (gm * up[...] * sig * (1.0 + gate[...] * (1.0 - sig))).astype(jnp.bfloat16)
    du = (gm * (gate[...] * sig)).astype(jnp.bfloat16)
    dgate[...] = dg
    dup[...] = du
    total[...] += f32dot(dg, gate_w[...], ((1,), (1,))) + f32dot(du, up_w[...], ((1,), (1,)))

    @pl.when(k == STEPS - 1)
    def _():
        mid, dn2 = middle[...], total[...]
        r2 = lax.rsqrt(jnp.mean(mid * mid, axis=-1, keepdims=True) + EPS)
        u2 = mid * r2
        dgain[...] = jnp.broadcast_to(jnp.sum(dn2 * u2, axis=0, keepdims=True), dgain.shape)
        dm = g_low[...].astype(jnp.float32) + norm_back(dn2, gain[0:1, :], u2, r2)
        dmiddle[...] = dm
        low = dm.astype(jnp.bfloat16)
        db[...] = low
        low_half = lax.broadcasted_iota(jnp.int32, (4, 16, PACKED), 2) < 2 * HEAD
        for pair in range(KV_HEADS // 2):
            y = f32dot(low, o_w[PACKED * pair : PACKED * (pair + 1), :], ((1,), (1,)))
            turned = pltpu.roll(y, 2 * HEAD, axis=1).reshape(4, 32, PACKED)
            y = y.reshape(4, 32, PACKED)
            even = jnp.where(low_half, y[:, :16], turned[:, 16:])
            odd = jnp.where(low_half, turned[:, :16], y[:, 16:])
            for j, z in enumerate((even, odd)):
                datt[:, 2 * pair + j] = z.astype(jnp.bfloat16).reshape(2, 2, 16, PACKED)


def mlp_back(g_low, gate, up, middle, gain, o_w, gate_w, up_w, down_w):
    tokens, width = g_low.shape
    ff = gate_w.shape[1]
    in_block = pl.BlockSpec((width, FF_BLOCK), lambda k: (0, k))
    ff_block = pl.BlockSpec((tokens, FF_BLOCK), lambda k: (0, k))
    fixed = pl.BlockSpec((tokens, width), lambda k: (0, 0))
    datt_shape = (2, KV_HEADS, 2, 16, PACKED)
    return pl.pallas_call(
        mlp_back_kernel,
        grid=(STEPS,),
        out_shape=[
            jax.ShapeDtypeStruct((tokens, ff), jnp.bfloat16),
            jax.ShapeDtypeStruct((tokens, ff), jnp.bfloat16),
            jax.ShapeDtypeStruct((tokens, width), jnp.float32),
            jax.ShapeDtypeStruct((tokens, width), jnp.bfloat16),
            jax.ShapeDtypeStruct((8, width), jnp.float32),
            jax.ShapeDtypeStruct(datt_shape, jnp.bfloat16),
        ],
        in_specs=[
            whole_spec(g_low),
            ff_block,
            ff_block,
            whole_spec(middle),
            whole_spec(gain),
            whole_spec(o_w),
            in_block,
            in_block,
            pl.BlockSpec((FF_BLOCK, width), lambda k: (k, 0)),
        ],
        out_specs=[
            ff_block,
            ff_block,
            fixed,
            fixed,
            pl.BlockSpec((8, width), lambda k: (0, 0)),
            pl.BlockSpec(datt_shape, lambda k: (0,) * 5),
        ],
        scratch_shapes=[pltpu.VMEM((tokens, width), jnp.float32)],
        compiler_params=pltpu.CompilerParams(vmem_limit_bytes=48 * MIB),
        name="mlp_back",
    )(g_low, gate, up, middle, gain, o_w, gate_w, up_w, down_w)


def qkv_back_kernel(back_in, cos, ahead, back, w, x, dmiddle, gain, dqkv, dx, dgain, total):
    k = pl.program_id(0)

    @pl.when(k == 0)
    def _():
        total[...] = jnp.zeros_like(total)

    z = back_in[...].reshape(128, PACKED).astype(jnp.float32)
    packed = turn_heads(z, cos[...], -ahead[...], -back[...]).astype(jnp.bfloat16)
    dqkv[...] = packed
    total[...] += f32dot(packed, w[...], ((1,), (1,)))

    @pl.when(k == KV_HEADS - 1)
    def _():
        hidden, dn1 = x[...].astype(jnp.float32), total[...]
        r1 = lax.rsqrt(jnp.mean(hidden * hidden, axis=-1, keepdims=True) + EPS)
        u1 = hidden * r1
        dgain[...] = jnp.broadcast_to(jnp.sum(dn1 * u1, axis=0, keepdims=True), dgain.shape)
        dx[...] = (dmiddle[...] + norm_back(dn1, gain[0:1, :], u1, r1)).astype(jnp.bfloat16)


def project_back(back_in, tables, w, x, dmiddle, gain):
    tokens, width = x.shape
    return pl.pallas_call(
        qkv_back_kernel,
        grid=(KV_HEADS,),
        out_shape=[
            jax.ShapeDtypeStruct((tokens, 2 * width), jnp.bfloat16),
            jax.ShapeDtypeStruct((tokens, width), jnp.bfloat16),
            jax.ShapeDtypeStruct((8, width), jnp.float32),
        ],
        in_specs=[
            pl.BlockSpec((2, 1, tokens // 2, PACKED), lambda k: (0, k, 0, 0)),
            *[whole_spec(t) for t in tables],
            pl.BlockSpec((width, 4 * HEAD), lambda k: (0, k)),
            whole_spec(x),
            whole_spec(dmiddle),
            whole_spec(gain),
        ],
        out_specs=[
            pl.BlockSpec((tokens, 4 * HEAD), lambda k: (0, k)),
            pl.BlockSpec((tokens, width), lambda k: (0, 0)),
            pl.BlockSpec((8, width), lambda k: (0, 0)),
        ],
        scratch_shapes=[pltpu.VMEM((tokens, width), jnp.float32)],
        compiler_params=pltpu.CompilerParams(vmem_limit_bytes=56 * MIB),
        name="project_back",
    )(back_in, *tables, w, x, dmiddle, gain)


def hand_over_kernel(*refs):
    n = len(refs) // 2
    for src, dst in zip(refs[:n], refs[n:], strict=True):
        dst[0] = src[...]


def hand_over(results):
    n = len(results)
    return pl.pallas_call(
        hand_over_kernel,
        grid=(1,),
        out_shape=[jax.ShapeDtypeStruct((1, *a.shape), a.dtype) for a in results],
        in_specs=[pl.BlockSpec(a.shape, lambda k: (0, 0)) for a in results],
        out_specs=[pl.BlockSpec((1, *a.shape), lambda k: (0, 0, 0)) for a in results],
        compiler_params=pltpu.CompilerParams(vmem_limit_bytes=60 * MIB),
        name="hand_over",
    )(*results)


def body(
    inputs, prefix, cotangent, attn_gain, w_query, w_key, w_value, w_out, mlp_gain, w_gate, w_up, w_down
):
    seqs, rows, width = inputs.shape
    tokens = seqs * rows
    section = lax.axis_index("section")
    seq = lax.axis_index("seq")
    positions = seq * rows + jnp.arange(rows, dtype=jnp.int32)
    tables = rope_tables(jnp.concatenate([positions, positions]))
    own_prefix = lax.dynamic_slice_in_dim(prefix, seq // 16, 1)

    part = w_query.shape[1]
    qkv_shard = jnp.concatenate(
        [
            w_key[0].reshape(part, KV_HEADS, HEAD),
            w_value[0].reshape(part, KV_HEADS, HEAD),
            w_query[0].reshape(part, KV_HEADS, 2 * HEAD),
        ],
        -1,
    ).reshape(part, 2 * width)
    gain_shard = jnp.concatenate(
        [
            jnp.broadcast_to(attn_gain[0][:, None], (part, LANES)),
            jnp.broadcast_to(mlp_gain[0][:, None], (part, LANES)),
        ],
        -1,
    )
    x0 = inputs.reshape(tokens, width)
    gate_w, up_w, qkv_split, o_w, _, down_w, gains, att = enter(
        own_prefix, x0, tables, [w_gate[0], w_up[0], qkv_shard, w_out[0], gain_shard, w_down[0]]
    )
    gate_w, up_w, qkv_w, o_w, down_w = (
        w.reshape(-1, w.shape[-1]) for w in (gate_w, up_w, qkv_split, o_w, down_w)
    )
    gain_attn, gain_mlp = gains[0], gains[1]

    def feed_forward(att, x):
        return mlp(att.reshape(2, KV_HEADS, 2, 16, PACKED), x, gain_mlp, o_w, gate_w, up_w, down_w)

    out0 = feed_forward(att, x0)[0]
    received = lax.ppermute(out0, "section", [(0, 1)])
    x = jnp.where(section == 0, x0, received)
    normed, *kept, att = attend(own_prefix, x, gain_attn, tables, qkv_split)
    out, attended, middle, normed_two, gate, up, mixed = feed_forward(att, x)

    def feed_forward_back(g_low):
        return mlp_back(g_low, gate, up, middle, gain_mlp, o_w, gate_w, up_w, down_w)

    def attention_back(back, dmiddle):
        back = back.reshape(2, KV_HEADS, rows, PACKED)
        return project_back(back, tables, qkv_w, x, dmiddle, gain_attn)

    g0 = cotangent.reshape(tokens, width)
    _, _, dmiddle, _, _, datt = feed_forward_back(g0)
    back = attend_back(own_prefix, kept, datt.reshape(ORIGINS, 16, PACKED))
    _, dx0, _ = attention_back(back, dmiddle)
    received = lax.ppermute(dx0, "section", [(1, 0)])
    g_low = jnp.where(section == 1, g0, received)

    def outer(a, b):
        a, b = a.reshape(2 * tokens, -1), b.reshape(2 * tokens, -1)
        return lax.dot_general(
            a, b, (((0,), (0,)), ((), ())), preferred_element_type=jnp.float32
        ).astype(jnp.bfloat16)

    dgate, dup, dmiddle, db, dgain_mlp, datt = feed_forward_back(g_low)
    normed_two, mixed, attended, g_half, dgate, dup, db = pair_up(
        6, [normed_two, mixed, attended], [g_low, dgate, dup, db]
    )
    gate_g, up_g, o_g, down_g, key_g, value_g, query_g, gain_g, dx, _, _ = leave(
        own_prefix,
        kept,
        datt.reshape(ORIGINS, 16, PACKED),
        x,
        dmiddle,
        normed,
        gain_attn,
        dgain_mlp,
        tables,
        qkv_split,
        [outer(normed_two, dgate), outer(normed_two, dup), outer(attended, db), outer(mixed, g_half)],
    )
    dx, query_g, key_g, value_g, o_g, gate_g, up_g, down_g = hand_over(
        [dx, query_g, key_g, value_g, o_g, gate_g, up_g, down_g]
    )
    return (
        out.reshape(1, seqs, rows, width),
        dx.reshape(1, seqs, rows, width),
        gain_g[:, 0][None],
        query_g,
        key_g,
        value_g,
        o_g,
        gain_g[:, LANES][None],
        gate_g,
        up_g,
        down_g,
    )


def solution(mesh):
    split = ("dp", "seq")
    matrix = P("section", split, None)
    vector = P("section", split)
    rows = P("dp", "seq", None)
    layer = P("section", "dp", "seq", None)
    return jax.shard_map(
        body,
        mesh=mesh,
        in_specs=(
            rows, P("dp"), rows, vector, matrix, matrix, matrix, matrix, vector, matrix, matrix, matrix
        ),
        out_specs=(
            layer, layer, vector, matrix, matrix, matrix, matrix, vector, matrix, matrix, matrix
        ),
        check_vma=False,
    )
```

```python
import functools
import math

import jax
import jax.numpy as jnp
from jax import lax
from jax.experimental import pallas as pl
from jax.experimental.pallas import tpu as pltpu
from jax.sharding import PartitionSpec as P

HEADS = 16
KV_HEADS = 8
HEAD = 96
LANES = 128
HALF = HEAD // 2
PACKED = 4 * HEAD
EPS = 1e-05
ROPE_BASE = 100000.0
NEG = -1e30
PREFIX_MAX = 1024
SCALE = 1.0 / math.sqrt(HEAD)
MESH = pl.DeviceIdType.MESH
ANY = pl.BlockSpec(memory_space=pl.ANY)
VMEM = pl.BlockSpec(memory_space=pltpu.VMEM)
SMEM = pl.BlockSpec(memory_space=pltpu.SMEM)
MIB = 1 << 20

ARRAYS = ((24, 2048), (24, 2048), (24, 1536), (24, 768), (24, 128), (64, 768))
GATE, UP, QKV, OUT, GAIN, DOWN = range(6)
QKV_PIECES = (
    (QKV, 0, 512, "y", 1, -1),
    (QKV, 512, 256, "y", -1, -1),
    (QKV, 768, 512, "z", 1, -1),
    (QKV, 1280, 256, "z", -1, -1),
    (GAIN, 0, 128, "y", 1, -1),
)
CROSSING_PIECES = (
    (GATE, 1024, 1024, "y", -1, None),
    (UP, 1024, 1024, "z", -1, None),
)
REST_PIECES = (
    (OUT, 0, 384, "y", -1, 1),
    (OUT, 384, 384, "z", -1, 1),
    (GATE, 0, 1024, "y", 1, -1),
    (UP, 0, 1024, "z", 1, -1),
    (DOWN, 0, 384, "y", 1, 1),
    (DOWN, 384, 384, "z", 1, 1),
)
GATHER_PIECES = QKV_PIECES + CROSSING_PIECES + REST_PIECES
LAST_ARRAYS = (QKV, GAIN)
LAST_PIECES = (
    (QKV, 0, 256, "y", 1, 1),
    (QKV, 768, 256, "z", 1, 1),
    (QKV, 256, 256, "y", -1, -1),
    (QKV, 1024, 256, "z", -1, -1),
    (GAIN, 0, 128, "y", -1, -1),
    (QKV, 512, 256, "y", 1, None),
    (QKV, 1280, 256, "z", 1, None),
)
MAIN_ARRAYS = (GATE, UP, OUT, DOWN)
MAIN_PIECES = (
    (GATE, 0, 1024, "y", 1, 1),
    (UP, 0, 1024, "z", 1, 1),
    (DOWN, 0, 384, "y", -1, -1),
    (DOWN, 384, 384, "z", -1, -1),
    (OUT, 0, 384, "y", -1, None),
    (OUT, 384, 384, "z", -1, None),
    (GATE, 1024, 1024, "y", 1, None),
    (UP, 1024, 1024, "z", 1, None),
)
OTHER = {"y": "z", "z": "y"}


def f32dot(a, b, dims):
    return lax.dot_general(a, b, (dims, ((), ())), preferred_element_type=jnp.float32)


class Place:
    def __init__(self):
        self.s = lax.axis_index("section")
        self.d = lax.axis_index("dp")
        self.q = lax.axis_index("seq")
        self.y = lax.div(self.q, 8)
        self.z = lax.rem(lax.div(self.q, 2), 4)
        self.c = lax.rem(self.q, 2)

    def coord(self, axis):
        return self.y if axis == "y" else self.z

    def step(self, axis, by):
        y, z = self.y, self.z
        if axis == "y":
            y = lax.rem(y + by + 4, 4)
        else:
            z = lax.rem(z + by + 4, 4)
        return (self.s, self.d, y * 8 + z * 2 + self.c)

    def sibling(self):
        return (self.s, self.d, self.q + 1 - 2 * self.c)

    def section_peer(self):
        return (1 - self.s, self.d, self.q)

    def dp_peer(self):
        return (self.s, 1 - self.d, self.q)


def meet(devices):
    barrier = pltpu.get_barrier_semaphore()
    for device in devices:
        pl.semaphore_signal(barrier, inc=1, device_id=device, device_id_type=MESH)
    pl.semaphore_wait(barrier, len(devices))


def remote(src, dst, send, recv, device):
    return pltpu.make_async_remote_copy(
        src_ref=src, dst_ref=dst, send_sem=send, recv_sem=recv, device_id=device, device_id_type=MESH
    )


class Handover:
    def __init__(self, me, source, made, own, result, sems):
        self.me, self.source, self.own, self.result = me, source, own, result
        self.copy = remote(made, result, sems.at[0], sems.at[1], me.section_peer())

    def start(self):
        @pl.when(self.me.s == self.source)
        def _():
            self.copy.start()
            self.result[...] = self.own[...]

    def wait(self):
        @pl.when(self.me.s == self.source)
        def _():
            self.copy.wait_send()

        @pl.when(self.me.s != self.source)
        def _():
            self.copy.wait_recv()


class Gather:
    def __init__(self, me, ins, outs, scratch):
        n = len(ARRAYS)
        self.me, self.ins, self.outs = me, ins, outs
        self.give, self.got, self.chip = scratch[:n], scratch[n : 2 * n], scratch[2 * n : 3 * n]
        self.first, self.local, self.over, self.ring_s, self.ring_r, self.sib_s, self.sib_r = scratch[3 * n :]
        self.dps = (me.d, 1 - me.d)
        self.one, self.two, self.held, self.overs, self.swaps = {}, {}, {}, {}, {}
        self.shares, self.pending = {}, []

    def neighbours(self):
        me = self.me
        near = [me.step(axis, by) for axis in "yz" for by in (1, -1)]
        return near + [me.dp_peer(), me.sibling()]

    def lanes(self, i):
        array, start, width = GATHER_PIECES[i][:3]
        return pl.ds(pl.multiple_of(self.me.c * ARRAYS[array][1] + start, LANES), width)

    def along(self, i, dp, by):
        array, _, _, a1 = GATHER_PIECES[i][:4]
        pos = lax.rem(self.me.coord(a1) + by + 4, 4)
        y, z = (pos, self.me.z) if a1 == "y" else (self.me.y, pos)
        return self.outs[array].at[dp, y, z, :, self.lanes(i)]

    def across(self, i, dp, by):
        array, _, _, a1 = GATHER_PIECES[i][:4]
        pos = lax.rem(self.me.coord(OTHER[a1]) + by + 4, 4)
        if a1 == "y":
            return self.outs[array].at[dp, pl.ds(0, 4), pos, :, self.lanes(i)]
        return self.outs[array].at[dp, pos, pl.ds(0, 4), :, self.lanes(i)]

    def send(self, i, block, k, src, dst, device):
        cp = remote(src, dst, self.ring_s.at[i, block, k], self.ring_r.at[i, block, k], device)
        cp.start()
        self.pending.append(cp)
        return cp

    def share(self, i, block, k, ref, src=None):
        src = ref if src is None else src
        cp = remote(src, ref, self.sib_s.at[i, block, k], self.sib_r.at[i, block, k], self.me.sibling())
        cp.start()
        self.pending.append(cp)
        self.shares.setdefault(i, []).append(cp)
        if block == 0 and (k == 0 or self.crosses(i)):
            cp = remote(src, ref, self.over.at[0, i, k], self.over.at[1, i, k], self.me.dp_peer())
            cp.start()
            self.pending.append(cp)
            self.overs[i, k] = cp

    def crosses(self, i):
        return GATHER_PIECES[i][5] is None

    def way(self, i, block):
        return GATHER_PIECES[i][4 + block]

    def both(self, pieces):
        return [i for i in pieces if not self.crosses(i)]

    def cross(self, pieces, spots):
        for k in spots:
            for i in pieces:
                if self.crosses(i):
                    way = self.way(i, 0)
                    by = (0, -way, way, 2, -way, way, 2)[k]
                    place = self.along if k < 4 else self.across
                    self.overs[i, k].wait_recv()
                    self.share(i, 1, k, place(i, self.dps[1], by))

    def swap(self):
        me = self.me
        for a, (_, width) in enumerate(ARRAYS):
            start = pl.multiple_of((1 - me.c) * width, LANES)
            self.give[a][...] = self.ins[a][:, pl.ds(start, width)].astype(jnp.float32)
            cp = remote(self.give[a], self.got[a], self.first.at[0, a], self.first.at[1, a], me.sibling())
            cp.start()
            self.swaps[a] = cp

    def join(self, *arrays):
        me = self.me
        for a in arrays:
            width = ARRAYS[a][1]
            self.swaps[a].wait()
            start = pl.multiple_of(me.c * width, LANES)
            mine = self.ins[a][:, pl.ds(start, width)].astype(jnp.float32)
            theirs = self.got[a][...]
            low = jnp.where(me.c == 0, mine, theirs)
            high = jnp.where(me.c == 0, theirs, mine)
            self.chip[a][...] = jnp.concatenate([low, high], axis=0).astype(jnp.bfloat16)

    def start(self, pieces):
        me = self.me
        for i in pieces:
            array, start, width, a1 = GATHER_PIECES[i][:4]
            src = self.chip[array].at[:, pl.ds(start, width)]
            here = self.along(i, me.d, 0)
            self.one[i, 0, 1] = self.send(i, 0, 0, src, here, me.step(a1, 1))
            self.one[i, 0, -1] = self.send(i, 0, 1, src, here, me.step(a1, -1))
            cp = pltpu.make_async_copy(src, here, self.local.at[i])
            cp.start()
            self.held[i] = cp
            self.share(i, 0, 0, here, src)

    def start_other(self, pieces):
        me = self.me
        for i in self.both(pieces):
            a1 = GATHER_PIECES[i][3]
            self.overs[i, 0].wait_recv()
            here = self.along(i, self.dps[1], 0)
            self.one[i, 1, 1] = self.send(i, 1, 0, here, here, me.step(a1, 1))
            self.one[i, 1, -1] = self.send(i, 1, 1, here, here, me.step(a1, -1))
            self.share(i, 1, 0, here)

    def hop(self, pieces, block, second):
        kept, place, base = (self.two, self.across, 3) if second else (self.one, self.along, 0)
        dp = self.dps[block]
        pieces = self.both(pieces) if block else pieces
        for i in pieces:
            axis, way = GATHER_PIECES[i][3], self.way(i, block)
            axis = OTHER[axis] if second else axis
            kept[i, block, way].wait_recv()
            came = place(i, dp, -way)
            kept[i, block, 0] = self.send(i, block, base + 2, came, came, self.me.step(axis, way))
            self.share(i, block, base + 1, came)
        for i in pieces:
            way = self.way(i, block)
            kept[i, block, -way].wait_recv()
            self.share(i, block, base + 2, place(i, dp, way))

    def turn(self, pieces, block):
        dp = self.dps[block]
        for i in self.both(pieces) if block else pieces:
            a2 = OTHER[GATHER_PIECES[i][3]]
            self.one[i, block, 0].wait_recv()
            self.share(i, block, 3, self.along(i, dp, 2))
            if block == 0:
                self.held[i].wait()
            here = self.across(i, dp, 0)
            self.two[i, block, 1] = self.send(i, block, 3, here, here, self.me.step(a2, 1))
            self.two[i, block, -1] = self.send(i, block, 4, here, here, self.me.step(a2, -1))

    def finish(self, pieces, block):
        for i in self.both(pieces) if block else pieces:
            self.two[i, block, 0].wait_recv()
            self.share(i, block, 6, self.across(i, self.dps[block], 2))

    def shown(self, pieces):
        for i in pieces:
            for cp in self.shares[i]:
                cp.wait_recv()

    def drain(self):
        for cp in self.pending:
            cp.wait_send()


GATHER_SCRATCH = (
    [pltpu.VMEM(shape, jnp.float32) for shape in ARRAYS]
    + [pltpu.VMEM(shape, jnp.float32) for shape in ARRAYS]
    + [pltpu.VMEM((2 * rows, width), jnp.bfloat16) for rows, width in ARRAYS]
    + [
        pltpu.SemaphoreType.DMA((2, len(ARRAYS))),
        pltpu.SemaphoreType.DMA((len(GATHER_PIECES),)),
        pltpu.SemaphoreType.DMA((2, len(GATHER_PIECES), 7)),
        pltpu.SemaphoreType.DMA((len(GATHER_PIECES), 2, 6)),
        pltpu.SemaphoreType.DMA((len(GATHER_PIECES), 2, 6)),
        pltpu.SemaphoreType.DMA((len(GATHER_PIECES), 2, 7)),
        pltpu.SemaphoreType.DMA((len(GATHER_PIECES), 2, 7)),
    ]
)


def add_into(total, term):
    def step(j, carry):
        total[j] = total[j] + term[j]
        return carry

    lax.fori_loop(0, total.shape[0], step, 0)


def add_two(total, left, right):
    def step(j, carry):
        total[j] = total[j] + (left[j] + right[j])
        return carry

    lax.fori_loop(0, total.shape[0], step, 0)


class Scatter:
    def __init__(self, me, pieces, arrays, ins, outs, scratch):
        n, m = len(pieces), len(arrays)
        self.me, self.pieces, self.ins, self.outs = me, pieces, ins, outs
        self.at = {a: k for k, a in enumerate(arrays)}
        names = ("near", "far", "last", "mid", "own", "near1", "far1", "last1", "sent", "came")
        for k, name in enumerate(names):
            setattr(self, name, scratch[k * n : (k + 1) * n])
        rest = scratch[len(names) * n :]
        whole = [i for i in range(n) if self.crosses(i)]
        self.ours, rest = dict(zip(whole, rest)), rest[len(whole) :]
        self.theirs, rest = dict(zip(whole, rest)), rest[len(whole) :]
        self.total, rest = rest[:m], rest[m:]
        self.load, self.ring_s, self.ring_r, self.over, self.fin, self.keep = rest
        self.dps = (1 - me.d, me.d)
        self.loads, self.one, self.two, self.overs, self.pending = {}, {}, {}, {}, []

    def neighbours(self):
        me = self.me
        near = [me.step(axis, by) for axis in "yz" for by in (1, -1)]
        return near + [me.dp_peer(), me.sibling()]

    def crosses(self, i):
        return self.pieces[i][5] is None

    def way(self, i, block):
        return self.pieces[i][5 - block]

    def of(self, block, crossing=None):
        picked = [i for i in range(len(self.pieces)) if block or not self.crosses(i)]
        return [i for i in picked if crossing is None or self.crosses(i) == crossing]

    def slot(self, i, block):
        return 0 if self.crosses(i) else block

    def column(self, i, block, by):
        array, start, width, a1 = self.pieces[i][:4]
        pos = lax.rem(self.me.coord(OTHER[a1]) + by + 4, 4)
        ref, dp, lanes = self.ins[self.at[array]], self.dps[block], pl.ds(start, width)
        if a1 == "z":
            return ref.at[dp, pos, pl.ds(0, 4), :, lanes]
        return ref.at[dp, pl.ds(0, 4), pos, :, lanes]

    def send(self, i, block, k, src, dst, device):
        cp = remote(src, dst, self.ring_s.at[i, block, k], self.ring_r.at[i, block, k], device)
        cp.start()
        self.pending.append(cp)
        return cp

    def start_crossing(self):
        for k in range(4):
            for i in self.of(1, True):
                way = self.way(i, 1)
                by = (2 * way, -way, way, 0)[k]
                there = self.theirs[i].at[k]
                cp = remote(
                    self.column(i, 0, by), there, self.over.at[0, i, k], self.over.at[1, i, k], self.me.dp_peer()
                )
                cp.start()
                self.pending.append(cp)
                self.overs[i, k] = cp
                cp = pltpu.make_async_copy(self.column(i, 1, by), self.ours[i].at[k], self.load.at[k, i, 0])
                cp.start()
                self.loads[i, k] = cp

    def add_crossed(self, i, k):
        self.overs[i, k].wait_recv()
        self.loads[i, k].wait()
        add_into(self.ours[i].at[k], self.theirs[i].at[k])

    def start(self, block):
        for i in self.of(block, False):
            way = self.way(i, block)
            there = self.me.step(OTHER[self.pieces[i][3]], way)
            self.one[i, block, 0] = self.send(
                i, block, 0, self.column(i, block, 2 * way), self.near[i].at[block], there
            )
        for i in self.of(block, False):
            way = self.way(i, block)
            there = self.me.step(OTHER[self.pieces[i][3]], -way)
            self.one[i, block, 1] = self.send(
                i, block, 1, self.column(i, block, -way), self.far[i].at[block], there
            )
        for i in self.of(block, False):
            way = self.way(i, block)
            self.fetch(i, block, 1, 0, self.own[i].at[block])
            if block == 0:
                self.fetch(i, block, 0, way, self.mid[i])

    def fetch(self, i, block, k, by, ref):
        cp = pltpu.make_async_copy(self.column(i, block, by), ref, self.load.at[k, i, block])
        cp.start()
        self.loads[i, block, k] = cp

    def start_crossed(self):
        for k in range(2):
            for i in self.of(1, True):
                way = self.way(i, 1)
                self.add_crossed(i, k)
                there = self.me.step(OTHER[self.pieces[i][3]], -way if k else way)
                dst = (self.far if k else self.near)[i].at[0]
                self.one[i, 1, k] = self.send(i, 1, k, self.ours[i].at[k], dst, there)

    def hop(self, block, crossing):
        for i in self.of(block, crossing):
            slot = self.slot(i, block)
            self.one[i, block, 0].wait_recv()
            if crossing:
                self.add_crossed(i, 2)
                mid = self.ours[i].at[2]
            else:
                self.loads[i, block, 0].wait()
                mid = self.mid[i]
            near = self.near[i].at[slot]
            add_into(near, mid)
            if block == 0:
                self.fetch(i, 1, 0, self.way(i, 1), mid)
            there = self.me.step(OTHER[self.pieces[i][3]], self.way(i, block))
            self.one[i, block, 2] = self.send(i, block, 2, near, self.last[i].at[slot], there)

    def own_of(self, i, block):
        return self.ours[i].at[3] if self.crosses(i) else self.own[i].at[block]

    def turn(self, block, crossing):
        me = self.me
        for i in self.of(block, crossing):
            slot, a1, way = self.slot(i, block), self.pieces[i][3], self.way(i, block)
            if crossing:
                self.add_crossed(i, 3)
            else:
                self.loads[i, block, 1].wait()
            self.one[i, block, 1].wait_recv()
            self.one[i, block, 2].wait_recv()
            own = self.own_of(i, block)
            add_two(own, self.far[i].at[slot], self.last[i].at[slot])
            pos = me.coord(a1)
            self.two[i, block, 0] = self.send(
                i, block, 3, own.at[lax.rem(pos + 2, 4)], self.near1[i].at[slot], me.step(a1, way)
            )
            self.two[i, block, 1] = self.send(
                i, block, 4, own.at[lax.rem(pos - way + 4, 4)], self.far1[i].at[slot], me.step(a1, -way)
            )

    def hop_two(self, block, crossing):
        me = self.me
        for i in self.of(block, crossing):
            slot, a1, way = self.slot(i, block), self.pieces[i][3], self.way(i, block)
            self.two[i, block, 0].wait_recv()
            place = lax.rem(me.coord(a1) + way + 4, 4)
            add_into(self.near1[i].at[pl.ds(slot, 1)], self.own_of(i, block).at[pl.ds(place, 1)])
            self.two[i, block, 2] = self.send(
                i, block, 5, self.near1[i].at[slot], self.last1[i].at[slot], me.step(a1, way)
            )

    def finish(self, block, crossing):
        me = self.me
        for i in self.of(block, crossing):
            array, start, width, a1 = self.pieces[i][:4]
            slot, pos = self.slot(i, block), me.coord(a1)
            self.two[i, block, 1].wait_recv()
            self.two[i, block, 2].wait_recv()
            if block == 1 and not crossing:
                self.overs[i, 0].wait_recv()
            far1, last1, sent, came = (ref[i] for ref in (self.far1, self.last1, self.sent, self.came))
            own = self.own_of(i, block)
            total = self.total[self.at[array]]

            def step(k, carry):
                part = pl.ds(pl.multiple_of(k * 16, 16), 16)
                both = far1[slot, part, :].astype(jnp.float32) + last1[slot, part, :].astype(jnp.float32)
                both = both + own[pos, part, :].astype(jnp.float32)
                if block == 0:
                    sent[part, :] = both.astype(jnp.bfloat16)
                elif crossing:
                    total[part, start : start + width] = both
                else:
                    total[part, start : start + width] = both + came[part, :].astype(jnp.float32)
                return carry

            lax.fori_loop(0, 2 * ARRAYS[array][0] // 16, step, 0)
            if block == 0:
                cp = remote(sent, came, self.over.at[0, i, 0], self.over.at[1, i, 0], me.dp_peer())
                cp.start()
                self.pending.append(cp)
                self.overs[i, 0] = cp

    def hand_out(self):
        me = self.me
        copies = []

        def give(k, first, width, out):
            rows = out.shape[0]
            lanes = pl.ds(first, width)
            mine = self.total[k].at[pl.ds(pl.multiple_of(me.c * rows, 8), rows), lanes]
            theirs = self.total[k].at[pl.ds(pl.multiple_of((1 - me.c) * rows, 8), rows), lanes]
            place = out.at[:, pl.ds(pl.multiple_of(me.c * width, LANES), width)]
            n = len(copies) // 2
            copies.append(pltpu.make_async_copy(mine, place, self.keep.at[n]))
            copies.append(remote(theirs, place, self.fin.at[0, n], self.fin.at[1, n], me.sibling()))

        for array, k in self.at.items():
            width = ARRAYS[array][1]
            if array == QKV:
                total = self.total[k]
                groups = [split_four(total[:, PACKED * g : PACKED * (g + 1)]) for g in range(4)]
                total[:, 0:PACKED] = pack_four([heads[0] for heads in groups])
                total[:, PACKED : 2 * PACKED] = pack_four([heads[1] for heads in groups])
                for pair in range(2):
                    queries = [heads[h] for heads in groups[2 * pair : 2 * pair + 2] for h in (2, 3)]
                    total[:, PACKED * (2 + pair) : PACKED * (3 + pair)] = pack_four(queries)
                for j, (first, part) in enumerate(((0, PACKED), (PACKED, PACKED), (2 * PACKED, 2 * PACKED))):
                    give(k, first, part, self.outs[k][j])
            else:
                give(k, 0, width, self.outs[k])
        for cp in copies:
            cp.start()
        for cp in copies:
            cp.wait()
        for cp in self.pending:
            cp.wait_send()


def scatter_scratch(pieces, arrays):
    n, m = len(pieces), len(arrays)
    bf16 = jnp.bfloat16
    shapes = [(2 * ARRAYS[piece[0]][0], piece[2]) for piece in pieces]
    crossing = [piece[5] is None for piece in pieces]

    def buffers(count, *lead):
        return [pltpu.VMEM((1 if one else 2, *lead, *shape), bf16) for _ in range(count) for shape, one in zip(shapes, crossing)]

    held = [
        pltpu.VMEM((1, 16, LANES) if one else (*lead, *shape), bf16)
        for lead in ((4,), (2, 4))
        for shape, one in zip(shapes, crossing)
    ]
    whole = [pltpu.VMEM((4, 4, *shape), bf16) for _ in range(2) for shape, one in zip(shapes, crossing) if one]
    return (
        buffers(3, 4)
        + held
        + buffers(3)
        + [pltpu.VMEM((16, LANES) if one else shape, bf16) for _ in range(2) for shape, one in zip(shapes, crossing)]
        + whole
        + [pltpu.VMEM((2 * ARRAYS[a][0], ARRAYS[a][1]), jnp.float32) for a in arrays]
        + [
            pltpu.SemaphoreType.DMA((4, n, 2)),
            pltpu.SemaphoreType.DMA((n, 2, 6)),
            pltpu.SemaphoreType.DMA((n, 2, 6)),
            pltpu.SemaphoreType.DMA((2, n, 4)),
            pltpu.SemaphoreType.DMA((2, m + 2)),
            pltpu.SemaphoreType.DMA((m + 2,)),
        ]
    )


def scatter_shapes(arrays):
    return [jax.ShapeDtypeStruct((ARRAYS[a][0], 2 * ARRAYS[a][1]), jnp.float32) for a in arrays]


def in_shards(parts, arrays):
    return [part.reshape(2, 4, 4, 2 * ARRAYS[a][0], ARRAYS[a][1]) for part, a in zip(parts, arrays, strict=True)]


ORIGINS = 32
BLOCK = 8
BLOCKS = ORIGINS // BLOCK


def meet_plane(me, others=()):
    barrier = pltpu.get_barrier_semaphore()
    for device in others:
        pl.semaphore_signal(barrier, inc=1, device_id=device, device_id_type=MESH)

    def greet(k, carry):
        to = lax.rem(me.q + k, ORIGINS)
        pl.semaphore_signal(barrier, inc=1, device_id=(me.s, me.d, to), device_id_type=MESH)
        return carry

    lax.fori_loop(1, ORIGINS, greet, 0)
    pl.semaphore_wait(barrier, ORIGINS - 1 + len(others))


class Exchange:
    def __init__(self, me, src, dst_of, sems):
        self.me, self.src, self.dst_of, self.sems = me, src, dst_of, sems

    def copy(self, origin, to):
        me, (send, recv, _) = self.me, self.sems
        peer = to + origin - me.q
        return remote(
            self.src.at[to], self.dst_of(origin, to), send.at[to], recv.at[origin], (me.s, me.d, peer)
        )

    def own(self):
        q = self.me.q
        return pltpu.make_async_copy(self.src.at[q], self.dst_of(q, q), self.sems[2].at[0])

    def start_all(self):
        self.own().start()

        def step(k, carry):
            by = (k + 1) // 2
            by = jnp.where(lax.rem(k, 2) == 1, by, ORIGINS - by)
            self.copy(self.me.q, lax.rem(self.me.q + by, ORIGINS)).start()
            return carry

        lax.fori_loop(1, ORIGINS, step, 0)

    def start_one(self, to):
        @pl.when(to == self.me.q)
        def _():
            self.own().start()

        @pl.when(to != self.me.q)
        def _():
            self.copy(self.me.q, to).start()

    def start(self, block):
        def step(k, carry):
            self.start_one(block * BLOCK + lax.rem(self.me.q + k, BLOCK))
            return carry

        lax.fori_loop(0, BLOCK, step, 0)

    def arrived(self, first, count):
        def step(k, carry):
            origin = first + k

            @pl.when(origin == self.me.q)
            def _():
                self.own().wait()

            @pl.when(origin != self.me.q)
            def _():
                self.copy(origin, self.me.q).wait_recv()

            return carry

        lax.fori_loop(0, count, step, 0)

    def sent(self):
        def step(k, carry):
            self.copy(self.me.q, lax.rem(self.me.q + k, ORIGINS)).wait_send()
            return carry

        lax.fori_loop(1, ORIGINS, step, 0)


EXCHANGE_SEMS = [
    pltpu.SemaphoreType.DMA((ORIGINS,)),
    pltpu.SemaphoreType.DMA((ORIGINS,)),
    pltpu.SemaphoreType.DMA((1,)),
]


def block_mask(block, keys, core, prefix_len):
    rows = BLOCK * 32
    row = lax.broadcasted_iota(jnp.int32, (rows, keys), 0)
    key = lax.broadcasted_iota(jnp.int32, (rows, keys), 1)
    pos = block * BLOCK * 64 + 64 * (row // 32) + 32 * core + row % 32
    return (key <= pos) | (key < prefix_len)


def keys_of(block):
    return max((block + 1) * BLOCK * 64, PREFIX_MAX)


def group(block):
    return pl.ds(block * BLOCK, BLOCK)


def split_four(y):
    inside = lax.broadcasted_iota(jnp.int32, (y.shape[0], LANES), 1) < HEAD
    heads = [y[:, :LANES]] + [pltpu.roll(y, PACKED - HEAD * h, axis=1)[:, :LANES] for h in (1, 2, 3)]
    return [jnp.where(inside, z, 0.0) for z in heads]


def pack_four(heads):
    zero = jnp.zeros((heads[0].shape[0], 2 * LANES), jnp.float32)
    wide = [jnp.concatenate([z, zero], axis=1) for z in heads]
    total = wide[0]
    for h in (1, 2, 3):
        total = total + pltpu.roll(wide[h], HEAD * h, axis=1)
    return total


def turn_heads(z, cos, ahead, back):
    return z * cos + pltpu.roll(z, PACKED - HALF, axis=1) * ahead + pltpu.roll(z, HALF, axis=1) * back


def project_and_send(x, gain, w, tables, normed, bundle, held, held_sem, coming):
    cos, ahead, back = tables
    tokens = x.shape[0]

    def fetch(g, slot):
        lanes = pl.ds(pl.multiple_of(g * PACKED, LANES), PACKED)
        return pltpu.make_async_copy(w.at[:, :, :, :, lanes], held.at[slot], held_sem.at[slot])

    begin = lax.rem(coming.me.q // 2, KV_HEADS)
    fetch(begin, 0).start()
    hidden = x[...].astype(jnp.float32)
    r1 = lax.rsqrt(jnp.mean(hidden * hidden, axis=-1, keepdims=True) + EPS)
    normed[...] = (hidden * r1 * gain).astype(jnp.bfloat16)

    def step(k, carry):
        slot = lax.rem(k, 2)
        g = lax.rem(begin + k, KV_HEADS)
        fetch(g, slot).wait()

        @pl.when(k + 1 < KV_HEADS)
        def _():
            fetch(lax.rem(g + 1, KV_HEADS), 1 - slot).start()

        y = f32dot(normed[...], held[slot].reshape(x.shape[1], PACKED), ((1,), (0,)))
        z = turn_heads(y, cos[...], ahead[...], back[...]).astype(jnp.bfloat16)
        for part in range(4):
            to = (part // 2) * 16 + g * 2 + part % 2
            bundle[to] = z[part * 32 : (part + 1) * 32]
            coming.start_one(to)
        return carry

    lax.fori_loop(0, KV_HEADS, step, 0)


PROJECT_SCRATCH = [
    pltpu.VMEM((ORIGINS, 32, PACKED), jnp.bfloat16),
    pltpu.VMEM((2, 2, 4, 4, 48, PACKED), jnp.bfloat16),
    pltpu.SemaphoreType.DMA((2,)),
]


class Attend:
    def __init__(self, me, prefix, bundle, dst, keys, values, queries, scratch):
        self.me, self.prefix, self.keys, self.values, self.queries = me, prefix, keys, values, queries
        self.whole, self.out = scratch[:2]
        self.sib = scratch[8]
        self.coming = Exchange(
            me, bundle, lambda origin, to: self.whole.at[origin, lax.rem(to, 2)], scratch[2:5]
        )
        self.going = Exchange(me, self.out, lambda origin, to: dst.at[origin], scratch[5:8])
        self.shares = []

    def receive(self):
        for block in range(BLOCKS):
            self.coming.arrived(block * BLOCK, BLOCK)
            mine = self.whole.at[group(block), self.me.c, :, pl.ds(0, 2 * LANES)]
            cp = remote(mine, mine, self.sib.at[0, block], self.sib.at[1, block], self.me.sibling())
            cp.start()
            self.shares.append(cp)
            y = self.whole[group(block), self.me.c].reshape(BLOCK * 32, PACKED).astype(jnp.float32)
            heads = split_four(y)
            for h in range(2):
                self.queries[h, pl.ds(block * BLOCK * 32, BLOCK * 32), :] = heads[2 + h].astype(jnp.bfloat16)

    def unpack(self, block):
        self.shares[block].wait_recv()
        rows = BLOCK * 64
        both = self.whole[group(block), :, :, 0 : 2 * LANES].reshape(rows, 2 * LANES)
        at = pl.ds(block * rows, rows)
        self.keys[at, :] = both[:, :LANES]
        turned = pltpu.roll(both.astype(jnp.float32), 2 * LANES - HEAD, axis=1)
        self.values[at, :] = turned[:, :LANES].astype(jnp.bfloat16)

    def compute(self):
        ready = 0
        for block in range(BLOCKS):
            count = keys_of(block)
            while ready * BLOCK * 64 < count:
                self.unpack(ready)
                ready += 1
            k = self.keys[pl.ds(0, count), :]
            v = self.values[pl.ds(0, count), :]
            allowed = block_mask(block, count, self.me.c, self.prefix[lax.div(self.me.q, 16)])
            quarters = []
            for h in range(2):
                q = self.queries[h, pl.ds(block * BLOCK * 32, BLOCK * 32), :]
                s = jnp.where(allowed, f32dot(q, k, ((1,), (1,))) * SCALE, NEG)
                top = jnp.max(s, axis=-1, keepdims=True)
                e = jnp.exp(s - top)
                p = (e * (1.0 / jnp.sum(e, axis=-1, keepdims=True))).astype(jnp.bfloat16)
                quarters.append(f32dot(p, v, ((1,), (0,))).reshape(BLOCK, 32, LANES))
            inside = lax.broadcasted_iota(jnp.int32, (BLOCK * 16, LANES), 1) < HEAD
            heads = [
                jnp.where(inside, o[:, r * 16 : r * 16 + 16].reshape(BLOCK * 16, LANES), 0.0)
                for r in range(2)
                for o in quarters
            ]
            packed = pack_four(heads).astype(jnp.bfloat16)
            self.out[group(block)] = packed.reshape(BLOCK, 16, PACKED)
        self.going.start_all()

    def drain(self):
        self.going.arrived(0, ORIGINS)
        self.coming.sent()
        self.going.sent()
        for cp in self.shares:
            cp.wait_send()


ATTEND_SCRATCH = [
    pltpu.VMEM((ORIGINS, 2, 32, PACKED), jnp.bfloat16),
    pltpu.VMEM((ORIGINS, 16, PACKED), jnp.bfloat16),
    *EXCHANGE_SEMS,
    *EXCHANGE_SEMS,
    pltpu.SemaphoreType.DMA((2, BLOCKS)),
]
KEPT = [
    ((ORIGINS * 64, LANES), jnp.bfloat16),
    ((ORIGINS * 64, LANES), jnp.bfloat16),
    ((2, ORIGINS * 32, LANES), jnp.bfloat16),
]
ATTENDED = ((ORIGINS, 16, PACKED), jnp.bfloat16)


def attend_kernel(
    prefix, made, own, gain, cos, ahead, back, w, x, normed, keys, values, queries, dst, handed, *scratch
):
    me = Place()
    meet_plane(me, [me.section_peer()])
    handover = Handover(me, 0, made, own, x, handed)
    handover.start()
    handover.wait()
    bundle, held, held_sem = scratch[:3]
    attention = Attend(me, prefix, bundle, dst, keys, values, queries, scratch[3:])
    project_and_send(
        x, gain[0:1, :], w, (cos, ahead, back), normed, bundle, held, held_sem, attention.coming
    )
    attention.receive()
    attention.compute()
    attention.drain()


def attend(prefix, made, own, gain, tables, w):
    return pl.pallas_call(
        attend_kernel,
        out_shape=[jax.ShapeDtypeStruct(own.shape, jnp.bfloat16)] * 2
        + [jax.ShapeDtypeStruct(*kept) for kept in KEPT]
        + [jax.ShapeDtypeStruct(*ATTENDED)],
        in_specs=[SMEM] + [VMEM] * 6 + [ANY],
        out_specs=[VMEM] * 6,
        scratch_shapes=[pltpu.SemaphoreType.DMA((2,))] + PROJECT_SCRATCH + ATTEND_SCRATCH,
        compiler_params=pltpu.CompilerParams(
            collective_id=3, has_side_effects=True, vmem_limit_bytes=60 * MIB
        ),
        name="attend",
    )(prefix, made, own, gain, *tables, w)


def enter_kernel(prefix, x, cos, ahead, back, *refs):
    n = len(ARRAYS)
    ins, outs = refs[:n], refs[n : 2 * n]
    gains, dst = refs[2 * n : 2 * n + 2]
    normed, keys, values, queries, column, column_sem = refs[2 * n + 2 : 2 * n + 8]
    rest = refs[2 * n + 8 :]
    bundle, held, held_sem = rest[:3]
    k = 3 + len(ATTEND_SCRATCH)
    me = Place()
    attention = Attend(me, prefix, bundle, dst, keys, values, queries, rest[3:k])
    gather = Gather(me, ins, outs, rest[k:])
    meet_plane(me, [me.dp_peer()])

    def project():
        cp = pltpu.make_async_copy(outs[GAIN], column, column_sem.at[0])
        cp.start()
        cp.wait()
        first = (lax.broadcasted_iota(jnp.int32, (8, LANES), 1) == 0).astype(jnp.bfloat16)
        for half in range(2):
            one = column[:, :, :, :, half * LANES : (half + 1) * LANES].reshape(x.shape[1], LANES)
            gains[half] = f32dot(first, one, ((1,), (1,)))
        tables = (cos, ahead, back)
        project_and_send(
            x, gains[0, 0:1, :], outs[QKV], tables, normed, bundle, held, held_sem, attention.coming
        )

    first, second = len(QKV_PIECES), len(QKV_PIECES + CROSSING_PIECES)
    early, crossing, rest = range(first), range(first, second), range(second, len(GATHER_PIECES))
    gather.swap()
    gather.join(QKV, GAIN)
    gather.start(early)
    gather.join(GATE, UP)
    gather.join(OUT, DOWN)
    gather.start(crossing)
    gather.start(rest)
    gather.hop(early, 0, False)
    gather.turn(early, 0)
    gather.start_other(early)
    gather.hop(crossing, 0, False)
    gather.hop(rest, 0, False)
    gather.hop(early, 1, False)
    gather.turn(early, 1)
    gather.turn(crossing, 0)
    gather.turn(rest, 0)
    gather.start_other(rest)
    gather.hop(early, 0, True)
    gather.hop(rest, 1, False)
    gather.hop(early, 1, True)
    gather.finish(early, 0)
    gather.hop(crossing, 0, True)
    gather.hop(rest, 0, True)
    gather.turn(rest, 1)
    gather.finish(early, 1)
    gather.shown(early)
    project()
    attention.receive()
    gather.finish(crossing, 0)
    gather.finish(rest, 0)
    gather.cross(crossing, range(4))
    gather.hop(rest, 1, True)
    attention.compute()
    gather.finish(rest, 1)
    gather.cross(crossing, range(4, 7))
    gather.shown(crossing)
    gather.shown(rest)
    gather.drain()
    attention.drain()


def enter(prefix, x, tables, shards):
    n = len(ARRAYS)
    width = x.shape[1]
    return pl.pallas_call(
        enter_kernel,
        out_shape=[jax.ShapeDtypeStruct((2, 4, 4, 2 * r, 2 * w), jnp.bfloat16) for r, w in ARRAYS]
        + [jax.ShapeDtypeStruct((2, 8, width), jnp.float32), jax.ShapeDtypeStruct(*ATTENDED)],
        in_specs=[SMEM] + [VMEM] * (4 + n),
        out_specs=[ANY] * n + [VMEM] * 2,
        scratch_shapes=[pltpu.VMEM(x.shape, jnp.bfloat16)]
        + [pltpu.VMEM(*kept) for kept in KEPT]
        + [pltpu.VMEM((2, 4, 4, 48, 2 * LANES), jnp.bfloat16), pltpu.SemaphoreType.DMA((1,))]
        + PROJECT_SCRATCH
        + ATTEND_SCRATCH
        + GATHER_SCRATCH,
        compiler_params=pltpu.CompilerParams(
            collective_id=1, has_side_effects=True, vmem_limit_bytes=60 * MIB
        ),
        name="enter",
    )(prefix, x, *tables, *shards)


class AttendBack:
    def __init__(self, me, prefix, keys, values, queries, src, dst, scratch):
        self.me, self.prefix, self.keys, self.values, self.queries = me, prefix, keys, values, queries
        self.datt, self.acc, self.theirs, self.dq, self.bundle = scratch[:5]
        self.sib = scratch[11]
        self.coming = Exchange(me, src, lambda origin, to: self.datt.at[origin], scratch[5:8])
        self.going = Exchange(me, self.bundle, lambda origin, to: dst.at[origin], scratch[8:11])
        self.shares = {}

    def share(self, block):
        cp = remote(
            self.acc.at[group(block), 1 - self.me.c],
            self.theirs.at[group(block)],
            self.sib.at[0, block],
            self.sib.at[1, block],
            self.me.sibling(),
        )
        cp.start()
        self.shares[block] = cp

    def finish(self, block):
        self.shares[block].wait_recv()
        rows = BLOCK * 32
        both = self.acc[group(block), self.me.c] + self.theirs[group(block)]
        both = both.reshape(rows, 2 * LANES)
        dq = self.dq[group(block)].reshape(rows, 2 * LANES)
        heads = [both[:, :LANES] * SCALE, both[:, LANES:], dq[:, :LANES], dq[:, LANES:]]
        self.bundle[group(block)] = pack_four(heads).astype(jnp.bfloat16).reshape(BLOCK, 32, PACKED)
        self.going.start(block)

    def block(self, block):
        count = keys_of(block)
        spread = pl.ds(0, count // 64)
        k = self.keys[pl.ds(0, count), :]
        v = self.values[pl.ds(0, count), :]
        allowed = block_mask(block, count, self.me.c, self.prefix[lax.div(self.me.q, 16)])
        quarters = split_four(self.datt[group(block)].reshape(BLOCK * 16, PACKED).astype(jnp.float32))
        inside = lax.broadcasted_iota(jnp.int32, (BLOCK * 32, LANES), 1) < HEAD
        for h in range(2):
            q = self.queries[h, pl.ds(block * BLOCK * 32, BLOCK * 32), :]
            g = jnp.concatenate([quarters[2 * r + h].reshape(BLOCK, 16, LANES) for r in range(2)], axis=1)
            g = g.reshape(BLOCK * 32, LANES).astype(jnp.bfloat16)
            s = jnp.where(allowed, f32dot(q, k, ((1,), (1,))) * SCALE, NEG)
            top = jnp.max(s, axis=-1, keepdims=True)
            e = jnp.exp(s - top)
            p = e * (1.0 / jnp.sum(e, axis=-1, keepdims=True))
            dp = f32dot(g, v, ((1,), (1,)))
            delta = jnp.sum(p * dp, axis=-1, keepdims=True)
            ds = (p * (dp - delta)).astype(jnp.bfloat16)
            dq = jnp.where(inside, f32dot(ds, k, ((1,), (0,))) * SCALE, 0.0)
            self.dq[group(block), :, LANES * h : LANES * (h + 1)] = dq.reshape(BLOCK, 32, LANES)
            dk = f32dot(ds, q, ((0,), (0,))).reshape(count // 64, 2, 32, LANES)
            dv = f32dot(p.astype(jnp.bfloat16), g, ((0,), (0,))).reshape(count // 64, 2, 32, LANES)
            if block == BLOCKS - 1 and h == 0:
                self.acc[spread, :, :, 0:LANES] = dk
                self.acc[spread, :, :, LANES : 2 * LANES] = dv
            else:
                self.acc[spread, :, :, 0:LANES] += dk
                self.acc[spread, :, :, LANES : 2 * LANES] += dv

    def steps(self):
        self.coming.start_all()
        yield
        self.coming.arrived(0, ORIGINS)
        yield
        self.block(3)
        self.share(3)
        self.block(2)
        self.share(2)
        self.finish(3)
        self.block(1)
        self.finish(2)
        self.block(0)
        self.share(1)
        self.share(0)
        self.finish(1)
        self.finish(0)
        yield
        self.going.arrived(0, ORIGINS)
        self.coming.sent()
        self.going.sent()
        for cp in self.shares.values():
            cp.wait_send()


ATTEND_BACK_SCRATCH = [
    pltpu.VMEM((ORIGINS, 16, PACKED), jnp.bfloat16),
    pltpu.VMEM((ORIGINS, 2, 32, 2 * LANES), jnp.float32),
    pltpu.VMEM((ORIGINS, 32, 2 * LANES), jnp.float32),
    pltpu.VMEM((ORIGINS, 32, 2 * LANES), jnp.float32),
    pltpu.VMEM((ORIGINS, 32, PACKED), jnp.bfloat16),
    *EXCHANGE_SEMS,
    *EXCHANGE_SEMS,
    pltpu.SemaphoreType.DMA((2, BLOCKS)),
]
RETURNED = ((ORIGINS, 32, PACKED), jnp.bfloat16)


def norm_back(dn, gain, u, r):
    scaled = dn * gain
    return r * (scaled - u * jnp.mean(scaled * u, axis=-1, keepdims=True))


def projections_back(me, back, tables, w, x, dmiddle, gain, dqkv, dx, total, held, held_sem):
    cos, ahead, behind = tables

    def fetch(g, slot):
        lanes = pl.ds(pl.multiple_of(g * PACKED, LANES), PACKED)
        return pltpu.make_async_copy(w.at[:, :, :, :, lanes], held.at[slot], held_sem.at[slot])

    fetch(0, 0).start()
    total[...] = jnp.zeros_like(total)

    def step(g, carry):
        slot = lax.rem(g, 2)
        fetch(g, slot).wait()

        @pl.when(g + 1 < KV_HEADS)
        def _():
            fetch(g + 1, 1 - slot).start()

        parts = [back[(part // 2) * 16 + g * 2 + part % 2] for part in range(4)]
        z = jnp.concatenate(parts, axis=0).astype(jnp.float32)
        z = turn_heads(z, cos[...], -ahead[...], -behind[...]).astype(jnp.bfloat16)
        dqkv[g] = z
        total[...] += f32dot(z, held[slot].reshape(x.shape[1], PACKED), ((1,), (1,)))
        return carry

    lax.fori_loop(0, KV_HEADS, step, 0)
    hidden, dn1 = x[...].astype(jnp.float32), total[...]
    r1 = lax.rsqrt(jnp.mean(hidden * hidden, axis=-1, keepdims=True) + EPS)
    u1 = hidden * r1
    dx[...] = (dmiddle[...] + norm_back(dn1, gain[0:1, :], u1, r1)).astype(jnp.bfloat16)
    return jnp.sum(dn1 * u1, axis=0, keepdims=True)


def attend_back_kernel(
    prefix, keys, values, queries, src, x, dmiddle, gain, own, cos, ahead, behind, w, result, handed, *scratch
):
    me = Place()
    back, dqkv, dx, total, held, held_sem = scratch[:6]
    meet_plane(me, [me.section_peer()])
    for _ in AttendBack(me, prefix, keys, values, queries, src, back, scratch[6:]).steps():
        pass
    projections_back(me, back, (cos, ahead, behind), w, x, dmiddle, gain, dqkv, dx, total, held, held_sem)
    handover = Handover(me, 1, dx, own, result, handed)
    handover.start()
    handover.wait()


def attend_back(prefix, kept, src, x, dmiddle, gain, own, tables, w):
    bf16 = jnp.bfloat16
    return pl.pallas_call(
        attend_back_kernel,
        out_shape=jax.ShapeDtypeStruct(x.shape, bf16),
        in_specs=[SMEM] + [VMEM] * 11 + [ANY],
        out_specs=VMEM,
        scratch_shapes=[
            pltpu.SemaphoreType.DMA((2,)),
            pltpu.VMEM(*RETURNED),
            pltpu.VMEM((KV_HEADS, x.shape[0], PACKED), bf16),
            pltpu.VMEM(x.shape, bf16),
            pltpu.VMEM(x.shape, jnp.float32),
            pltpu.VMEM((2, 2, 4, 4, 48, PACKED), bf16),
            pltpu.SemaphoreType.DMA((2,)),
        ]
        + ATTEND_BACK_SCRATCH,
        compiler_params=pltpu.CompilerParams(
            collective_id=4, has_side_effects=True, vmem_limit_bytes=60 * MIB
        ),
        name="attend_back",
    )(prefix, *kept, src, x, dmiddle, gain, own, *tables, w)


def leave_kernel(
    prefix, keys, values, queries, src, x, dmiddle, normed, gain, dgain_mlp, cos, ahead, behind, w, *refs
):
    m = len(MAIN_ARRAYS)
    ins, refs = refs[:m], refs[m:]
    outs, refs = refs[:m], refs[m:]
    last_outs, gain_out, dx, qkv_part, gain_part = refs[:3], refs[3], refs[4], refs[5], refs[6]
    scratch = refs[7:]
    (back, dqkv, total, held, held_sem, normed_s, dqkv_s, dgain_give, dgain_got, stage, column) = scratch[:11]
    pair, out_sem = scratch[11:13]
    scratch = scratch[13:]
    n = len(ATTEND_BACK_SCRATCH)
    k = n + len(scatter_scratch(MAIN_PIECES, MAIN_ARRAYS))
    me = Place()
    main = Scatter(me, MAIN_PIECES, MAIN_ARRAYS, ins, outs, scratch[n:k])
    last = Scatter(me, LAST_PIECES, LAST_ARRAYS, (qkv_part, gain_part), (last_outs, gain_out), scratch[k:])
    attention = AttendBack(me, prefix, keys, values, queries, src, back, scratch[:n]).steps()
    half = KV_HEADS // 2
    shown = []

    def project():
        dgain = projections_back(
            me, back, (cos, ahead, behind), w, x, dmiddle, gain, dqkv, dx, total, held, held_sem
        )
        dgain = jnp.broadcast_to(dgain, dgain_give.shape)
        dgain_give[...] = jnp.where(me.c == 0, dgain_mlp[...], dgain)
        shown.append(dgain)
        shown.extend([
            remote(normed, normed_s, pair.at[0, 0], pair.at[1, 0], me.sibling()),
            remote(dqkv.at[pl.ds((1 - me.c) * half, half)], dqkv_s, pair.at[0, 1], pair.at[1, 1], me.sibling()),
            remote(dgain_give, dgain_got, pair.at[0, 2], pair.at[1, 2], me.sibling()),
        ])
        for cp in shown[1:]:
            cp.start()

    def weigh():
        dgain = shown[0]
        for cp in shown[1:]:
            cp.wait()
        rows = jnp.where(me.c == 0, dgain, dgain_mlp[...]) + dgain_got[...]
        first = (lax.broadcasted_iota(jnp.int32, (8, LANES), 0) == 0).astype(jnp.bfloat16)
        gains = f32dot(rows.astype(jnp.bfloat16), first, ((0,), (0,))).astype(jnp.bfloat16)
        column[...] = gains.reshape(column.shape)
        writes = [pltpu.make_async_copy(column, gain_part, out_sem.at[2])]
        writes[0].start()
        right = jnp.concatenate(
            [jnp.concatenate([dqkv[me.c * half + g], dqkv_s[g]], axis=0) for g in range(half)], axis=1
        )
        for r in range(4):
            lanes = slice(PACKED * r, PACKED * (r + 1))
            left = jnp.concatenate([normed[:, lanes], normed_s[:, lanes]], axis=0)
            sums = f32dot(left, right, ((0,), (0,))).astype(jnp.bfloat16)
            if r:
                writes[r].wait()
            stage[...] = sums.reshape(stage.shape)
            cp = pltpu.make_async_copy(stage, qkv_part.at[r // 2, pl.ds(2 * (r % 2), 2)], out_sem.at[r % 2])
            cp.start()
            writes.append(cp)
        for cp in (writes[0], writes[4]):
            cp.wait()

    meet_plane(me, [me.dp_peer()])
    next(attention, None)
    main.start_crossing()
    next(attention, None)
    main.start(0)
    next(attention, None)
    main.hop(0, False)
    main.start(1)
    main.start_crossed()
    next(attention, None)
    project()
    main.turn(0, False)
    main.hop(1, False)
    weigh()
    last.start_crossing()
    last.start(0)
    main.hop_two(0, False)
    last.start(1)
    main.finish(0, False)
    main.hop(1, True)
    last.hop(0, False)
    main.turn(1, False)
    last.start_crossed()
    last.hop(1, False)
    main.hop_two(1, False)
    last.turn(0, False)
    main.turn(1, True)
    last.hop_two(0, False)
    last.hop(1, True)
    main.finish(1, False)
    last.finish(0, False)
    last.turn(1, False)
    main.hop_two(1, True)
    last.hop_two(1, False)
    last.turn(1, True)
    main.finish(1, True)
    last.finish(1, False)
    last.hop_two(1, True)
    last.finish(1, True)
    last.hand_out()
    main.hand_out()


def leave(prefix, kept, src, x, dmiddle, normed, gain, dgain_mlp, tables, w, parts):
    m = len(MAIN_ARRAYS)
    width = x.shape[1]
    bf16, f32 = jnp.bfloat16, jnp.float32
    rows, half = ARRAYS[QKV]
    return pl.pallas_call(
        leave_kernel,
        out_shape=scatter_shapes(MAIN_ARRAYS)
        + [jax.ShapeDtypeStruct((rows, size), f32) for size in (half // 2, half // 2, half)]
        + scatter_shapes((GAIN,))
        + [jax.ShapeDtypeStruct(x.shape, bf16)]
        + [jax.ShapeDtypeStruct((2, 4, 4, 2 * rows, size), bf16) for size in (half, LANES)],
        in_specs=[SMEM] + [VMEM] * 12 + [ANY] * (1 + m),
        out_specs=[ANY] * (m + 4) + [VMEM] + [ANY] * 2,
        scratch_shapes=[
            pltpu.VMEM(*RETURNED),
            pltpu.VMEM((KV_HEADS, x.shape[0], PACKED), bf16),
            pltpu.VMEM(x.shape, f32),
            pltpu.VMEM((2, 2, 4, 4, 48, PACKED), bf16),
            pltpu.SemaphoreType.DMA((2,)),
            pltpu.VMEM(x.shape, bf16),
            pltpu.VMEM((KV_HEADS // 2, x.shape[0], PACKED), bf16),
            pltpu.VMEM((8, width), f32),
            pltpu.VMEM((8, width), f32),
            pltpu.VMEM((2, 4, 48, half), bf16),
            pltpu.VMEM((2, 4, 4, 48, LANES), bf16),
            pltpu.SemaphoreType.DMA((2, 3)),
            pltpu.SemaphoreType.DMA((3,)),
        ]
        + ATTEND_BACK_SCRATCH
        + scatter_scratch(MAIN_PIECES, MAIN_ARRAYS)
        + scatter_scratch(LAST_PIECES, LAST_ARRAYS),
        compiler_params=pltpu.CompilerParams(
            collective_id=5, has_side_effects=True, vmem_limit_bytes=62 * MIB
        ),
        name="leave",
    )(prefix, *kept, src, x, dmiddle, normed, gain, dgain_mlp, *tables, w, *in_shards(parts, MAIN_ARRAYS))


def pair_kernel(whole_count, *refs):
    n = (len(refs) - 3) // 2
    ins, outs = refs[:n], refs[n : 2 * n]
    send_sem, recv_sem, own_sem = refs[2 * n :]
    me = Place()
    meet([me.sibling()])
    copies = []
    for i in range(n):
        here = there = ins[i]
        if i >= whole_count:
            width = ins[i].shape[1] // 2
            here = ins[i].at[:, pl.ds(pl.multiple_of(me.c * width, LANES), width)]
            there = ins[i].at[:, pl.ds(pl.multiple_of((1 - me.c) * width, LANES), width)]
        cp = remote(there, outs[i].at[me.c], send_sem.at[i], recv_sem.at[i], me.sibling())
        cp.start()
        copies.append(cp)
        cp = pltpu.make_async_copy(here, outs[i].at[me.c], own_sem.at[i])
        cp.start()
        copies.append(cp)
    for cp in copies:
        cp.wait()


def pair_up(collective_id, whole, halved):
    n = len(whole) + len(halved)
    return pl.pallas_call(
        functools.partial(pair_kernel, len(whole)),
        out_shape=[jax.ShapeDtypeStruct((2, *a.shape), a.dtype) for a in whole]
        + [jax.ShapeDtypeStruct((2, a.shape[0], a.shape[1] // 2), a.dtype) for a in halved],
        in_specs=[VMEM] * n,
        out_specs=[VMEM] * n,
        scratch_shapes=[pltpu.SemaphoreType.DMA((n,))] * 3,
        compiler_params=pltpu.CompilerParams(
            collective_id=collective_id, has_side_effects=True, vmem_limit_bytes=40 * MIB
        ),
        name="pair_up",
    )(*whole, *halved)


STEPS = 8
FF_BLOCK = 512


def rope_tables(positions):
    lane = jnp.arange(PACKED)
    head, spot = lane // HEAD, lane % HEAD
    frequency = ROPE_BASE ** (-(lane % HALF).astype(jnp.float32) * 2.0 / HEAD)
    angles = positions.astype(jnp.float32)[:, None] * frequency[None, :]
    cos, sin = jnp.cos(angles), jnp.sin(angles)
    still, low = (head == 1)[None, :], (spot < HALF)[None, :]
    return (
        jnp.where(still, 1.0, cos),
        jnp.where(still | ~low, 0.0, -sin),
        jnp.where(still | low, 0.0, sin),
    )


def whole_spec(a):
    return pl.BlockSpec(a.shape, lambda k: (0,) * a.ndim, pipeline_mode=pl.Buffered(1))


def mlp_kernel(
    att, x, gain, o_w, gate_w, up_w, down_w, result, attended, middle, normed_two, gate, up, mixed, total
):
    k = pl.program_id(0)

    @pl.when(k == 0)
    def _():
        low_half = lax.broadcasted_iota(jnp.int32, (64, PACKED), 1) < 2 * HEAD
        for pair in range(KV_HEADS // 2):
            even, odd = (
                att[:, 2 * pair + j].reshape(64, PACKED).astype(jnp.float32) for j in range(2)
            )
            upper = jnp.where(low_half, even, pltpu.roll(odd, 2 * HEAD, axis=1))
            lower = jnp.where(low_half, pltpu.roll(even, 2 * HEAD, axis=1), odd)
            rows = jnp.concatenate([upper.reshape(4, 16, PACKED), lower.reshape(4, 16, PACKED)], axis=1)
            attended[:, PACKED * pair : PACKED * (pair + 1)] = rows.reshape(128, PACKED).astype(jnp.bfloat16)
        mid = x[...].astype(jnp.float32) + f32dot(attended[...], o_w[...], ((1,), (0,)))
        middle[...] = mid
        r2 = lax.rsqrt(jnp.mean(mid * mid, axis=-1, keepdims=True) + EPS)
        normed_two[...] = (mid * r2 * gain[0:1, :]).astype(jnp.bfloat16)
        total[...] = mid

    g = f32dot(normed_two[...], gate_w[...], ((1,), (0,)))
    u = f32dot(normed_two[...], up_w[...], ((1,), (0,)))
    gate[...] = g
    up[...] = u
    m = (g * jax.nn.sigmoid(g) * u).astype(jnp.bfloat16)
    mixed[...] = m
    total[...] += f32dot(m, down_w[...], ((1,), (0,)))

    @pl.when(k == STEPS - 1)
    def _():
        result[...] = total[...].astype(jnp.bfloat16)


def mlp(att, x, gain, o_w, gate_w, up_w, down_w):
    tokens, width = x.shape
    ff = gate_w.shape[1]
    in_block = pl.BlockSpec((width, FF_BLOCK), lambda k: (0, k))
    ff_block = pl.BlockSpec((tokens, FF_BLOCK), lambda k: (0, k))
    fixed = pl.BlockSpec((tokens, width), lambda k: (0, 0))
    return pl.pallas_call(
        mlp_kernel,
        grid=(STEPS,),
        out_shape=[
            jax.ShapeDtypeStruct((tokens, width), jnp.bfloat16),
            jax.ShapeDtypeStruct((tokens, width), jnp.bfloat16),
            jax.ShapeDtypeStruct((tokens, width), jnp.float32),
            jax.ShapeDtypeStruct((tokens, width), jnp.bfloat16),
            jax.ShapeDtypeStruct((tokens, ff), jnp.float32),
            jax.ShapeDtypeStruct((tokens, ff), jnp.float32),
            jax.ShapeDtypeStruct((tokens, ff), jnp.bfloat16),
        ],
        in_specs=[
            whole_spec(att),
            whole_spec(x),
            whole_spec(gain),
            whole_spec(o_w),
            in_block,
            in_block,
            pl.BlockSpec((FF_BLOCK, width), lambda k: (k, 0)),
        ],
        out_specs=[fixed, fixed, fixed, fixed, ff_block, ff_block, ff_block],
        scratch_shapes=[pltpu.VMEM((tokens, width), jnp.float32)],
        compiler_params=pltpu.CompilerParams(vmem_limit_bytes=60 * MIB),
        name="mlp",
    )(att, x, gain, o_w, gate_w, up_w, down_w)


def mlp_back_kernel(
    g_low, gate, up, middle, gain, o_w, gate_w, up_w, down_w, dgate, dup, dmiddle, db, dgain, datt, total
):
    k = pl.program_id(0)

    @pl.when(k == 0)
    def _():
        total[...] = jnp.zeros_like(total)

    gm = f32dot(g_low[...], down_w[...], ((1,), (1,)))
    sig = jax.nn.sigmoid(gate[...])
    dg = (gm * up[...] * sig * (1.0 + gate[...] * (1.0 - sig))).astype(jnp.bfloat16)
    du = (gm * (gate[...] * sig)).astype(jnp.bfloat16)
    dgate[...] = dg
    dup[...] = du
    total[...] += f32dot(dg, gate_w[...], ((1,), (1,))) + f32dot(du, up_w[...], ((1,), (1,)))

    @pl.when(k == STEPS - 1)
    def _():
        mid, dn2 = middle[...], total[...]
        r2 = lax.rsqrt(jnp.mean(mid * mid, axis=-1, keepdims=True) + EPS)
        u2 = mid * r2
        dgain[...] = jnp.broadcast_to(jnp.sum(dn2 * u2, axis=0, keepdims=True), dgain.shape)
        dm = g_low[...].astype(jnp.float32) + norm_back(dn2, gain[0:1, :], u2, r2)
        dmiddle[...] = dm
        low = dm.astype(jnp.bfloat16)
        db[...] = low
        low_half = lax.broadcasted_iota(jnp.int32, (4, 16, PACKED), 2) < 2 * HEAD
        for pair in range(KV_HEADS // 2):
            y = f32dot(low, o_w[PACKED * pair : PACKED * (pair + 1), :], ((1,), (1,)))
            turned = pltpu.roll(y, 2 * HEAD, axis=1).reshape(4, 32, PACKED)
            y = y.reshape(4, 32, PACKED)
            even = jnp.where(low_half, y[:, :16], turned[:, 16:])
            odd = jnp.where(low_half, turned[:, :16], y[:, 16:])
            for j, z in enumerate((even, odd)):
                datt[:, 2 * pair + j] = z.astype(jnp.bfloat16).reshape(2, 2, 16, PACKED)


def mlp_back(g_low, gate, up, middle, gain, o_w, gate_w, up_w, down_w):
    tokens, width = g_low.shape
    ff = gate_w.shape[1]
    in_block = pl.BlockSpec((width, FF_BLOCK), lambda k: (0, k))
    ff_block = pl.BlockSpec((tokens, FF_BLOCK), lambda k: (0, k))
    fixed = pl.BlockSpec((tokens, width), lambda k: (0, 0))
    datt_shape = (2, KV_HEADS, 2, 16, PACKED)
    return pl.pallas_call(
        mlp_back_kernel,
        grid=(STEPS,),
        out_shape=[
            jax.ShapeDtypeStruct((tokens, ff), jnp.bfloat16),
            jax.ShapeDtypeStruct((tokens, ff), jnp.bfloat16),
            jax.ShapeDtypeStruct((tokens, width), jnp.float32),
            jax.ShapeDtypeStruct((tokens, width), jnp.bfloat16),
            jax.ShapeDtypeStruct((8, width), jnp.float32),
            jax.ShapeDtypeStruct(datt_shape, jnp.bfloat16),
        ],
        in_specs=[
            whole_spec(g_low),
            ff_block,
            ff_block,
            whole_spec(middle),
            whole_spec(gain),
            whole_spec(o_w),
            in_block,
            in_block,
            pl.BlockSpec((FF_BLOCK, width), lambda k: (k, 0)),
        ],
        out_specs=[
            ff_block,
            ff_block,
            fixed,
            fixed,
            pl.BlockSpec((8, width), lambda k: (0, 0)),
            pl.BlockSpec(datt_shape, lambda k: (0,) * 5),
        ],
        scratch_shapes=[pltpu.VMEM((tokens, width), jnp.float32)],
        compiler_params=pltpu.CompilerParams(vmem_limit_bytes=48 * MIB),
        name="mlp_back",
    )(g_low, gate, up, middle, gain, o_w, gate_w, up_w, down_w)


def outer_kernel(normed_two, attended, mixed, dgate, dup, db, g, gate, up, out, down):
    def rows(ref):
        return ref[...].reshape(2 * ref.shape[1], ref.shape[2])

    left = rows(normed_two)
    gate[...] = f32dot(left, rows(dgate), ((0,), (0,))).astype(jnp.bfloat16)
    up[...] = f32dot(left, rows(dup), ((0,), (0,))).astype(jnp.bfloat16)
    out[...] = f32dot(rows(attended), rows(db), ((0,), (0,))).astype(jnp.bfloat16)
    down[...] = f32dot(rows(mixed), rows(g), ((0,), (0,))).astype(jnp.bfloat16)


def outer_products(normed_two, attended, mixed, dgate, dup, db, g):
    steps = 4
    pairs = ((normed_two, dgate), (normed_two, dup), (attended, db), (mixed, g))

    def part(a):
        return pl.BlockSpec((*a.shape[:2], a.shape[2] // steps), lambda k: (0, 0, k))

    return pl.pallas_call(
        outer_kernel,
        grid=(steps,),
        out_shape=[jax.ShapeDtypeStruct((a.shape[2], b.shape[2]), jnp.bfloat16) for a, b in pairs],
        in_specs=[part(a) for a in (normed_two, attended, mixed)]
        + [whole_spec(b) for b in (dgate, dup, db, g)],
        out_specs=[pl.BlockSpec((a.shape[2] // steps, b.shape[2]), lambda k: (k, 0)) for a, b in pairs],
        compiler_params=pltpu.CompilerParams(vmem_limit_bytes=40 * MIB),
        name="outer_products",
    )(normed_two, attended, mixed, dgate, dup, db, g)


def hand_over_kernel(*refs):
    n = len(refs) // 2
    for src, dst in zip(refs[:n], refs[n:], strict=True):
        dst[0] = src[...]


def hand_over(results):
    n = len(results)
    return pl.pallas_call(
        hand_over_kernel,
        grid=(1,),
        out_shape=[jax.ShapeDtypeStruct((1, *a.shape), a.dtype) for a in results],
        in_specs=[pl.BlockSpec(a.shape, lambda k: (0, 0)) for a in results],
        out_specs=[pl.BlockSpec((1, *a.shape), lambda k: (0, 0, 0)) for a in results],
        compiler_params=pltpu.CompilerParams(vmem_limit_bytes=60 * MIB),
        name="hand_over",
    )(*results)


def body(
    inputs, prefix, cotangent, attn_gain, w_query, w_key, w_value, w_out, mlp_gain, w_gate, w_up, w_down
):
    seqs, rows, width = inputs.shape
    tokens = seqs * rows
    seq = lax.axis_index("seq")
    positions = seq * rows + jnp.arange(rows, dtype=jnp.int32)
    tables = rope_tables(jnp.concatenate([positions, positions]))

    part = w_query.shape[1]
    qkv_shard = jnp.concatenate(
        [
            w_key[0].reshape(part, KV_HEADS, HEAD),
            w_value[0].reshape(part, KV_HEADS, HEAD),
            w_query[0].reshape(part, KV_HEADS, 2 * HEAD),
        ],
        -1,
    ).reshape(part, 2 * width)
    gain_shard = jnp.concatenate(
        [
            jnp.broadcast_to(attn_gain[0][:, None], (part, LANES)),
            jnp.broadcast_to(mlp_gain[0][:, None], (part, LANES)),
        ],
        -1,
    )
    x0 = inputs.reshape(tokens, width)
    gate_w, up_w, qkv_split, o_w, _, down_w, gains, att = enter(
        prefix, x0, tables, [w_gate[0], w_up[0], qkv_shard, w_out[0], gain_shard, w_down[0]]
    )
    gate_w, up_w, o_w, down_w = (w.reshape(-1, w.shape[-1]) for w in (gate_w, up_w, o_w, down_w))
    gain_attn, gain_mlp = gains[0], gains[1]

    def feed_forward(att, x):
        return mlp(att.reshape(2, KV_HEADS, 2, 16, PACKED), x, gain_mlp, o_w, gate_w, up_w, down_w)

    out0 = feed_forward(att, x0)[0]
    x, normed, *kept, att = attend(prefix, out0, x0, gain_attn, tables, qkv_split)
    out, attended, middle, normed_two, gate, up, mixed = feed_forward(att, x)

    def feed_forward_back(g_low):
        return mlp_back(g_low, gate, up, middle, gain_mlp, o_w, gate_w, up_w, down_w)

    g0 = cotangent.reshape(tokens, width)
    _, _, dmiddle, _, _, datt = feed_forward_back(g0)
    g_low = attend_back(
        prefix, kept, datt.reshape(ORIGINS, 16, PACKED), x, dmiddle, gain_attn, g0, tables, qkv_split
    )

    dgate, dup, dmiddle, db, dgain_mlp, datt = feed_forward_back(g_low)
    normed_two, mixed, attended, g_half, dgate, dup, db = pair_up(
        6, [normed_two, mixed, attended], [g_low, dgate, dup, db]
    )
    gate_g, up_g, o_g, down_g, key_g, value_g, query_g, gain_g, dx, _, _ = leave(
        prefix,
        kept,
        datt.reshape(ORIGINS, 16, PACKED),
        x,
        dmiddle,
        normed,
        gain_attn,
        dgain_mlp,
        tables,
        qkv_split,
        outer_products(normed_two, attended, mixed, dgate, dup, db, g_half),
    )
    dx, query_g, key_g, value_g, o_g, gate_g, up_g, down_g = hand_over(
        [dx, query_g, key_g, value_g, o_g, gate_g, up_g, down_g]
    )
    return (
        out.reshape(1, seqs, rows, width),
        dx.reshape(1, seqs, rows, width),
        gain_g[:, 0][None],
        query_g,
        key_g,
        value_g,
        o_g,
        gain_g[:, LANES][None],
        gate_g,
        up_g,
        down_g,
    )


def solution(mesh):
    split = ("dp", "seq")
    matrix = P("section", split, None)
    vector = P("section", split)
    rows = P("dp", "seq", None)
    layer = P("section", "dp", "seq", None)
    return jax.shard_map(
        body,
        mesh=mesh,
        in_specs=(
            rows, P("dp"), rows, vector, matrix, matrix, matrix, matrix, vector, matrix, matrix, matrix
        ),
        out_specs=(
            layer, layer, vector, matrix, matrix, matrix, matrix, vector, matrix, matrix, matrix
        ),
        check_vma=False,
    )
```
